32 devices in a mesh: expert: 8 (over z, x), tensor: 4 (over y, core).
Axes of the slice: x: 2, y: 2, z: 4, core: 2. Of those that a mesh axis runs over, the one named last changes fastest.
Arguments:
- tokens: bfloat16 [1024, 768], P('expert', 'tensor'), may hold values from -6 to 6
- first_gain: float32 [768], replicated, may hold values from 0.25 to 1.75
- second_gain: float32 [768], replicated, may hold values from 0.25 to 1.75
- qkv_weight: bfloat16 [3, 768, 768], P(None, None, 'tensor'), may hold values from -0.21875 to 0.21875
- out_weight: bfloat16 [768, 768], P('tensor'), may hold values from -0.875 to 0.875
- rel_table: float32 [32, 12], P(None, 'tensor'), may hold values from -6 to 6
- router_weight: bfloat16 [768, 8], replicated, may hold values from -0.15625 to 0.15625
- up_weight: bfloat16 [8, 768, 3072], P('expert', None, 'tensor'), may hold values from -0.21875 to 0.21875
- down_weight: bfloat16 [8, 3072, 768], P('expert', 'tensor'), may hold values from -0.109375 to 0.109375
- routes: int32 [1024, 2], P('expert'), may hold values from 0 to 7, all different within a row; in each aligned block of 128 rows (0 to 127, 128 to 255, ...) at most 40 rows name the same one
- lengths: int32 [8, 3], P('expert'), may hold values from 1 to 112, 128 in all within a row
- bucket_ids: int32 [112], replicated, may hold values from 0 to 31
- cotangent: bfloat16 [1024, 768], P('expert', 'tensor'), may hold values from -6 to 6
Outputs:
- output: bfloat16 [1024, 768], P('expert', 'tensor')
- input_grad: float32 [1024, 768], P('expert', 'tensor')
- first_gain_grad: float32 [768], replicated
- second_gain_grad: float32 [768], replicated
- qkv_grad: float32 [3, 768, 768], P(None, None, 'tensor')
- out_grad: float32 [768, 768], P('tensor')
- rel_grad: float32 [32, 12], P(None, 'tensor')
- router_grad: float32 [768, 8], replicated
- up_grad: float32 [8, 768, 3072], P('expert', None, 'tensor')
- down_grad: float32 [8, 3072, 768], P('expert', 'tensor')
The draws below stay inside these ranges and needn't reach their ends.
Inputs may be any that keep to these rules, and one draw needn't show every extreme that they name: `routes`: each row names two different experts. Among the rows of one index of the expert axis no expert is named by more than 40 rows, a bound that some block reaches of them. The 3 lengths of one index of the expert axis sum to 128, and one of them is exactly 112.
All inputs are finite; a program needn't handle non-finite values.
Results may differ from the reference program's by a relative error of at most 0.015.
Values may be sent and summed in bfloat16 or wider, within the bound.
No kernel may reach another device: no remote copies, remote signals or barrier semaphores. Data moves between devices by JAX's collectives and lax.ppermute only.
A program may use at most 128 MiB of HBM per device.

```python
import math
import jax
import jax.numpy as jnp
import numpy as np
from jax import lax

D = 768
HEADS = 12
HD = 64
FF = 3072
BUCKETS = 32
TOK_DEV = 128
SEQ_DEV = 3
INNER = 768
EXPERTS = 8
MAXLEN = 112
CAP = 40
TOKENS = 1024
N_EXPERT = 8


def plant(values, rng, least, largest):
    spot = [jax.random.randint(jax.random.fold_in(rng, axis), (), 0, length) for axis, length in enumerate(values.shape)]
    main_axis = values.shape.index(max(values.shape))
    neighbour = spot[:main_axis] + [(spot[main_axis] + 1) % values.shape[main_axis]] + spot[main_axis + 1:]
    return values.at[tuple(spot)].set(least).at[tuple(neighbour)].set(largest)


def block_levels(rng, shape, pieces, smallest, high):
    def one(dim, shards_of):
        draws = jax.random.uniform(jax.random.fold_in(jax.random.fold_in(rng, 6), dim), (shards_of,), jnp.float32, smallest / len(pieces), high / len(pieces))
        return jnp.repeat(jnp.exp(draws), shape[dim] // shards_of).reshape((-1,) + (1,) * (len(shape) - dim - 1))

    level = one(*pieces[0])
    for cut in pieces[1:]:
        level = level * one(*cut)
    return level


def profile(number_of, total, bound, skew):
    loads = [(1 << 20) // math.isqrt(standing ** skew) + 1 for standing in range(2, number_of + 1)]
    rest, given = total - bound - (number_of - 1), [1] * (number_of - 1)
    while rest > 0:
        movable = [i for i in range(number_of - 1) if given[i] < bound]
        mass, budget = sum([loads[i] for i in movable]), rest
        for i in movable:
            extra = min(bound - given[i], max(1, budget * loads[i] // mass), rest)
            given[i] = given[i] + extra
            rest = rest - extra
    return np.array([bound] + given)


def ragged(rng, number_of, total, bound, skew):
    if number_of == 2:
        one = jax.random.randint(rng, (), max(1, total - bound), min(bound, total - 1) + 1)
        return jnp.stack([one, total - one])
    sizes = jnp.asarray(profile(number_of, total, bound, skew), jnp.int32)
    pairs = (number_of - 1) // 2
    donor, sink = sizes[1:1 + 2 * pairs:2], sizes[2:2 + 2 * pairs:2]
    slack = jnp.minimum(donor - 1, bound - sink)
    passed = jax.random.randint(jax.random.fold_in(rng, 1), (pairs,), 0, 1 << 20) % (slack + 1)
    sizes = sizes.at[1:1 + 2 * pairs:2].set(donor - passed).at[2:2 + 2 * pairs:2].set(sink + passed)
    return sizes[jax.random.permutation(jax.random.fold_in(rng, 2), number_of)]


def assign_block(stream_key, own, number, rows, count, top, most, slope):
    ranking = jax.random.permutation(stream_key, count)
    crowded, common = shares(count, rows * top, most, slope, True), shares(count, rows * top, most, slope, False)
    places = jnp.arange(count)

    def named(tallies, rotation):
        used = int((tallies > 0).sum())
        fixed = max(1, used // 4)
        passed = fixed + (places - fixed + rotation * (used - fixed)) % max(1, count - fixed)
        return jnp.zeros((count,), jnp.int32).at[ranking[jnp.where(places < fixed, places, passed)]].set(jnp.asarray(tallies, jnp.int32))

    tallies = jnp.where(number % 4 == 0, named(crowded, number // 4), named(common, number - number // 4 - 1))
    mixed = jax.random.permutation(jax.random.fold_in(own, 3), count)
    donor, taker = mixed[0:count // 2 * 2:2], mixed[1:count // 2 * 2:2]
    margin = jnp.minimum(tallies[donor] - 1, most - tallies[taker]) // 2
    margin = jnp.where((donor == ranking[0]) | (taker == ranking[0]) | (tallies[taker] == 0), 0, jnp.maximum(margin, 0))
    passed = jax.random.randint(jax.random.fold_in(own, 4), (count // 2,), 0, 1 << 20) % (margin + 1)
    tallies = tallies.at[donor].add(-passed).at[taker].add(passed)
    members = jnp.searchsorted(jnp.cumsum(tallies), jnp.arange(rows * top), side="right").astype(jnp.int32)
    table = members.reshape(top, rows).T
    table = table[jax.random.permutation(jax.random.fold_in(own, 1), rows)]
    rotation = jax.random.randint(jax.random.fold_in(own, 2), (rows, 1), 0, top)
    return jnp.take_along_axis(table, (jnp.arange(top)[None, :] + rotation) % top, axis=1)


def shares(number_of, total, limit, slope, full):
    loads = [(1 << 20) // math.isqrt(standing ** slope) + 1 for standing in range(1, number_of + 1)]
    largest = limit if full else min(limit, max(-(-total // number_of), total * loads[0] // sum(loads)))
    least = 1 if total - largest >= number_of - 1 else 0
    counts, rest = [largest] + [least] * (number_of - 1), total - largest - least * (number_of - 1)
    while rest > 0:
        candidates = [i for i in range(1, number_of) if counts[i] < largest] or [i for i in range(1, number_of) if counts[i] < limit]
        pool, budget = sum([loads[i] for i in candidates]), rest
        for i in candidates:
            extra = min(limit - counts[i], max(1, budget * loads[i] // pool), rest)
            counts[i] = counts[i] + extra
            rest = rest - extra
    return np.array(counts)


def scatter_about(rng, extent, deviation, most, shards=(), kind=jnp.bfloat16):
    level = block_levels(rng, extent, shards, -0.22, 0.18) if shards else 1.0
    values = jax.random.normal(rng, extent, jnp.float32) * deviation * level
    return jnp.minimum(jnp.maximum(values, -most), most).astype(kind)


def setup_inputs(seed: int = 0) -> dict:
    keys = jax.random.split(jax.random.key(seed), 14)
    tokens = scatter_about(keys[0], (TOKENS, D), 1.0, 6.0, ((0, 8), (1, 4)))
    first_gain = jnp.clip(1.0 + 0.15 * jax.random.normal(keys[1], (D,), jnp.float32), 0.25, 1.75)
    second_gain = jnp.clip(1.0 + 0.15 * jax.random.normal(keys[2], (D,), jnp.float32), 0.25, 1.75)
    qkv_weight = scatter_about(keys[3], (3, D, INNER), D ** -0.5, 0.21875, ((2, 4),))
    out_weight = scatter_about(keys[4], (INNER, D), (INNER // 16) ** -0.5, 0.875, ((0, 4),))
    rel_table = scatter_about(keys[5], (BUCKETS, HEADS), 1.0, 6.0, ((1, 4),), jnp.float32)
    router_weight = scatter_about(keys[6], (D, EXPERTS), (2 * D) ** -0.5, 0.15625)
    up_weight = scatter_about(keys[7], (EXPERTS, D, FF), D ** -0.5, 0.21875, ((0, 8), (2, 4)))
    down_weight = scatter_about(keys[8], (EXPERTS, FF, D), FF ** -0.5, 0.109375, ((0, 8), (1, 4)))
    routes_keys = jax.random.split(jax.random.fold_in(keys[9], 1), TOKENS // TOK_DEV)
    routes_turns = jax.random.permutation(jax.random.fold_in(keys[9], 3), TOKENS // TOK_DEV)
    routes = jax.vmap(lambda own, number: assign_block(jax.random.fold_in(keys[9], 2), own, number, TOK_DEV, EXPERTS, 2, CAP, 1))(routes_keys, routes_turns).reshape((TOKENS, 2))
    lengths = jax.vmap(lambda own: ragged(own, SEQ_DEV, TOK_DEV, MAXLEN, 1))(jax.random.split(keys[10], N_EXPERT)).reshape((N_EXPERT, SEQ_DEV)).astype(jnp.int32)
    bucket_ids = plant(jax.random.randint(keys[11], (MAXLEN,), 0, BUCKETS), jax.random.fold_in(keys[11], 1), 0, BUCKETS - 1).astype(jnp.int32)
    cotangent = scatter_about(keys[12], (TOKENS, D), 1.0, 6.0, ((0, 8), (1, 4)))
    return dict(tokens=tokens, first_gain=first_gain, second_gain=second_gain, qkv_weight=qkv_weight, out_weight=out_weight, rel_table=rel_table, router_weight=router_weight, up_weight=up_weight, down_weight=down_weight, routes=routes, lengths=lengths, bucket_ids=bucket_ids, cotangent=cotangent)


epsilon = 1e-06
highest = lax.Precision.HIGHEST

@jax.custom_vjp
def low(v):
    return lax.optimization_barrier(v.astype(jnp.bfloat16)).astype(jnp.float32)

@jax.custom_vjp
def low_back(v):
    return v

def low_keep(v):
    return (low(v), None)

def low_pass(kept, grad):
    return (grad,)

def back_keep(v):
    return (v, None)

def back_low(kept, grad):
    return (low(grad),)
low.defvjp(low_keep, low_pass)
low_back.defvjp(back_keep, back_low)

def slot_places(routes):
    flat_routes = routes.reshape(N_EXPERT, 2 * TOK_DEV)
    one_hot = (flat_routes[:, :, None] == jnp.arange(EXPERTS, dtype=jnp.int32)[None, None, :]).astype(jnp.int32)
    before = jnp.cumsum(one_hot, axis=1) - one_hot
    slot_index = lax.optimization_barrier(jnp.sum(before * one_hot, axis=2))
    block_ids = jnp.arange(N_EXPERT, dtype=jnp.int32)[:, None]
    destination = flat_routes * (N_EXPERT * CAP) + block_ids * CAP + slot_index
    return destination.reshape(-1).astype(jnp.int32)

def attend(packed, lengths_here, gain, weights, projection, table, bucket_ids):
    inverse = lax.rsqrt(lax.optimization_barrier(jnp.mean(packed * packed, axis=-1, keepdims=True)) + epsilon)
    normed_one = low(packed * inverse * gain)
    projected = jnp.einsum('td,jdi->jti', normed_one, weights, precision=highest)
    projected = low_back(low(projected))
    head_split = projected.reshape(3, TOK_DEV, HEADS, HD).transpose(0, 2, 1, 3)
    query_heads, key_heads, value_heads = (head_split[0], head_split[1], head_split[2])
    position = jnp.arange(TOK_DEV, dtype=jnp.int32)
    seq_ends = jnp.cumsum(lengths_here).astype(jnp.int32)
    segment = lax.optimization_barrier(jnp.sum((position[:, None] >= seq_ends[None, :]).astype(jnp.int32), axis=1))
    allowed = (segment[:, None] == segment[None, :]) & (position[None, :] <= position[:, None])
    distance = jnp.clip(position[:, None] - position[None, :], 0, MAXLEN - 1)
    rel_bias = table[bucket_ids[distance]].transpose(2, 0, 1)
    scores = jnp.einsum('hqd,hkd->hqk', query_heads, key_heads, precision=highest) * HD ** (-0.5) + rel_bias
    scores = low_back(scores)
    scores = jnp.where(allowed[None], scores, -1e+30)
    soft_weights = low(jax.nn.softmax(scores, axis=-1))
    attended = jnp.einsum('hqk,hkd->hqd', soft_weights, value_heads, precision=highest)
    attended = low_back(low(attended)).transpose(1, 0, 2).reshape(TOK_DEV, HEADS * HD)
    return low_back(jnp.dot(attended, projection, precision=highest))

def reference(tokens, first_gain, second_gain, qkv_weight, out_weight, rel_table, router_weight, up_weight, down_weight, routes, lengths, bucket_ids, cotangent):
    destination = slot_places(routes)
    filled = 2 * TOKENS
    source = jnp.full((EXPERTS * N_EXPERT * CAP,), filled, jnp.int32).at[destination].set(jnp.arange(filled, dtype=jnp.int32))
    token_of = jnp.where(source == filled, TOKENS, source // 2).astype(jnp.int32)

    def forward(inputs_x, gain_one, gain_two, weights, projection, table, router, first_proj, second_proj):
        packed_rows = inputs_x.reshape(N_EXPERT, TOK_DEV, D)

        def one_pack(inputs):
            return attend(inputs[0], inputs[1], gain_one, weights, projection, table, bucket_ids)
        attention = lax.map(jax.checkpoint(one_pack), (packed_rows, lengths))
        residual = inputs_x + attention.reshape(TOKENS, D)
        inverse = lax.rsqrt(lax.optimization_barrier(jnp.mean(residual * residual, axis=-1, keepdims=True)) + epsilon)
        normed_two = low(residual * inverse * gain_two)
        logits = jnp.dot(normed_two, router, precision=highest)
        chosen = jnp.take_along_axis(logits, routes, axis=1)
        gate_values = jax.nn.softmax(chosen, axis=1)
        padded = jnp.concatenate([normed_two, jnp.zeros((1, D), jnp.float32)], axis=0)
        expert_rows = low_back(padded[token_of]).reshape(EXPERTS, N_EXPERT * CAP, D)

        def one_expert(inputs):
            pre_act = low_back(jnp.dot(inputs[0], inputs[1], precision=highest))
            activated = low(jax.nn.gelu(pre_act))
            return low_back(low(jnp.dot(activated, inputs[2], precision=highest)))
        expert_outs = lax.map(jax.checkpoint(one_expert), (expert_rows, first_proj, second_proj))
        returned = expert_outs.reshape(-1, D)[destination].reshape(TOKENS, 2, D)
        return residual + lax.optimization_barrier(jnp.sum(gate_values[:, :, None] * returned, axis=1))
    primals = (tokens.astype(jnp.float32), first_gain, second_gain, qkv_weight.astype(jnp.float32), out_weight.astype(jnp.float32), rel_table, router_weight.astype(jnp.float32), up_weight.astype(jnp.float32), down_weight.astype(jnp.float32))
    result, pull = jax.vjp(forward, *primals)
    grads = pull(cotangent.astype(jnp.float32))
    return (result.astype(jnp.bfloat16), grads[0], grads[1], grads[2], grads[3], grads[4], grads[5], grads[6], grads[7], grads[8])
```

```python
import functools

import jax
import jax.numpy as jnp
from jax import lax
from jax.experimental import pallas as pl
from jax.experimental.pallas import tpu as pltpu
from jax.sharding import PartitionSpec as P

epsilon = 1e-06
highest = lax.Precision.HIGHEST
big_negative = -1e30
bf16 = jnp.bfloat16
f32 = jnp.float32
i32 = jnp.int32


def mm(a, b, contract=(1, 0), precision=None):
    return lax.dot_general(
        a,
        b,
        (((contract[0],), (contract[1],)), ((), ())),
        preferred_element_type=f32,
        precision=precision,
    )


def iota(shape, dim):
    return lax.broadcasted_iota(i32, shape, dim)


def split_hi_lo(v):
    hi = v.astype(bf16).astype(f32)
    return hi, v - hi


def lane_block(rows, values, width=64):
    lane = iota((rows, width), 1)
    block = jnp.zeros((rows, width), f32)
    for i, v in enumerate(values):
        block = jnp.where(lane == i, v, block)
    return block


def run(body, outs, *args, smem=0, scratch=(), vmem=None):
    return pl.pallas_call(
        body,
        out_shape=[jax.ShapeDtypeStruct(s, d) for s, d in outs],
        in_specs=[pl.BlockSpec(memory_space=pltpu.SMEM)] * smem
        + [pl.BlockSpec(memory_space=pltpu.VMEM)] * (len(args) - smem),
        out_specs=[pl.BlockSpec(memory_space=pltpu.VMEM)] * len(outs),
        scratch_shapes=list(scratch),
        compiler_params=pltpu.CompilerParams(vmem_limit_bytes=vmem or 24 * 2**20),
    )(*args)


def route_kernel(routes_t, routes, dy, disp, dest_t, dest, *, experts, cap):
    tok = routes.shape[0]
    rt = routes_t[...]
    x_of = iota((experts, tok), 0)
    m0 = (rt[0:1] == x_of).astype(f32)
    m1 = (rt[1:2] == x_of).astype(f32)
    earlier = (iota((tok, tok), 0) < iota((tok, tok), 1)).astype(f32).astype(bf16)
    counts = mm((m0 + m1).astype(bf16), earlier)
    d0 = rt[0:1].astype(f32) * cap + jnp.sum(m0 * counts, axis=0, keepdims=True)
    d1 = rt[1:2].astype(f32) * cap + jnp.sum(m1 * counts, axis=0, keepdims=True)
    row = iota((experts * cap, tok), 0).astype(f32)
    place = ((row == d0) | (row == d1)).astype(f32).astype(bf16)
    disp[...] = mm(place, dy[...]).astype(bf16)
    dest_t[0:1, :] = d0
    dest_t[1:2, :] = d1
    rc = routes[...]
    x_lane = iota((tok, experts), 1)
    n0 = (rc[:, 0:1] == x_lane).astype(f32)
    n1 = (rc[:, 1:2] == x_lane).astype(f32)
    later = (iota((tok, tok), 1) < iota((tok, tok), 0)).astype(f32).astype(bf16)
    counts_c = mm(later, (n0 + n1).astype(bf16))
    dest[:, 0:1] = rc[:, 0:1].astype(f32) * cap + jnp.sum(n0 * counts_c, axis=1, keepdims=True)
    dest[:, 1:2] = rc[:, 1:2].astype(f32) * cap + jnp.sum(n1 * counts_c, axis=1, keepdims=True)


def skew(values, sign):
    n = values.shape[0]
    row = iota(values.shape, 0)
    bit = 1
    while bit < n:
        moved = pltpu.roll(values, bit if sign > 0 else n - bit, 1)
        values = jnp.where((row & bit) != 0, moved, values)
        bit *= 2
    return values


def attention_kernel(
    ids, lengths, x0, x1, x2, x3, gain, qkv_w, out_w, table, buckets,
    own, p1, p2, p3, h1, inv1, heads, probs, attended,
    xs, parts, *, n_t,
):
    tok, width = x0.shape
    n_heads = table.shape[1]
    size = width // n_heads
    model = n_t * width
    r = ids[0]
    for k, x in enumerate((x0, x1, x2, x3)):
        xs[lax.rem(r + n_t - k, n_t)] = x[...].astype(f32)
    total = jnp.zeros((tok, 1), f32)
    for s in range(n_t):
        total += jnp.sum(xs[s] * xs[s], axis=1, keepdims=True)
    inverse = lax.rsqrt(total / model + epsilon)
    inv1[...] = inverse
    for s in range(n_t):
        h1[s] = (xs[s] * inverse * gain[s]).astype(bf16)
    for j in range(3):
        acc = jnp.zeros((tok, width), f32)
        for s in range(n_t):
            acc += mm(h1[s], qkv_w[j, s * width:(s + 1) * width, :])
        heads[j] = acc.astype(bf16)
    key_pos = iota((tok, tok), 0)
    query_pos = iota((tok, tok), 1)
    end0 = lengths[0, 0]
    end1 = end0 + lengths[0, 1]
    seg_k = (key_pos >= end0).astype(i32) + (key_pos >= end1).astype(i32)
    seg_q = (query_pos >= end0).astype(i32) + (query_pos >= end1).astype(i32)
    allowed = (seg_k == seg_q) & (key_pos <= query_pos)
    hot = (buckets[...] == iota((table.shape[0], tok), 0)).astype(f32)
    for h in range(n_heads):
        cols = slice(h * size, (h + 1) * size)
        bias = jnp.sum(hot * table[:, h:h + 1], axis=0, keepdims=True)
        bias = skew(jnp.broadcast_to(bias, (tok, tok)), 1)
        scores = mm(heads[1, :, cols], heads[0, :, cols], (1, 1)) * (size ** -0.5) + bias
        scores = jnp.where(allowed, scores, big_negative)
        peak = jnp.max(scores, axis=0, keepdims=True)
        weights = jnp.exp(scores - peak)
        prob = weights / jnp.sum(weights, axis=0, keepdims=True)
        probs[h] = prob
        attended[:, cols] = mm(prob.astype(bf16), heads[2, :, cols], (0, 0)).astype(bf16)
    for s in range(n_t):
        parts[s] = mm(attended[...], out_w[:, s * width:(s + 1) * width])
    own[...] = parts[r]
    for k, p in ((1, p1), (2, p2), (3, p3)):
        p[...] = parts[lax.rem(r + k, n_t)].astype(bf16)


def dispatch_kernel(
    ids, own, p1, p2, p3, tokens, gain, router, routes, dest_t,
    rows, token_pack, residual, pack,
):
    tok, width = tokens.shape
    experts = router.shape[1]
    r = ids[0]
    res = tokens[...].astype(f32) + own[...] + (
        p1[...].astype(f32) + p2[...].astype(f32) + p3[...].astype(f32)
    )
    residual[...] = res
    scaled = (res * gain[r]).astype(bf16)
    square = jnp.sum(res * res, axis=1, keepdims=True)
    logits = mm(scaled, router[pl.ds(pl.multiple_of(r * width, 64), width), :])
    x_lane = iota((tok, experts), 1)
    rc = routes[...]
    zero = jnp.zeros_like(logits)
    c0 = jnp.sum(jnp.where(rc[:, 0:1] == x_lane, logits, zero), axis=1, keepdims=True)
    c1 = jnp.sum(jnp.where(rc[:, 1:2] == x_lane, logits, zero), axis=1, keepdims=True)
    stats = lane_block(tok, split_hi_lo(square) + split_hi_lo(c0 - c1)).astype(bf16)
    token_pack[:, 0:width] = res.astype(bf16)
    token_pack[:, width:] = stats
    pack[:, 0:width] = scaled
    pack[:, width:] = stats
    total_rows = rows.shape[0]
    row = iota((total_rows, tok), 0).astype(f32)
    place0 = (row == dest_t[0:1, :]).astype(f32)
    place1 = (row == dest_t[1:2, :]).astype(f32)
    both = mm((place0 + place1).astype(bf16), pack[...])
    signed = mm((place0 - place1).astype(bf16), pack[...])
    lane = iota(both.shape, 1)
    rows[...] = jnp.where(lane >= width + 2, signed, both).astype(bf16)


def total_stats(packs, width):
    total = packs[0][:, width:].astype(f32)
    for p in packs[1:]:
        total += p[:, width:].astype(f32)
    return total


def gelu_pair(a):
    c = 0.7978845608028654
    t = jnp.tanh(c * (a + 0.044715 * a * a * a))
    value = 0.5 * a * (1.0 + t)
    slope = 0.5 * (1.0 + t) + 0.5 * a * (1.0 - t * t) * c * (1.0 + 3 * 0.044715 * a * a)
    return value, slope


def expert_kernel(
    ids, h0, h1, h2, h3, g0, g1, g2, g3, up, down,
    c0, c1, c2, c3, u, z, de, da,
    hs, gs, chunks, *, n_t,
):
    width = g0.shape[1]
    model = n_t * width
    r = ids[0]
    packs = (h0, h1, h2, h3)
    for k, (h, g) in enumerate(zip(packs, (g0, g1, g2, g3))):
        s = lax.rem(r + n_t - k, n_t)
        hs[s] = h[:, 0:width].astype(f32)
        gs[s] = g[...].astype(f32)
    stats = total_stats(packs, width)
    inverse = lax.rsqrt((stats[:, 0:1] + stats[:, 1:2]) / model + epsilon)
    gate = 1.0 / (1.0 + jnp.exp(-inverse * (stats[:, 2:3] + stats[:, 3:4])))
    for s in range(n_t):
        cols = slice(s * width, (s + 1) * width)
        u[:, cols] = (hs[s] * inverse).astype(bf16)
        de[:, cols] = (gs[s] * gate).astype(bf16)
    value, slope = gelu_pair(mm(u[...], up[0]))
    z[...] = value.astype(bf16)
    da[...] = (mm(de[...], down[0], (1, 1)) * slope).astype(bf16)
    eo = mm(z[...], down[0]).astype(bf16)
    du = mm(da[...], up[0], (1, 1)).astype(bf16)
    for s in range(n_t):
        cols = slice(s * width, (s + 1) * width)
        chunks[s, :, 0:width] = eo[:, cols]
        chunks[s, :, width:] = du[:, cols]
    for k, c in enumerate((c0, c1, c2, c3)):
        c[...] = chunks[lax.rem(r + k, n_t)]


def expert_grad_kernel(u, z, de, da, up_grad, down_grad):
    up_grad[0] = mm(u[...], da[...], (0, 0))
    down_grad[0] = mm(z[...], de[...], (0, 0))


def gates_of(stats, model):
    inverse = lax.rsqrt((stats[:, 0:1] + stats[:, 1:2]) / model + epsilon)
    delta = inverse * (stats[:, 2:3] + stats[:, 3:4])
    return inverse, 1.0 / (1.0 + jnp.exp(-delta)), 1.0 / (1.0 + jnp.exp(delta))


def combine_kernel(t0, t1, t2, t3, back, dest, dy, residual, output, pack, *, n_t):
    tok, width = dy.shape
    inverse, gate0, gate1 = gates_of(total_stats((t0, t1, t2, t3), width), n_t * width)
    lane = iota((tok, back.shape[0]), 1).astype(f32)
    pick0 = (lane == dest[:, 0:1]).astype(f32)
    pick1 = (lane == dest[:, 1:2]).astype(f32)
    e0 = mm(pick0.astype(bf16), back[:, 0:width])
    e1 = mm(pick1.astype(bf16), back[:, 0:width])
    du = mm((pick0 + pick1).astype(bf16), back[:, width:])
    output[...] = (residual[...] + gate0 * e0 + gate1 * e1).astype(bf16)
    dy_cols = dy[...].astype(f32)
    dg0 = jnp.sum(dy_cols * e0, axis=1, keepdims=True)
    dg1 = jnp.sum(dy_cols * e1, axis=1, keepdims=True)
    pack[:, 0:width] = du.astype(bf16)
    pack[:, width:] = lane_block(tok, split_hi_lo(dg0) + split_hi_lo(dg1)).astype(bf16)


def backward_kernel(
    ids, b0, b1, b2, b3, t0, t1, t2, t3, y0, y1, y2, y3,
    routes, router, gain, out_w, qkv_w, heads, probs, inv1, attended, h1, buckets,
    c0, c1, c2, c3, dr1_own, d_proj, d_att, d_logits, gain_grad, d_scores,
    bs, ts, ys, dr, d_o, chunks, *, n_t,
):
    tok, width = y0.shape
    experts = router.shape[1]
    n_heads = probs.shape[0]
    size = width // n_heads
    model = n_t * width
    r = ids[0]
    for k in range(n_t):
        s = lax.rem(r + n_t - k, n_t)
        bs[s] = (b0, b1, b2, b3)[k][:, 0:width].astype(f32)
        ts[s] = (t0, t1, t2, t3)[k][:, 0:width].astype(f32)
        ys[s] = (y0, y1, y2, y3)[k][...].astype(f32)
    inverse, gate0, gate1 = gates_of(total_stats((t0, t1, t2, t3), width), model)
    back = total_stats((b0, b1, b2, b3), width)
    dg0 = back[:, 0:1] + back[:, 1:2]
    dg1 = back[:, 2:3] + back[:, 3:4]
    mean_gate = gate0 * dg0 + gate1 * dg1
    rc = routes[...]
    x_lane = iota((tok, experts), 1)
    dlog = jnp.where(rc[:, 0:1] == x_lane, gate0 * (dg0 - mean_gate), 0.0) + jnp.where(
        rc[:, 1:2] == x_lane, gate1 * (dg1 - mean_gate), 0.0
    )
    d_logits[...] = dlog
    dot = jnp.zeros((tok, 1), f32)
    for s in range(n_t):
        from_router = mm(
            dlog, router[s * width:(s + 1) * width, :].astype(f32), (1, 1), precision=highest
        )
        dh2 = bs[s] + from_router
        weighted = dh2 * gain[s]
        gain_grad[s] = jnp.sum(dh2 * ts[s] * inverse, axis=0, keepdims=True)
        dot += jnp.sum(weighted * ts[s], axis=1, keepdims=True)
        bs[s] = weighted
    dot = dot * (inverse * inverse * inverse / model)
    for s in range(n_t):
        value = ys[s] + inverse * bs[s] - ts[s] * dot
        dr[s] = value
        d_att[s] = value.astype(bf16)
    dr1_own[...] = dr[r]
    acc = jnp.zeros((tok, width), f32)
    for s in range(n_t):
        acc += mm(d_att[s], out_w[:, s * width:(s + 1) * width], (1, 1))
    d_o[...] = acc.astype(bf16)
    scale = size ** -0.5
    for h in range(n_heads):
        cols = slice(h * size, (h + 1) * size)
        q, k, v = heads[0, :, cols], heads[1, :, cols], heads[2, :, cols]
        d_oh = d_o[:, cols]
        prob = probs[h]
        d_prob = mm(v, d_oh, (1, 1))
        centre = jnp.sum(prob * d_prob, axis=0, keepdims=True)
        ds = (prob * (d_prob - centre)).astype(bf16)
        d_scores[h] = ds
        d_proj[0, :, cols] = (mm(ds, k, (0, 0)) * scale).astype(bf16)
        d_proj[1, :, cols] = (mm(ds, q) * scale).astype(bf16)
        d_proj[2, :, cols] = mm(prob.astype(bf16), d_oh).astype(bf16)
    row_dot = jnp.zeros((tok, 1), f32)
    for j in range(3):
        row_dot += jnp.sum(
            d_proj[j].astype(f32) * heads[j].astype(f32), axis=1, keepdims=True
        )
    stats = lane_block(tok, split_hi_lo(row_dot)).astype(bf16)
    for s in range(n_t):
        acc = jnp.zeros((tok, width), f32)
        for j in range(3):
            acc += mm(d_proj[j], qkv_w[j, s * width:(s + 1) * width, :], (1, 1))
        chunks[s, :, 0:width] = acc.astype(bf16)
        chunks[s, :, width:] = stats
    for k, c in enumerate((c0, c1, c2, c3)):
        c[...] = chunks[lax.rem(r + k, n_t)]


def weight_grad_kernel(
    ids, t0, t1, t2, t3, d_logits, gain, h1, d_proj, attended, d_att, d_scores, buckets, qkv_w,
    qkv_grad, out_grad, first, rel_grad, router_grad, ts, *, n_t,
):
    tok, width = t0.shape[0], d_proj.shape[2]
    r = ids[0]
    packs = (t0, t1, t2, t3)
    for k, t in enumerate(packs):
        ts[lax.rem(r + n_t - k, n_t)] = t[:, 0:width].astype(f32)
    inverse, _, _ = gates_of(total_stats(packs, width), n_t * width)
    ones = jnp.ones((8, width), f32)
    for s in range(n_t):
        rows = slice(s * width, (s + 1) * width)
        product = jnp.zeros((width, width), f32)
        for j in range(3):
            grad = mm(h1[s], d_proj[j], (0, 0))
            qkv_grad[j, rows, :] = grad.astype(bf16)
            product += grad * qkv_w[j, rows, :].astype(f32)
        first[s] = mm(ones, product, (1, 1), precision=highest)[0:1] / gain[0, s]
        out_grad[:, rows] = mm(attended[...], d_att[s], (0, 0)).astype(bf16)
        normed = (ts[s] * inverse * gain[1, s]).astype(bf16).astype(f32)
        router_grad[rows, :] = mm(normed, d_logits[...], (0, 0), precision=highest)
    hot = (buckets[...] == iota((rel_grad.shape[0], tok), 0)).astype(f32)
    for h in range(d_scores.shape[0]):
        diagonal = jnp.sum(skew(d_scores[h].astype(f32), -1), axis=0, keepdims=True)
        rel_grad[:, h:h + 1] = jnp.sum(hot * diagonal, axis=1, keepdims=True)


def per_device(
    tokens,
    first_gain,
    second_gain,
    qkv_weight,
    out_weight,
    rel_table,
    router_weight,
    up_weight,
    down_weight,
    routes,
    lengths,
    bucket_ids,
    cotangent,
    *,
    n_t,
    n_e,
):
    tok, width = tokens.shape
    model = n_t * width
    experts = router_weight.shape[1]
    cap = 5 * tok // (2 * experts)
    rows = experts * cap
    n_heads = rel_table.shape[1]
    n_buckets = rel_table.shape[0]

    def shift(v, k):
        return lax.ppermute(v, "tensor", [(i, (i + k) % n_t) for i in range(n_t)])

    def around(v):
        return [v] + [shift(v, k) for k in range(1, n_t)]

    def exchange(v):
        w = v.shape[-1]
        return lax.all_to_all(
            v.reshape(n_e, rows // n_e, w), "expert", split_axis=0, concat_axis=0, tiled=True
        ).reshape(rows, w)

    ids = jnp.stack([lax.axis_index("tensor"), lax.axis_index("expert")]).astype(i32)
    gain_one = first_gain.reshape(n_t, 1, width)
    gain_two = second_gain.reshape(n_t, 1, width)
    buckets = jnp.pad(bucket_ids, (0, tok - bucket_ids.shape[0]), constant_values=-1)[None, :]

    xs = around(tokens)
    dys = around(cotangent)
    dy_rows, dest_t, dest = run(
        functools.partial(route_kernel, experts=experts, cap=cap),
        [((rows, width), bf16), ((2, tok), f32), ((tok, 2), f32)],
        routes.T, routes, cotangent,
    )
    dy_rows = around(exchange(dy_rows))

    own, p1, p2, p3, h1, inv1, heads, probs, attended = run(
        functools.partial(attention_kernel, n_t=n_t),
        [((tok, width), f32)]
        + [((tok, width), bf16)] * 3
        + [
            ((n_t, tok, width), bf16),
            ((tok, 1), f32),
            ((3, tok, width), bf16),
            ((n_heads, tok, tok), f32),
            ((tok, width), bf16),
        ],
        ids, lengths, *xs, gain_one, qkv_weight, out_weight, rel_table, buckets,
        smem=2,
        scratch=[pltpu.VMEM((n_t, tok, width), f32), pltpu.VMEM((n_t, tok, width), f32)],
    )
    got = [shift(p, k) for k, p in ((1, p1), (2, p2), (3, p3))]
    send_rows, token_pack, residual = run(
        dispatch_kernel,
        [((rows, 256), bf16), ((tok, 256), bf16), ((tok, width), f32)],
        ids, own, *got, tokens, gain_two, router_weight, routes, dest_t,
        smem=1,
        scratch=[pltpu.VMEM((tok, 256), bf16)],
    )
    in_rows = around(exchange(send_rows))
    token_packs = around(token_pack)

    c0, c1, c2, c3, u, z, de, da = run(
        functools.partial(expert_kernel, n_t=n_t),
        [((rows, 2 * width), bf16)] * 4 + [((rows, model), bf16)] * 4,
        ids, *in_rows, *dy_rows, up_weight, down_weight,
        smem=1,
        scratch=[
            pltpu.VMEM((n_t, rows, width), f32),
            pltpu.VMEM((n_t, rows, width), f32),
            pltpu.VMEM((n_t, rows, 2 * width), bf16),
        ],
    )
    got = [shift(c, k) for k, c in ((1, c1), (2, c2), (3, c3))]
    summed = c0.astype(f32)
    for c in got:
        summed = summed + c.astype(f32)
    back = exchange(summed.astype(bf16))
    up_grad, down_grad = run(
        expert_grad_kernel,
        [(up_weight.shape, f32), (down_weight.shape, f32)],
        u, z, de, da,
    )
    output, back_pack = run(
        functools.partial(combine_kernel, n_t=n_t),
        [((tok, width), bf16), ((tok, 256), bf16)],
        *token_packs, back, dest, cotangent, residual,
    )
    back_packs = around(back_pack)

    c0, c1, c2, c3, dr1, d_proj, d_att, d_logits, second, d_scores = run(
        functools.partial(backward_kernel, n_t=n_t),
        [((tok, 256), bf16)] * 4
        + [
            ((tok, width), f32),
            ((3, tok, width), bf16),
            ((n_t, tok, width), bf16),
            ((tok, experts), f32),
            ((n_t, 1, width), f32),
            ((n_heads, tok, tok), bf16),
        ],
        ids, *back_packs, *token_packs, *dys, routes, router_weight, gain_two, out_weight,
        qkv_weight, heads, probs, inv1, attended, h1, buckets,
        smem=1,
        scratch=[pltpu.VMEM((n_t, tok, width), f32)] * 4
        + [pltpu.VMEM((tok, width), bf16), pltpu.VMEM((n_t, tok, 256), bf16)],
    )
    got = [shift(c, k) for k, c in ((1, c1), (2, c2), (3, c3))]
    qkv_grad, out_grad, first, rel_grad, router_grad = run(
        functools.partial(weight_grad_kernel, n_t=n_t),
        [
            (qkv_weight.shape, bf16),
            (out_weight.shape, bf16),
            ((n_t, 1, width), f32),
            ((n_buckets, n_heads), f32),
            (router_weight.shape, f32),
        ],
        ids, *token_packs, d_logits, jnp.stack([gain_one, gain_two]), h1, d_proj, attended, d_att,
        d_scores, buckets, qkv_weight,
        smem=1,
        scratch=[pltpu.VMEM((n_t, tok, width), f32)],
    )
    total = c0.astype(f32)
    for c in got:
        total = total + c.astype(f32)
    row_dot = (total[:, width:width + 1] + total[:, width + 1:width + 2]) / model
    gain_cols = lax.dynamic_index_in_dim(gain_one, lax.axis_index("tensor"), 0, False)
    input_grad = (
        dr1 + inv1 * (total[:, :width] * gain_cols) - tokens.astype(f32) * inv1**2 * row_dot
    )
    qkv_grad, out_grad = lax.psum((qkv_grad, out_grad), "expert")
    second, rel_grad, router_grad = lax.psum((second, rel_grad, router_grad), "expert")
    first = lax.psum(first, ("expert", "tensor"))
    return (
        output,
        input_grad,
        first.reshape(model),
        second.reshape(model),
        qkv_grad.astype(f32),
        out_grad.astype(f32),
        rel_grad,
        router_grad,
        up_grad,
        down_grad,
    )


def solution(mesh):
    placed = (
        P("expert", "tensor"),
        P(),
        P(),
        P(None, None, "tensor"),
        P("tensor", None),
        P(None, "tensor"),
        P(),
        P("expert", None, "tensor"),
        P("expert", "tensor", None),
        P("expert", None),
        P("expert", None),
        P(),
        P("expert", "tensor"),
    )
    return jax.shard_map(
        functools.partial(per_device, n_t=mesh.shape["tensor"], n_e=mesh.shape["expert"]),
        mesh=mesh,
        in_specs=placed,
        out_specs=(
            P("expert", "tensor"),
            P("expert", "tensor"),
            P(),
            P(),
            P(None, None, "tensor"),
            P("tensor", None),
            P(None, "tensor"),
            P(),
            P("expert", None, "tensor"),
            P("expert", "tensor", None),
        ),
        check_vma=False,
    )
```

```python
import functools
import math

import jax
import jax.numpy as jnp
from jax import lax
from jax.experimental import pallas as pl
from jax.experimental.pallas import tpu as pltpu
from jax.sharding import PartitionSpec as P

epsilon = 1e-06
highest = lax.Precision.HIGHEST
big_negative = -1e30
bf16 = jnp.bfloat16
f32 = jnp.float32
i32 = jnp.int32


def mm(a, b, contract=(1, 0), precision=None):
    return lax.dot_general(
        a,
        b,
        (((contract[0],), (contract[1],)), ((), ())),
        preferred_element_type=f32,
        precision=precision,
    )


def iota(shape, dim):
    return lax.broadcasted_iota(i32, shape, dim)


def split_hi_lo(v):
    hi = v.astype(bf16).astype(f32)
    return hi, v - hi


def row_block(values, rows=16):
    lanes = values[0].shape[1]
    row = iota((rows, lanes), 0)
    block = jnp.zeros((rows, lanes), f32)
    for i, v in enumerate(values):
        block = jnp.where(row == i, v, block)
    return block


def run(body, outs, *args, smem=0, scratch=(), flops=0):
    moved = sum(a.size * a.dtype.itemsize for a in args)
    moved += sum(math.prod(s) * jnp.dtype(d).itemsize for s, d in outs)
    return pl.pallas_call(
        body,
        out_shape=[jax.ShapeDtypeStruct(s, d) for s, d in outs],
        in_specs=[pl.BlockSpec(memory_space=pltpu.SMEM)] * smem
        + [pl.BlockSpec()] * (len(args) - smem),
        out_specs=[pl.BlockSpec()] * len(outs),
        scratch_shapes=list(scratch),
        compiler_params=pltpu.CompilerParams(vmem_limit_bytes=32 * 2**20),
        cost_estimate=pl.CostEstimate(flops=flops, bytes_accessed=moved, transcendentals=0),
    )(*args)


def column_of(row, out):
    for c in range(row.shape[1] // 128):
        part = jnp.broadcast_to(row[:, c * 128:(c + 1) * 128], (128, 128))
        part = jnp.where(iota((128, 128), 0) == iota((128, 128), 1), part, 0.0)
        out[c * 128:(c + 1) * 128, :] = jnp.sum(part, axis=1, keepdims=True)


def skew(values, sign):
    n = values.shape[0]
    row = iota(values.shape, 0)
    bit = 1
    while bit < n:
        moved = pltpu.roll(values, bit if sign > 0 else n - bit, 1)
        values = jnp.where((row & bit) != 0, moved, values)
        bit *= 2
    return values


def bucket_hot(buckets, padded, count):
    padded[...] = jnp.full(padded.shape, -1, i32)
    padded[:, 0:buckets.shape[1]] = buckets[...]
    return (padded[...] == iota((count, padded.shape[1]), 0)).astype(f32)


def prepare_kernel(lengths, gain, out_w, table, buckets, gain_col, out_wt, bias, padded):
    tok = bias.shape[1]
    column_of(gain[...], gain_col)
    out_wt[...] = out_w[...].astype(f32).T.astype(bf16)
    key_pos = iota((tok, tok), 0)
    query_pos = iota((tok, tok), 1)
    end0 = lengths[0, 0]
    end1 = end0 + lengths[0, 1]
    seg_k = (key_pos >= end0).astype(i32) + (key_pos >= end1).astype(i32)
    seg_q = (query_pos >= end0).astype(i32) + (query_pos >= end1).astype(i32)
    allowed = (seg_k == seg_q) & (key_pos <= query_pos)
    hot = bucket_hot(buckets, padded, table.shape[1])
    per_head = mm(table[...], hot, precision=highest)
    for h in range(table.shape[0]):
        full = skew(jnp.broadcast_to(per_head[h:h + 1], (tok, tok)), 1)
        bias[h] = jnp.where(allowed, full, big_negative)


def route_kernel(
    ids, routes, dy, router, gain, qkv_w, after, *refs, experts, cap, n_e, direct, n_t,
):
    pieces = list(refs[:-5])
    dest, gain_col, rw_own, qkv_wt, chunks = refs[-5:]
    tok = routes.shape[1]
    width = dy.shape[0]
    rows = experts * cap
    e = ids[1].astype(f32)
    rt = routes[...]
    x_of = iota((experts, tok), 0)
    m0 = (rt[0:1] == x_of).astype(f32)
    m1 = (rt[1:2] == x_of).astype(f32)
    earlier = (iota((tok, tok), 0) < iota((tok, tok), 1)).astype(f32).astype(bf16)
    counts = mm((m0 + m1).astype(bf16), earlier)
    send, back = [], []
    for i, m in enumerate((m0, m1)):
        slot = jnp.sum(m * counts, axis=0, keepdims=True)
        owner = rt[i:i + 1].astype(f32)
        if direct:
            ahead = owner - e
            behind = e - owner
            send.append(jnp.where(ahead < 0, ahead + n_e, ahead) * cap + slot)
            back.append(jnp.where(behind < 0, behind + n_e, behind) * cap + slot)
        else:
            send.append(owner * cap + slot)
            back.append(owner * cap + slot)
    dest[...] = row_block(send + back, 8)
    row = iota((rows, tok), 0).astype(f32)
    place = ((row == send[0]) | (row == send[1])).astype(f32).astype(bf16)
    full = mm(place, dy[...], (1, 1))
    size = rows // len(pieces)
    for k, piece in enumerate(pieces):
        piece[...] = full[k * size:(k + 1) * size].astype(bf16)
    column_of(gain[...], gain_col)
    wide = router[...].astype(f32)
    for s in range(n_t):
        chunks[s] = wide[:, s * width:(s + 1) * width]
    rw_own[...] = chunks[ids[0]].astype(bf16)
    qkv_wt[...] = qkv_w[...].astype(f32).T.astype(bf16)


def chunk(ref, s, width):
    return ref.at[pl.ds(pl.multiple_of(s * width, 64), width)]


def attention_kernel(
    ids, x0, x1, x2, x3, gain, qkv_w, out_wt, bias,
    own, p1, p2, p3, h1, inv1, heads, probs, attended,
    xs, parts, *, n_t,
):
    width, tok = x0.shape
    n_heads = bias.shape[0]
    size = width // n_heads
    model = n_t * width
    r = ids[0]
    for k, x in enumerate((x0, x1, x2, x3)):
        chunk(xs, lax.rem(r + n_t - k, n_t), width)[...] = x[...].astype(f32)
    inverse = lax.rsqrt(jnp.sum(xs[...] * xs[...], axis=0, keepdims=True) / model + epsilon)
    inv1[...] = inverse
    h1[...] = (xs[...] * inverse * gain[...]).astype(bf16)
    heads[...] = mm(qkv_w[...], h1[...]).astype(bf16)
    for h in range(n_heads):
        q, k, v = (heads[j * width + h * size:j * width + (h + 1) * size] for j in range(3))
        scores = mm(k, q, (0, 0)) * (size ** -0.5) + bias[h]
        weights = jnp.exp(scores - jnp.max(scores, axis=0, keepdims=True))
        prob = weights / jnp.sum(weights, axis=0, keepdims=True)
        probs[h] = prob
        attended[h * size:(h + 1) * size] = mm(v, prob.astype(bf16)).astype(bf16)
    parts[...] = mm(out_wt[...], attended[...])
    own[...] = chunk(parts, r, width)[...]
    for k, p in ((1, p1), (2, p2), (3, p3)):
        p[...] = chunk(parts, lax.rem(r + k, n_t), width)[...].astype(bf16)


def dispatch_kernel(
    ids, own, p1, p2, p3, x, dy, gain, rw_own, routes, dest, *refs
):
    pieces = refs[:-3]
    token_pack, residual, pack = refs[-3:]
    width, tok = x.shape
    experts = rw_own.shape[0]
    r = ids[0]
    res = x[...].astype(f32) + own[...] + (
        p1[...].astype(f32) + p2[...].astype(f32) + p3[...].astype(f32)
    )
    residual[...] = res
    scaled = (res * chunk(gain, r, width)[...]).astype(bf16)
    square = jnp.sum(res * res, axis=0, keepdims=True)
    logits = mm(rw_own[...], scaled)
    x_of = iota((experts, tok), 0)
    c0 = jnp.sum(jnp.where(routes[0:1, :] == x_of, logits, 0.0), axis=0, keepdims=True)
    c1 = jnp.sum(jnp.where(routes[1:2, :] == x_of, logits, 0.0), axis=0, keepdims=True)
    stats = row_block(split_hi_lo(square) + split_hi_lo(c0 - c1)).astype(bf16)
    token_pack[0:width] = res.astype(bf16)
    token_pack[width:width + 16] = stats
    token_pack[width + 16:] = dy[...]
    pack[0:width] = scaled
    pack[width:] = stats
    size = pieces[0].shape[0]
    row = iota((size * len(pieces), tok), 0).astype(f32)
    place0 = (row == dest[0:1, :]).astype(f32)
    place1 = (row == dest[1:2, :]).astype(f32)
    both = mm((place0 + place1).astype(bf16), pack[...], (1, 1))
    signed = mm((place0 - place1).astype(bf16), pack[...], (1, 1))
    full = jnp.where(iota(both.shape, 1) >= width + 2, signed, both)
    for k, piece in enumerate(pieces):
        piece[...] = full[k * size:(k + 1) * size].astype(bf16)


def gelu_pair(a):
    c = 0.7978845608028654
    t = jnp.tanh(c * (a + 0.044715 * a * a * a))
    value = 0.5 * a * (1.0 + t)
    slope = 0.5 * (1.0 + t) + 0.5 * a * (1.0 - t * t) * c * (1.0 + 3 * 0.044715 * a * a)
    return value, slope


def expert_kernel(
    ids, h0, h1, h2, h3, g0, g1, g2, g3, up, down,
    c0, c1, c2, c3, u, z, de, da,
    hs, gs, chunks, *, n_t,
):
    width = g0.shape[1]
    model = n_t * width
    r = ids[0]
    packs = (h0, h1, h2, h3)
    for k, (h, g) in enumerate(zip(packs, (g0, g1, g2, g3))):
        s = lax.rem(r + n_t - k, n_t)
        hs[s] = h[:, 0:width].astype(f32)
        gs[s] = g[...].astype(f32)
    stats = h0[:, width:].astype(f32)
    for h in packs[1:]:
        stats += h[:, width:].astype(f32)
    inverse = lax.rsqrt((stats[:, 0:1] + stats[:, 1:2]) / model + epsilon)
    gate = 1.0 / (1.0 + jnp.exp(-inverse * (stats[:, 2:3] + stats[:, 3:4])))
    for s in range(n_t):
        cols = slice(s * width, (s + 1) * width)
        u[:, cols] = (hs[s] * inverse).astype(bf16)
        de[:, cols] = (gs[s] * gate).astype(bf16)
    value, slope = gelu_pair(mm(u[...], up[0]))
    z[...] = value.astype(bf16)
    da[...] = (mm(de[...], down[0], (1, 1)) * slope).astype(bf16)
    eo = mm(z[...], down[0]).astype(bf16)
    du = mm(da[...], up[0], (1, 1)).astype(bf16)
    for s in range(n_t):
        cols = slice(s * width, (s + 1) * width)
        chunks[s, :, 0:width] = eo[:, cols]
        chunks[s, :, width:] = du[:, cols]
    for k, c in enumerate((c0, c1, c2, c3)):
        c[...] = chunks[lax.rem(r + k, n_t)]


def expert_grad_kernel(u, z, de, da, up_grad, down_grad):
    up_grad[0] = mm(u[...], da[...], (0, 0))
    down_grad[0] = mm(z[...], de[...], (0, 0))


def join_kernel(*refs):
    pieces, out = refs[:-1], refs[-1]
    out[...] = jnp.concatenate([p[...].astype(f32) for p in pieces], axis=0).astype(bf16)


def expert_sum_kernel(c0, c1, c2, c3, *pieces):
    total = c0[...].astype(f32) + c1[...].astype(f32) + (c2[...].astype(f32) + c3[...].astype(f32))
    count = len(pieces)
    size = total.shape[0] // count
    for k, piece in enumerate(pieces):
        j = (count - k) % count
        piece[...] = total[j * size:(j + 1) * size].astype(bf16)


def total_stats(packs, width):
    total = packs[0][width:width + 16].astype(f32)
    for p in packs[1:]:
        total += p[width:width + 16].astype(f32)
    return total


def gates_of(stats, model):
    inverse = lax.rsqrt((stats[0:1] + stats[1:2]) / model + epsilon)
    delta = inverse * (stats[2:3] + stats[3:4])
    return inverse, 1.0 / (1.0 + jnp.exp(-delta)), 1.0 / (1.0 + jnp.exp(delta))


def combine_kernel(t0, t1, t2, t3, dest, dy, residual, *refs, n_t):
    pieces, (output, pack) = refs[:-2], refs[-2:]
    width, tok = dy.shape
    _, gate0, gate1 = gates_of(total_stats((t0, t1, t2, t3), width), n_t * width)
    back = jnp.concatenate([p[...].astype(f32) for p in pieces], axis=0).astype(bf16)
    row = iota((back.shape[0], tok), 0).astype(f32)
    pick0 = (row == dest[2:3, :]).astype(f32).astype(bf16)
    pick1 = (row == dest[3:4, :]).astype(f32).astype(bf16)
    got0 = mm(back, pick0, (0, 0))
    got1 = mm(back, pick1, (0, 0))
    e0, e1 = got0[0:width], got1[0:width]
    output[...] = (residual[...] + gate0 * e0 + gate1 * e1).astype(bf16)
    dy_own = dy[...].astype(f32)
    dg0 = jnp.sum(dy_own * e0, axis=0, keepdims=True)
    dg1 = jnp.sum(dy_own * e1, axis=0, keepdims=True)
    pack[0:width] = (got0[width:] + got1[width:]).astype(bf16)
    pack[width:] = row_block(split_hi_lo(dg0) + split_hi_lo(dg1)).astype(bf16)


def backward_kernel(
    ids, b0, b1, b2, b3, t0, t1, t2, t3,
    routes, router, gain, out_w, qkv_wt, heads, probs,
    c0, c1, c2, c3, dr1_own, d_proj, d_att, d_logits, gain_terms, d_scores,
    bs, ts, ys, dr, *, n_t,
):
    width = dr1_own.shape[0]
    tok = b0.shape[1]
    experts = router.shape[0]
    n_heads = probs.shape[0]
    size = width // n_heads
    model = n_t * width
    r = ids[0]
    packs, tokens = (b0, b1, b2, b3), (t0, t1, t2, t3)
    for k in range(n_t):
        s = lax.rem(r + n_t - k, n_t)
        chunk(bs, s, width)[...] = packs[k][0:width].astype(f32)
        chunk(ts, s, width)[...] = tokens[k][0:width].astype(f32)
        chunk(ys, s, width)[...] = tokens[k][width + 16:].astype(f32)
    inverse, gate0, gate1 = gates_of(total_stats(tokens, width), model)
    back = total_stats(packs, width)
    dg0 = back[0:1] + back[1:2]
    dg1 = back[2:3] + back[3:4]
    mean_gate = gate0 * dg0 + gate1 * dg1
    x_of = iota((experts, tok), 0)
    dlog = jnp.where(routes[0:1, :] == x_of, gate0 * (dg0 - mean_gate), 0.0) + jnp.where(
        routes[1:2, :] == x_of, gate1 * (dg1 - mean_gate), 0.0
    )
    d_logits[...] = dlog
    dh2 = bs[...] + mm(router[...].astype(f32), dlog, (0, 0), precision=highest)
    res = ts[...]
    gain_terms[...] = dh2 * res * inverse
    weighted = dh2 * gain[...]
    dot = jnp.sum(weighted * res, axis=0, keepdims=True) * (inverse**3 / model)
    dr[...] = ys[...] + inverse * weighted - res * dot
    d_att[...] = dr[...].astype(bf16)
    dr1_own[...] = chunk(dr, r, width)[...]
    d_o = mm(out_w[...], d_att[...]).astype(bf16)
    scale = size ** -0.5
    for h in range(n_heads):
        q, k, v = (heads[j * width + h * size:j * width + (h + 1) * size] for j in range(3))
        d_oh = d_o[h * size:(h + 1) * size]
        prob = probs[h]
        d_prob = mm(v, d_oh, (0, 0))
        centre = jnp.sum(prob * d_prob, axis=0, keepdims=True)
        ds = (prob * (d_prob - centre)).astype(bf16)
        d_scores[h] = ds
        here = h * size
        d_proj[here:here + size] = (mm(k, ds) * scale).astype(bf16)
        here += width
        d_proj[here:here + size] = (mm(q, ds, (1, 1)) * scale).astype(bf16)
        here += width
        d_proj[here:here + size] = mm(d_oh, prob.astype(bf16), (1, 1)).astype(bf16)
    row_dot = jnp.sum(
        d_proj[...].astype(f32) * heads[...].astype(f32), axis=0, keepdims=True
    )
    stats = row_block(split_hi_lo(row_dot)).astype(bf16)
    dr[...] = mm(qkv_wt[...], d_proj[...])
    for k, c in enumerate((c0, c1, c2, c3)):
        c[0:width] = chunk(dr, lax.rem(r + k, n_t), width)[...].astype(bf16)
        c[width:] = stats


def small_grad_kernel(
    ids, t0, t1, t2, t3, d_logits, gain_terms, gain1_row, gain2, h1, d_proj, attended, d_att,
    d_scores, buckets, qkv_w, small, out_grad, ts, padded, *, n_t, n_buckets,
):
    packs = (t0, t1, t2, t3)
    width = attended.shape[0]
    model = n_t * width
    experts = d_logits.shape[0]
    tok = t0.shape[1]
    r = ids[0]
    for k, t in enumerate(packs):
        chunk(ts, lax.rem(r + n_t - k, n_t), width)[...] = t[0:width].astype(f32)
    out_grad[...] = mm(attended[...], d_att[...], (1, 1)).astype(out_grad.dtype)
    inverse, _, _ = gates_of(total_stats(packs, width), model)
    normed = (ts[...] * inverse * gain2[...]).astype(bf16).astype(f32)
    small[0:experts] = mm(d_logits[...], normed, (1, 1), precision=highest)
    ones = jnp.ones((8, tok), f32)
    small[experts:] = jnp.zeros((small.shape[0] - experts, model), f32)
    small[experts:experts + 1] = mm(ones, gain_terms[...], (1, 1), precision=highest)[0:1]
    grad = mm(d_proj[...], h1[...], (1, 1))
    first = jnp.sum(grad * qkv_w[...].astype(f32), axis=0, keepdims=True)
    small[experts + 1:experts + 2] = first / gain1_row[...]
    hot = bucket_hot(buckets, padded, n_buckets)
    for h in range(d_scores.shape[0]):
        diagonal = jnp.sum(skew(d_scores[h].astype(f32), -1), axis=0, keepdims=True)
        per_bucket = mm(jnp.broadcast_to(diagonal, (8, tok)), hot, (1, 1), precision=highest)
        here = experts + 2 + h
        small[here:here + 1, 0:n_buckets] = per_bucket[0:1]


def small_sum_kernel(*refs):
    parts, out = refs[:-1], refs[-1]
    total = parts[0][...]
    for p in parts[1:]:
        total = total + p[...]
    out[...] = total


def input_grad_kernel(ids, c0, c1, c2, c3, dr1, inv1, x, gain, out, *, n_t):
    width = x.shape[0]
    total = c0[...].astype(f32) + c1[...].astype(f32) + (c2[...].astype(f32) + c3[...].astype(f32))
    row_dot = (total[width:width + 1] + total[width + 1:width + 2]) / (n_t * width)
    inverse = inv1[...]
    weighted = total[0:width] * chunk(gain, ids[0], width)[...]
    out[...] = dr1[...] + inverse * weighted - x[...].astype(f32) * (inverse * inverse * row_dot)


def qkv_grad_kernel(*refs):
    out = refs[-1]
    count = (len(refs) - 1) // 2
    total = mm(refs[0][...], refs[count][...], (1, 1))
    for k in range(1, count):
        total += mm(refs[k][...], refs[count + k][...], (1, 1))
    out[...] = total


def per_device(
    tokens,
    first_gain,
    second_gain,
    qkv_weight,
    out_weight,
    rel_table,
    router_weight,
    up_weight,
    down_weight,
    routes,
    lengths,
    bucket_ids,
    cotangent,
    *,
    n_t,
    n_e,
):
    tok, width = tokens.shape
    model = n_t * width
    inner = 3 * width
    experts = router_weight.shape[1]
    cap = 5 * tok // (2 * experts)
    rows = experts * cap
    n_heads = rel_table.shape[1]
    n_buckets = rel_table.shape[0]
    direct = n_e <= 8 and cap % 8 == 0
    n_pieces = n_e if direct else 1
    padded = pltpu.VMEM((1, tok), i32)

    def shift(v, k, axis="tensor", n=n_t):
        return lax.ppermute(v, axis, [(i, (i + k) % n) for i in range(n)])

    def around(v):
        return [v] + [shift(v, k) for k in range(1, n_t)]

    def around_experts(v):
        return [v] + [shift(v, k, "expert", n_e) for k in range(1, n_e)]

    def exchange(pieces):
        if direct:
            return list(pieces[:1]) + [
                shift(p, k, "expert", n_e) for k, p in enumerate(pieces) if k
            ]
        w = pieces[0].shape[-1]
        v = pieces[0].reshape(n_e, rows // n_e, w)
        v = lax.all_to_all(v, "expert", split_axis=0, concat_axis=0, tiled=True)
        return [v.reshape(rows, w)]

    def join(pieces):
        if len(pieces) == 1:
            return pieces[0]
        return run(join_kernel, [((rows, pieces[0].shape[1]), bf16)], *pieces)[0]

    def piece_shapes(w):
        return [((rows // n_pieces, w), bf16)] * n_pieces

    ids = jnp.stack([lax.axis_index("tensor"), lax.axis_index("expert")]).astype(i32)
    x = tokens.T
    dy = cotangent.T
    qkv_w = qkv_weight.transpose(0, 2, 1).reshape(inner, model)
    router = router_weight.T
    table = rel_table.T
    routes_t = routes.T
    gain1_row = first_gain.reshape(1, model)
    gain2_row = second_gain.reshape(1, model)
    buckets = bucket_ids.reshape(1, -1)

    xs = around(x)
    gain1, out_wt, bias = run(
        prepare_kernel,
        [((model, 1), f32), ((model, width), bf16), ((n_heads, tok, tok), f32)],
        lengths, gain1_row, out_weight, table, buckets,
        smem=1, scratch=[padded],
    )
    own, p1, p2, p3, h1, inv1, heads, probs, attended = run(
        functools.partial(attention_kernel, n_t=n_t),
        [((width, tok), f32)]
        + [((width, tok), bf16)] * 3
        + [
            ((model, tok), bf16),
            ((1, tok), f32),
            ((inner, tok), bf16),
            ((n_heads, tok, tok), f32),
            ((width, tok), bf16),
        ],
        ids, *xs, gain1, qkv_w, out_wt, bias,
        smem=1,
        scratch=[pltpu.VMEM((model, tok), f32), pltpu.VMEM((model, tok), f32)],
    )
    got = [shift(p, k) for k, p in ((1, p1), (2, p2), (3, p3))]
    *dy_pieces, dest, gain2, rw_own, qkv_wt = run(
        functools.partial(
            route_kernel, experts=experts, cap=cap, n_e=n_e, direct=direct, n_t=n_t
        ),
        piece_shapes(width)
        + [
            ((8, tok), f32),
            ((model, 1), f32),
            ((experts, width), bf16),
            ((model, inner), bf16),
        ],
        ids, routes_t, dy, router, gain2_row, qkv_w, inv1,
        smem=1, scratch=[pltpu.VMEM((n_t, experts, width), f32)],
    )
    dy_rows = around(join(exchange(dy_pieces)))
    *row_pieces, token_pack, residual = run(
        dispatch_kernel,
        piece_shapes(width + 16) + [((2 * width + 16, tok), bf16), ((width, tok), f32)],
        ids, own, *got, x, dy, gain2, rw_own, routes_t, dest,
        smem=1, scratch=[pltpu.VMEM((width + 16, tok), bf16)],
    )
    in_rows = around(join(exchange(row_pieces)))
    token_packs = around(token_pack)

    c0, c1, c2, c3, u, z, de, da = run(
        functools.partial(expert_kernel, n_t=n_t),
        [((rows, 2 * width), bf16)] * 4 + [((rows, model), bf16)] * 4,
        ids, *in_rows, *dy_rows, up_weight, down_weight,
        smem=1,
        scratch=[
            pltpu.VMEM((n_t, rows, width), f32),
            pltpu.VMEM((n_t, rows, width), f32),
            pltpu.VMEM((n_t, rows, 2 * width), bf16),
        ],
    )
    got = [shift(c, k) for k, c in ((1, c1), (2, c2), (3, c3))]
    if direct:
        h1_late, _ = lax.optimization_barrier((h1, c0))
        h1_all = around_experts(h1_late)
    up_grad, down_grad = run(
        expert_grad_kernel,
        [(up_weight.shape, f32), (down_weight.shape, f32)],
        u, z, de, da,
    )
    back = exchange(run(expert_sum_kernel, piece_shapes(2 * width), c0, *got))
    output, back_pack = run(
        functools.partial(combine_kernel, n_t=n_t),
        [((width, tok), bf16), ((width + 16, tok), bf16)],
        *token_packs, dest, dy, residual, *back,
    )
    back_packs = around(back_pack)

    c0, c1, c2, c3, dr1, d_proj, d_att, d_logits, gain_terms, d_scores = run(
        functools.partial(backward_kernel, n_t=n_t),
        [((width + 16, tok), bf16)] * 4
        + [
            ((width, tok), f32),
            ((inner, tok), bf16),
            ((model, tok), bf16),
            ((experts, tok), f32),
            ((model, tok), f32),
            ((n_heads, tok, tok), bf16),
        ],
        ids, *back_packs, *token_packs, routes_t, router, gain2, out_weight, qkv_wt, heads, probs,
        smem=1,
        scratch=[pltpu.VMEM((model, tok), f32)] * 4,
    )
    got = [shift(c, k) for k, c in ((1, c1), (2, c2), (3, c3))]
    if direct:
        d_proj_all = around_experts(d_proj)
    small, out_part = run(
        functools.partial(small_grad_kernel, n_t=n_t, n_buckets=n_buckets),
        [((experts + 8, model), f32), (out_weight.shape, bf16)],
        ids, *token_packs, d_logits, gain_terms, gain1_row, gain2, h1, d_proj, attended, d_att,
        d_scores, buckets, qkv_w,
        smem=1,
        scratch=[pltpu.VMEM((model, tok), f32), padded],
    )
    (input_grad,) = run(
        functools.partial(input_grad_kernel, n_t=n_t),
        [((width, tok), f32)],
        ids, c0, *got, dr1, inv1, x, gain1,
        smem=1,
    )
    out_grad = lax.psum(out_part, "expert").astype(f32)
    if direct:
        (small,) = run(small_sum_kernel, [(small.shape, f32)], *around_experts(small))
        (qkv_grad,) = run(
            qkv_grad_kernel, [((inner, model), f32)], *d_proj_all, *h1_all
        )
    else:
        small = lax.psum(small, "expert")
        (qkv_grad,) = run(qkv_grad_kernel, [((inner, model), f32)], d_proj, h1)
        qkv_grad = lax.psum(qkv_grad.astype(bf16), "expert").astype(f32)
    first = small[experts + 1:experts + 2]
    first = functools.reduce(lambda a, b: a + b, around(first))
    return (
        output.T,
        input_grad.T,
        first.reshape(model),
        small[experts].reshape(model),
        qkv_grad.reshape(3, width, model).transpose(0, 2, 1),
        out_grad,
        small[experts + 2:experts + 2 + n_heads, :n_buckets].T,
        small[:experts].T,
        up_grad,
        down_grad,
    )


def solution(mesh):
    placed = (
        P("expert", "tensor"),
        P(),
        P(),
        P(None, None, "tensor"),
        P("tensor", None),
        P(None, "tensor"),
        P(),
        P("expert", None, "tensor"),
        P("expert", "tensor", None),
        P("expert", None),
        P("expert", None),
        P(),
        P("expert", "tensor"),
    )
    return jax.shard_map(
        functools.partial(per_device, n_t=mesh.shape["tensor"], n_e=mesh.shape["expert"]),
        mesh=mesh,
        in_specs=placed,
        out_specs=(
            P("expert", "tensor"),
            P("expert", "tensor"),
            P(),
            P(),
            P(None, None, "tensor"),
            P("tensor", None),
            P(None, "tensor"),
            P(),
            P("expert", None, "tensor"),
            P("expert", "tensor", None),
        ),
        check_vma=False,
    )
```

```python
import functools
import math

import jax
import jax.numpy as jnp
from jax import lax
from jax.experimental import pallas as pl
from jax.experimental.pallas import tpu as pltpu
from jax.sharding import PartitionSpec as P

epsilon = 1e-06
highest = lax.Precision.HIGHEST
big_negative = -1e30
bf16 = jnp.bfloat16
f32 = jnp.float32
i32 = jnp.int32


def mm(a, b, contract=(1, 0), precision=None):
    return lax.dot_general(
        a,
        b,
        (((contract[0],), (contract[1],)), ((), ())),
        preferred_element_type=f32,
        precision=precision,
    )


def iota(shape, dim):
    return lax.broadcasted_iota(i32, shape, dim)


def split_hi_lo(v):
    hi = v.astype(bf16).astype(f32)
    return hi, v - hi


def row_block(values, rows=16):
    lanes = values[0].shape[1]
    row = iota((rows, lanes), 0)
    block = jnp.zeros((rows, lanes), f32)
    for i, v in enumerate(values):
        block = jnp.where(row == i, v, block)
    return block


def run(body, outs, *args, smem=0, scratch=(), flops=0, limit=32):
    moved = sum(a.size * a.dtype.itemsize for a in args)
    moved += sum(math.prod(s) * jnp.dtype(d).itemsize for s, d in outs)
    return pl.pallas_call(
        body,
        out_shape=[jax.ShapeDtypeStruct(s, d) for s, d in outs],
        in_specs=[pl.BlockSpec(memory_space=pltpu.SMEM)] * smem
        + [pl.BlockSpec()] * (len(args) - smem),
        out_specs=[pl.BlockSpec()] * len(outs),
        scratch_shapes=list(scratch),
        compiler_params=pltpu.CompilerParams(vmem_limit_bytes=limit * 2**20),
        cost_estimate=pl.CostEstimate(flops=flops, bytes_accessed=moved, transcendentals=0),
    )(*args)


def column_of(row, out):
    for c in range(row.shape[1] // 128):
        part = jnp.broadcast_to(row[:, c * 128:(c + 1) * 128], (128, 128))
        part = jnp.where(iota((128, 128), 0) == iota((128, 128), 1), part, 0.0)
        out[c * 128:(c + 1) * 128, :] = jnp.sum(part, axis=1, keepdims=True)


def skew(values, sign):
    n = values.shape[0]
    row = iota(values.shape, 0)
    bit = 1
    while bit < n:
        moved = pltpu.roll(values, bit if sign > 0 else n - bit, 1)
        values = jnp.where((row & bit) != 0, moved, values)
        bit *= 2
    return values


def bucket_hot(buckets, padded, count):
    padded[...] = jnp.full(padded.shape, -1, i32)
    padded[:, 0:buckets.shape[1]] = buckets[...]
    return (padded[...] == iota((count, padded.shape[1]), 0)).astype(f32)


def prepare_kernel(lengths, gain, out_w, table, buckets, gain_col, out_wt, bias, padded):
    tok = bias.shape[1]
    column_of(gain[...], gain_col)
    out_wt[...] = out_w[...].astype(f32).T.astype(bf16)
    key_pos = iota((tok, tok), 0)
    query_pos = iota((tok, tok), 1)
    end0 = lengths[0, 0]
    end1 = end0 + lengths[0, 1]
    seg_k = (key_pos >= end0).astype(i32) + (key_pos >= end1).astype(i32)
    seg_q = (query_pos >= end0).astype(i32) + (query_pos >= end1).astype(i32)
    allowed = (seg_k == seg_q) & (key_pos <= query_pos)
    hot = bucket_hot(buckets, padded, table.shape[1])
    per_head = mm(table[...], hot, precision=highest)
    for h in range(table.shape[0]):
        full = skew(jnp.broadcast_to(per_head[h:h + 1], (tok, tok)), 1)
        bias[h] = jnp.where(allowed, full, big_negative)


def route_kernel(
    ids, routes, router, gain, qkv_w, after, dest, gain_col, rw_own, qkv_wt, chunks,
    *, experts, cap, n_e, direct, n_t,
):
    tok = routes.shape[1]
    width = rw_own.shape[1]
    e = ids[1].astype(f32)
    rt = routes[...]
    x_of = iota((experts, tok), 0)
    m0 = (rt[0:1] == x_of).astype(f32)
    m1 = (rt[1:2] == x_of).astype(f32)
    earlier = (iota((tok, tok), 0) < iota((tok, tok), 1)).astype(f32).astype(bf16)
    counts = mm((m0 + m1).astype(bf16), earlier)
    send, back = [], []
    for i, m in enumerate((m0, m1)):
        slot = jnp.sum(m * counts, axis=0, keepdims=True)
        owner = rt[i:i + 1].astype(f32)
        if direct:
            ahead = owner - e
            behind = e - owner
            send.append(jnp.where(ahead < 0, ahead + n_e, ahead) * cap + slot)
            back.append(jnp.where(behind < 0, behind + n_e, behind) * cap + slot)
        else:
            send.append(owner * cap + slot)
            back.append(owner * cap + slot)
    dest[...] = row_block(send + back, 8)
    column_of(gain[...], gain_col)
    wide = router[...].astype(f32)
    for s in range(n_t):
        chunks[s] = wide[:, s * width:(s + 1) * width]
    rw_own[...] = chunks[ids[0]].astype(bf16)
    qkv_wt[...] = qkv_w[...].astype(f32).T.astype(bf16)


def chunk(ref, s, width):
    return ref.at[pl.ds(pl.multiple_of(s * width, 64), width)]


def attention_kernel(
    ids, x0, x1, x2, x3, gain, qkv_w, out_wt, bias,
    own, p1, p2, p3, h1, inv1, heads, probs, attended,
    xs, parts, *, n_t,
):
    width, tok = x0.shape
    n_heads = bias.shape[0]
    size = width // n_heads
    model = n_t * width
    r = ids[0]
    for k, x in enumerate((x0, x1, x2, x3)):
        chunk(xs, lax.rem(r + n_t - k, n_t), width)[...] = x[...].astype(f32)
    inverse = lax.rsqrt(jnp.sum(xs[...] * xs[...], axis=0, keepdims=True) / model + epsilon)
    inv1[...] = inverse
    h1[...] = (xs[...] * inverse * gain[...]).astype(bf16)
    heads[...] = mm(qkv_w[...], h1[...]).astype(bf16)
    for h in range(n_heads):
        q, k, v = (heads[j * width + h * size:j * width + (h + 1) * size] for j in range(3))
        scores = mm(k, q, (0, 0)) * (size ** -0.5) + bias[h]
        weights = jnp.exp(scores - jnp.max(scores, axis=0, keepdims=True))
        prob = weights / jnp.sum(weights, axis=0, keepdims=True)
        probs[h] = prob
        attended[h * size:(h + 1) * size] = mm(v, prob.astype(bf16)).astype(bf16)
    parts[...] = mm(out_wt[...], attended[...])
    own[...] = chunk(parts, r, width)[...]
    for k, p in ((1, p1), (2, p2), (3, p3)):
        p[...] = chunk(parts, lax.rem(r + k, n_t), width)[...].astype(bf16)


def dispatch_kernel(
    ids, own, p1, p2, p3, x, gain, rw_own, routes, dest, *refs
):
    pieces = refs[:-3]
    token_pack, residual, pack = refs[-3:]
    width, tok = x.shape
    experts = rw_own.shape[0]
    r = ids[0]
    res = x[...].astype(f32) + own[...] + (
        p1[...].astype(f32) + p2[...].astype(f32) + p3[...].astype(f32)
    )
    residual[...] = res
    scaled = (res * chunk(gain, r, width)[...]).astype(bf16)
    square = jnp.sum(res * res, axis=0, keepdims=True)
    logits = mm(rw_own[...], scaled)
    x_of = iota((experts, tok), 0)
    c0 = jnp.sum(jnp.where(routes[0:1, :] == x_of, logits, 0.0), axis=0, keepdims=True)
    c1 = jnp.sum(jnp.where(routes[1:2, :] == x_of, logits, 0.0), axis=0, keepdims=True)
    number = (iota((1, tok), 1) + 1).astype(f32)
    stats = row_block(split_hi_lo(square) + split_hi_lo(c0 - c1) + (number,)).astype(bf16)
    token_pack[0:width] = res.astype(bf16)
    token_pack[width:] = stats
    pack[0:width] = scaled
    pack[width:] = stats
    size = pieces[0].shape[0]
    row = iota((size * len(pieces), tok), 0).astype(f32)
    place0 = (row == dest[0:1, :]).astype(f32)
    place1 = (row == dest[1:2, :]).astype(f32)
    both = mm((place0 + place1).astype(bf16), pack[...], (1, 1))
    signed = mm((place0 - place1).astype(bf16), pack[...], (1, 1))
    lane = iota(both.shape, 1)
    full = jnp.where((lane == width + 2) | (lane == width + 3), signed, both)
    for k, piece in enumerate(pieces):
        piece[...] = full[k * size:(k + 1) * size].astype(bf16)


def gelu_pair(a):
    c = 0.7978845608028654
    t = jnp.tanh(c * (a + 0.044715 * a * a * a))
    value = 0.5 * a * (1.0 + t)
    slope = 0.5 * (1.0 + t) + 0.5 * a * (1.0 - t * t) * c * (1.0 + 3 * 0.044715 * a * a)
    return value, slope


def expert_kernel(
    ids, h0, h1, h2, h3, dy_all, up, down,
    c0, c1, c2, c3, u, z, de, da, dy_here,
    hs, place, de_rows, chunks, *, n_t, n_e, direct,
):
    width = h0.shape[1] - 16
    model, tok = dy_here.shape
    r, e = ids[0], ids[1]
    packs = (h0, h1, h2, h3)
    for k, h in enumerate(packs):
        hs[lax.rem(r + n_t - k, n_t)] = h[:, 0:width].astype(f32)
    dy_here[...] = chunk(dy_all, e, model)[...]
    stats = h0[:, width:].astype(f32)
    for h in packs[1:]:
        stats += h[:, width:].astype(f32)
    inverse = lax.rsqrt((stats[:, 0:1] + stats[:, 1:2]) / model + epsilon)
    gate = 1.0 / (1.0 + jnp.exp(-inverse * (stats[:, 2:3] + stats[:, 3:4])))
    number = h0[:, width + 4:width + 5].astype(f32)
    place[...] = (iota((h0.shape[0], tok), 1).astype(f32) + 1.0 == number).astype(f32)
    cap = h0.shape[0] // n_e
    for k in range(n_e):
        part = slice(k * cap, (k + 1) * cap)
        sender = lax.rem(e + n_e - k, n_e) if direct else k
        got = mm(place[part].astype(bf16), chunk(dy_all, sender, model)[...], (1, 1))
        de_rows[part] = got * gate[part]
    de[...] = de_rows[...].astype(bf16)
    for s in range(n_t):
        cols = slice(s * width, (s + 1) * width)
        u[:, cols] = (hs[s] * inverse).astype(bf16)
    value, slope = gelu_pair(mm(u[...], up[0]))
    z[...] = value.astype(bf16)
    da[...] = (mm(de[...], down[0], (1, 1)) * slope).astype(bf16)
    eo = mm(z[...], down[0]).astype(bf16)
    du = mm(da[...], up[0], (1, 1)).astype(bf16)
    for s in range(n_t):
        cols = slice(s * width, (s + 1) * width)
        chunks[s, :, 0:width] = eo[:, cols]
        chunks[s, :, width:] = du[:, cols]
    for k, c in enumerate((c0, c1, c2, c3)):
        c[...] = chunks[lax.rem(r + k, n_t)]


def expert_grad_kernel(u, z, de, da, up_grad, down_grad):
    up_grad[0] = mm(u[...], da[...], (0, 0))
    down_grad[0] = mm(z[...], de[...], (0, 0))


def join_kernel(*refs):
    pieces, out = refs[:-1], refs[-1]
    out[...] = jnp.concatenate([p[...].astype(f32) for p in pieces], axis=0).astype(bf16)


def expert_sum_kernel(c0, c1, c2, c3, *pieces):
    total = c0[...].astype(f32) + c1[...].astype(f32) + (c2[...].astype(f32) + c3[...].astype(f32))
    count = len(pieces)
    size = total.shape[0] // count
    for k, piece in enumerate(pieces):
        j = (count - k) % count
        piece[...] = total[j * size:(j + 1) * size].astype(bf16)


def total_stats(packs, width):
    total = packs[0][width:width + 16].astype(f32)
    for p in packs[1:]:
        total += p[width:width + 16].astype(f32)
    return total


def gates_of(stats, model):
    inverse = lax.rsqrt((stats[0:1] + stats[1:2]) / model + epsilon)
    delta = inverse * (stats[2:3] + stats[3:4])
    return inverse, 1.0 / (1.0 + jnp.exp(-delta)), 1.0 / (1.0 + jnp.exp(delta))


def combine_kernel(t0, t1, t2, t3, dest, dy, residual, *refs, n_t):
    pieces, (output, pack) = refs[:-2], refs[-2:]
    width, tok = dy.shape
    _, gate0, gate1 = gates_of(total_stats((t0, t1, t2, t3), width), n_t * width)
    back = jnp.concatenate([p[...].astype(f32) for p in pieces], axis=0).astype(bf16)
    row = iota((back.shape[0], tok), 0).astype(f32)
    pick0 = (row == dest[2:3, :]).astype(f32).astype(bf16)
    pick1 = (row == dest[3:4, :]).astype(f32).astype(bf16)
    got0 = mm(back, pick0, (0, 0))
    got1 = mm(back, pick1, (0, 0))
    e0, e1 = got0[0:width], got1[0:width]
    output[...] = (residual[...] + gate0 * e0 + gate1 * e1).astype(bf16)
    dy_own = dy[...].astype(f32)
    dg0 = jnp.sum(dy_own * e0, axis=0, keepdims=True)
    dg1 = jnp.sum(dy_own * e1, axis=0, keepdims=True)
    pack[0:width] = (got0[width:] + got1[width:]).astype(bf16)
    pack[width:] = row_block(split_hi_lo(dg0) + split_hi_lo(dg1)).astype(bf16)


def backward_kernel(
    ids, b0, b1, b2, b3, t0, t1, t2, t3, dy,
    routes, router, gain, out_w, qkv_wt, heads, probs,
    c0, c1, c2, c3, dr1_own, d_proj, d_att, d_logits, gain_terms, d_scores,
    bs, ts, dr, *, n_t,
):
    width = dr1_own.shape[0]
    tok = b0.shape[1]
    experts = router.shape[0]
    n_heads = probs.shape[0]
    size = width // n_heads
    model = n_t * width
    r = ids[0]
    packs, tokens = (b0, b1, b2, b3), (t0, t1, t2, t3)
    for k in range(n_t):
        s = lax.rem(r + n_t - k, n_t)
        chunk(bs, s, width)[...] = packs[k][0:width].astype(f32)
        chunk(ts, s, width)[...] = tokens[k][0:width].astype(f32)
    inverse, gate0, gate1 = gates_of(total_stats(tokens, width), model)
    back = total_stats(packs, width)
    dg0 = back[0:1] + back[1:2]
    dg1 = back[2:3] + back[3:4]
    mean_gate = gate0 * dg0 + gate1 * dg1
    x_of = iota((experts, tok), 0)
    dlog = jnp.where(routes[0:1, :] == x_of, gate0 * (dg0 - mean_gate), 0.0) + jnp.where(
        routes[1:2, :] == x_of, gate1 * (dg1 - mean_gate), 0.0
    )
    d_logits[...] = dlog
    dh2 = bs[...] + mm(router[...].astype(f32), dlog, (0, 0), precision=highest)
    res = ts[...]
    gain_terms[...] = dh2 * res * inverse
    weighted = dh2 * gain[...]
    dot = jnp.sum(weighted * res, axis=0, keepdims=True) * (inverse**3 / model)
    dr[...] = dy[...].astype(f32) + inverse * weighted - res * dot
    d_att[...] = dr[...].astype(bf16)
    dr1_own[...] = chunk(dr, r, width)[...]
    d_o = mm(out_w[...], d_att[...]).astype(bf16)
    scale = size ** -0.5
    for h in range(n_heads):
        q, k, v = (heads[j * width + h * size:j * width + (h + 1) * size] for j in range(3))
        d_oh = d_o[h * size:(h + 1) * size]
        prob = probs[h]
        d_prob = mm(v, d_oh, (0, 0))
        centre = jnp.sum(prob * d_prob, axis=0, keepdims=True)
        ds = (prob * (d_prob - centre)).astype(bf16)
        d_scores[h] = ds
        here = h * size
        d_proj[here:here + size] = (mm(k, ds) * scale).astype(bf16)
        here += width
        d_proj[here:here + size] = (mm(q, ds, (1, 1)) * scale).astype(bf16)
        here += width
        d_proj[here:here + size] = mm(d_oh, prob.astype(bf16), (1, 1)).astype(bf16)
    row_dot = jnp.sum(
        d_proj[...].astype(f32) * heads[...].astype(f32), axis=0, keepdims=True
    )
    stats = row_block(split_hi_lo(row_dot)).astype(bf16)
    dr[...] = mm(qkv_wt[...], d_proj[...])
    for k, c in enumerate((c0, c1, c2, c3)):
        c[0:width] = chunk(dr, lax.rem(r + k, n_t), width)[...].astype(bf16)
        c[width:] = stats


def small_grad_kernel(
    ids, t0, t1, t2, t3, d_logits, gain_terms, gain1_row, gain2, h1, d_proj, attended, d_att,
    d_scores, buckets, qkv_w, small, last, ts, padded, *, n_t, n_buckets, direct,
):
    packs = (t0, t1, t2, t3)
    width = attended.shape[0]
    model = n_t * width
    inner = d_proj.shape[0]
    experts = d_logits.shape[0]
    tok = t0.shape[1]
    r = ids[0]
    for k, t in enumerate(packs):
        chunk(ts, lax.rem(r + n_t - k, n_t), width)[...] = t[0:width].astype(f32)
    inverse, _, _ = gates_of(total_stats(packs, width), model)
    normed = (ts[...] * inverse * gain2[...]).astype(bf16).astype(f32)
    small[0:experts] = mm(d_logits[...], normed, (1, 1), precision=highest)
    ones = jnp.ones((8, tok), f32)
    small[experts:] = jnp.zeros((small.shape[0] - experts, model), f32)
    small[experts:experts + 1] = mm(ones, gain_terms[...], (1, 1), precision=highest)[0:1]
    grad = mm(d_proj[...], h1[...], (1, 1))
    first = jnp.sum(grad * qkv_w[...].astype(f32), axis=0, keepdims=True)
    small[experts + 1:experts + 2] = first / gain1_row[...]
    hot = bucket_hot(buckets, padded, n_buckets)
    for h in range(d_scores.shape[0]):
        diagonal = jnp.sum(skew(d_scores[h].astype(f32), -1), axis=0, keepdims=True)
        per_bucket = mm(jnp.broadcast_to(diagonal, (8, tok)), hot, (1, 1), precision=highest)
        here = experts + 2 + h
        small[here:here + 1, 0:n_buckets] = per_bucket[0:1]
    if direct:
        last[0:inner] = d_proj[...]
        last[inner:inner + width] = chunk(d_att, r, width)[...]
        height = small.shape[0]
        for c in range(model // tok):
            here = inner + width + c * height
            last[here:here + height] = small[:, c * tok:(c + 1) * tok].astype(bf16)
    else:
        last[...] = mm(attended[...], d_att[...], (1, 1)).astype(last.dtype)


def late_sum_kernel(ids, last, att_all, small, own, q1, q2, q3, blocks, *, n_t, n_e, inner):
    model = small.shape[1]
    width = model // n_t
    tok = last.shape[1]
    stride = last.shape[0] // n_e
    height = small.shape[0]
    r = ids[0]
    total = last[inner + width:stride].astype(f32)
    grad = mm(att_all[0:model], last[inner:inner + width], (1, 1))
    for k in range(1, n_e):
        base = k * stride
        total += last[base + inner + width:base + stride].astype(f32)
        grad += mm(
            att_all[k * model:(k + 1) * model], last[base + inner:base + inner + width], (1, 1)
        )
    for c in range(model // tok):
        small[:, c * tok:(c + 1) * tok] = total[c * height:(c + 1) * height]
    for s in range(n_t):
        blocks[s] = grad[s * width:(s + 1) * width]
    own[...] = blocks[r]
    for k, q in ((1, q1), (2, q2), (3, q3)):
        q[...] = blocks[lax.rem(r + k, n_t)].astype(bf16)


def out_grad_kernel(ids, own, q1, q2, q3, f0, f1, f2, f3, out, first, blocks, *, n_t):
    width = own.shape[0]
    r = ids[0]
    blocks[r] = own[...]
    for k, q in ((1, q1), (2, q2), (3, q3)):
        blocks[lax.rem(r + n_t - k, n_t)] = q[...].astype(f32)
    for s in range(n_t):
        out[:, s * width:(s + 1) * width] = blocks[s]
    first[...] = f0[...] + f1[...] + (f2[...] + f3[...])


def input_grad_kernel(ids, c0, c1, c2, c3, dr1, inv1, x, gain, out, *, n_t):
    width = x.shape[0]
    total = c0[...].astype(f32) + c1[...].astype(f32) + (c2[...].astype(f32) + c3[...].astype(f32))
    row_dot = (total[width:width + 1] + total[width + 1:width + 2]) / (n_t * width)
    inverse = inv1[...]
    weighted = total[0:width] * chunk(gain, ids[0], width)[...]
    out[...] = dr1[...] + inverse * weighted - x[...].astype(f32) * (inverse * inverse * row_dot)


def qkv_grad_kernel(last, h1_all, out, *, count):
    inner, model = out.shape
    stride = last.shape[0] // count
    total = mm(last[0:inner], h1_all[0:model], (1, 1))
    for k in range(1, count):
        total += mm(
            last[k * stride:k * stride + inner], h1_all[k * model:(k + 1) * model], (1, 1)
        )
    out[...] = total


def per_device(
    tokens,
    first_gain,
    second_gain,
    qkv_weight,
    out_weight,
    rel_table,
    router_weight,
    up_weight,
    down_weight,
    routes,
    lengths,
    bucket_ids,
    cotangent,
    *,
    n_t,
    n_e,
):
    tok, width = tokens.shape
    model = n_t * width
    inner = 3 * width
    experts = router_weight.shape[1]
    cap = 5 * tok // (2 * experts)
    rows = experts * cap
    n_heads = rel_table.shape[1]
    n_buckets = rel_table.shape[0]
    direct = n_e <= 8 and cap % 8 == 0
    n_pieces = n_e if direct else 1
    padded = pltpu.VMEM((1, tok), i32)

    def shift(v, k, axis="tensor", n=n_t):
        return lax.ppermute(v, axis, [(i, (i + k) % n) for i in range(n)])

    def around(v):
        return [v] + [shift(v, k) for k in range(1, n_t)]

    def gather(v, axes):
        return lax.all_gather(v, axes, axis=0, tiled=True)

    def exchange(pieces):
        if direct:
            return list(pieces[:1]) + [
                shift(p, k, "expert", n_e) for k, p in enumerate(pieces) if k
            ]
        w = pieces[0].shape[-1]
        v = pieces[0].reshape(n_e, rows // n_e, w)
        v = lax.all_to_all(v, "expert", split_axis=0, concat_axis=0, tiled=True)
        return [v.reshape(rows, w)]

    def join(pieces):
        if len(pieces) == 1:
            return pieces[0]
        return run(join_kernel, [((rows, pieces[0].shape[1]), bf16)], *pieces)[0]

    def piece_shapes(w):
        return [((rows // n_pieces, w), bf16)] * n_pieces

    ids = jnp.stack([lax.axis_index("tensor"), lax.axis_index("expert")]).astype(i32)
    x = tokens.T
    dy = cotangent.T
    qkv_w = qkv_weight.transpose(0, 2, 1).reshape(inner, model)
    router = router_weight.T
    table = rel_table.T
    routes_t = routes.T
    gain1_row = first_gain.reshape(1, model)
    gain2_row = second_gain.reshape(1, model)
    buckets = bucket_ids.reshape(1, -1)

    xs = around(x)
    dy_all = gather(dy, ("expert", "tensor"))
    gain1, out_wt, bias = run(
        prepare_kernel,
        [((model, 1), f32), ((model, width), bf16), ((n_heads, tok, tok), f32)],
        lengths, gain1_row, out_weight, table, buckets,
        smem=1, scratch=[padded],
    )
    own, p1, p2, p3, h1, inv1, heads, probs, attended = run(
        functools.partial(attention_kernel, n_t=n_t),
        [((width, tok), f32)]
        + [((width, tok), bf16)] * 3
        + [
            ((model, tok), bf16),
            ((1, tok), f32),
            ((inner, tok), bf16),
            ((n_heads, tok, tok), f32),
            ((width, tok), bf16),
        ],
        ids, *xs, gain1, qkv_w, out_wt, bias,
        smem=1,
        scratch=[pltpu.VMEM((model, tok), f32), pltpu.VMEM((model, tok), f32)],
    )
    got = [shift(p, k) for k, p in ((1, p1), (2, p2), (3, p3))]
    dest, gain2, rw_own, qkv_wt = run(
        functools.partial(
            route_kernel, experts=experts, cap=cap, n_e=n_e, direct=direct, n_t=n_t
        ),
        [
            ((8, tok), f32),
            ((model, 1), f32),
            ((experts, width), bf16),
            ((model, inner), bf16),
        ],
        ids, routes_t, router, gain2_row, qkv_w, inv1,
        smem=1, scratch=[pltpu.VMEM((n_t, experts, width), f32)],
    )
    if direct:
        h1_all = gather(h1, "expert")
        att_all = gather(attended, ("expert", "tensor"))
    *row_pieces, token_pack, residual = run(
        dispatch_kernel,
        piece_shapes(width + 16) + [((width + 16, tok), bf16), ((width, tok), f32)],
        ids, own, *got, x, gain2, rw_own, routes_t, dest,
        smem=1, scratch=[pltpu.VMEM((width + 16, tok), bf16)],
    )
    in_rows = around(join(exchange(row_pieces)))
    token_packs = around(token_pack)

    c0, c1, c2, c3, u, z, de, da, dy_here = run(
        functools.partial(expert_kernel, n_t=n_t, n_e=n_e, direct=direct),
        [((rows, 2 * width), bf16)] * 4
        + [((rows, model), bf16)] * 4
        + [((model, tok), bf16)],
        ids, *in_rows, dy_all, up_weight, down_weight,
        smem=1,
        limit=32 if direct else 48,
        scratch=[
            pltpu.VMEM((n_t, rows, width), f32),
            pltpu.VMEM((rows, tok), f32),
            pltpu.VMEM((rows, model), f32),
            pltpu.VMEM((n_t, rows, 2 * width), bf16),
        ],
    )
    got = [shift(c, k) for k, c in ((1, c1), (2, c2), (3, c3))]
    up_grad, down_grad = run(
        expert_grad_kernel,
        [(up_weight.shape, f32), (down_weight.shape, f32)],
        u, z, de, da,
    )
    back = exchange(run(expert_sum_kernel, piece_shapes(2 * width), c0, *got))
    output, back_pack = run(
        functools.partial(combine_kernel, n_t=n_t),
        [((width, tok), bf16), ((width + 16, tok), bf16)],
        *token_packs, dest, dy, residual, *back,
    )
    back_packs = around(back_pack)

    c0, c1, c2, c3, dr1, d_proj, d_att, d_logits, gain_terms, d_scores = run(
        functools.partial(backward_kernel, n_t=n_t),
        [((width + 16, tok), bf16)] * 4
        + [
            ((width, tok), f32),
            ((inner, tok), bf16),
            ((model, tok), bf16),
            ((experts, tok), f32),
            ((model, tok), f32),
            ((n_heads, tok, tok), bf16),
        ],
        ids, *back_packs, *token_packs, dy_here, routes_t, router, gain2, out_weight, qkv_wt, heads, probs,
        smem=1,
        scratch=[pltpu.VMEM((model, tok), f32)] * 3,
    )
    got = [shift(c, k) for k, c in ((1, c1), (2, c2), (3, c3))]
    height = experts + 8
    if direct:
        last_shape = (inner + width + height * (model // tok), tok)
    else:
        last_shape = out_weight.shape
    small, last = run(
        functools.partial(small_grad_kernel, n_t=n_t, n_buckets=n_buckets, direct=direct),
        [((height, model), f32), (last_shape, bf16)],
        ids, *token_packs, d_logits, gain_terms, gain1_row, gain2, h1, d_proj, attended, d_att,
        d_scores, buckets, qkv_w,
        smem=1,
        scratch=[pltpu.VMEM((model, tok), f32), padded],
    )
    (input_grad,) = run(
        functools.partial(input_grad_kernel, n_t=n_t),
        [((width, tok), f32)],
        ids, c0, *got, dr1, inv1, x, gain1,
        smem=1,
    )
    if direct:
        last = gather(last, "expert")
        small, own, q1, q2, q3 = run(
            functools.partial(late_sum_kernel, n_t=n_t, n_e=n_e, inner=inner),
            [((height, model), f32), ((width, width), f32)] + [((width, width), bf16)] * 3,
            ids, last, att_all,
            smem=1, scratch=[pltpu.VMEM((n_t, width, width), f32)],
        )
        firsts = around(small[experts + 1:experts + 2])
        got = [shift(q, k) for k, q in ((1, q1), (2, q2), (3, q3))]
        (qkv_grad,) = run(
            functools.partial(qkv_grad_kernel, count=n_e), [((inner, model), f32)], last, h1_all
        )
        out_grad, first = run(
            functools.partial(out_grad_kernel, n_t=n_t),
            [(out_weight.shape, f32), ((1, model), f32)],
            ids, own, *got, *firsts,
            smem=1, scratch=[pltpu.VMEM((n_t, width, width), f32)],
        )
    else:
        small, out_grad = lax.psum((small, last.astype(f32)), "expert")
        (qkv_grad,) = run(
            functools.partial(qkv_grad_kernel, count=1), [((inner, model), f32)], d_proj, h1
        )
        qkv_grad = lax.psum(qkv_grad, "expert")
        first = lax.psum(small[experts + 1], "tensor")
    return (
        output.T,
        input_grad.T,
        first.reshape(model),
        small[experts].reshape(model),
        qkv_grad.reshape(3, width, model).transpose(0, 2, 1),
        out_grad,
        small[experts + 2:experts + 2 + n_heads, :n_buckets].T,
        small[:experts].T,
        up_grad,
        down_grad,
    )


def solution(mesh):
    placed = (
        P("expert", "tensor"),
        P(),
        P(),
        P(None, None, "tensor"),
        P("tensor", None),
        P(None, "tensor"),
        P(),
        P("expert", None, "tensor"),
        P("expert", "tensor", None),
        P("expert", None),
        P("expert", None),
        P(),
        P("expert", "tensor"),
    )
    return jax.shard_map(
        functools.partial(per_device, n_t=mesh.shape["tensor"], n_e=mesh.shape["expert"]),
        mesh=mesh,
        in_specs=placed,
        out_specs=(
            P("expert", "tensor"),
            P("expert", "tensor"),
            P(),
            P(),
            P(None, None, "tensor"),
            P("tensor", None),
            P(None, "tensor"),
            P(),
            P("expert", None, "tensor"),
            P("expert", "tensor", None),
        ),
        check_vma=False,
    )
```

```python
import functools
import math

import jax
import jax.numpy as jnp
from jax import lax
from jax.experimental import pallas as pl
from jax.experimental.pallas import tpu as pltpu
from jax.sharding import PartitionSpec as P

epsilon = 1e-06
highest = lax.Precision.HIGHEST
big_negative = -1e30
bf16 = jnp.bfloat16
f32 = jnp.float32
i32 = jnp.int32


def mm(a, b, contract=(1, 0), precision=None):
    return lax.dot_general(
        a,
        b,
        (((contract[0],), (contract[1],)), ((), ())),
        preferred_element_type=f32,
        precision=precision,
    )


def iota(shape, dim):
    return lax.broadcasted_iota(i32, shape, dim)


def split_hi_lo(v):
    hi = v.astype(bf16).astype(f32)
    return hi, v - hi


def row_block(values, rows=16):
    lanes = values[0].shape[1]
    row = iota((rows, lanes), 0)
    block = jnp.zeros((rows, lanes), f32)
    for i, v in enumerate(values):
        block = jnp.where(row == i, v, block)
    return block


def run(body, outs, *args, fetch=(), scratch=(), limit=32):
    n, m, f = len(args), len(outs), len(fetch)
    moved = sum(a.size * a.dtype.itemsize for a in args)
    moved += sum(math.prod(s) * jnp.dtype(d).itemsize for s, d in outs)
    held = [pltpu.VMEM(args[i].shape, args[i].dtype) for i in fetch]
    sems = [pltpu.SemaphoreType.DMA((f,))] if f else []

    def whole(*refs):
        ins, rest = list(refs[:n]), refs[n + m:]
        copies = [
            pltpu.make_async_copy(ins[i], rest[j], rest[f].at[j]) for j, i in enumerate(fetch)
        ]
        for copy in copies:
            copy.start()
        for copy in copies:
            copy.wait()
        for j, i in enumerate(fetch):
            ins[i] = rest[j]
        body(*ins, *refs[n:n + m], *rest[f + len(sems):])

    return pl.pallas_call(
        whole,
        out_shape=[jax.ShapeDtypeStruct(s, d) for s, d in outs],
        in_specs=[
            pl.BlockSpec(memory_space=pltpu.HBM) if i in fetch else pl.BlockSpec()
            for i in range(n)
        ],
        out_specs=[pl.BlockSpec()] * m,
        scratch_shapes=held + sems + list(scratch),
        compiler_params=pltpu.CompilerParams(vmem_limit_bytes=limit * 2**20),
        cost_estimate=pl.CostEstimate(flops=0, bytes_accessed=moved, transcendentals=0),
    )(*args)


def my_place():
    return lax.axis_index("tensor"), lax.axis_index("expert")


def column_of(row, out):
    for c in range(row.shape[1] // 128):
        part = jnp.broadcast_to(row[:, c * 128:(c + 1) * 128], (128, 128))
        part = jnp.where(iota((128, 128), 0) == iota((128, 128), 1), part, 0.0)
        out[c * 128:(c + 1) * 128, :] = jnp.sum(part, axis=1, keepdims=True)


def skew(values, sign):
    n = values.shape[0]
    row = iota(values.shape, 0)
    bit = 1
    while bit < n:
        moved = pltpu.roll(values, bit if sign > 0 else n - bit, 1)
        values = jnp.where((row & bit) != 0, moved, values)
        bit *= 2
    return values


def bucket_hot(buckets, padded, count):
    padded[...] = jnp.full(padded.shape, -1, i32)
    padded[:, 0:buckets.shape[1]] = buckets[...]
    return (padded[...] == iota((count, padded.shape[1]), 0)).astype(f32)


def prepare_kernel(lengths, gain, out_w, table, buckets, gain_col, out_wt, bias, padded):
    tok = bias.shape[1]
    column_of(gain[...], gain_col)
    out_wt[...] = out_w[...].astype(f32).T.astype(bf16)
    key_pos = iota((tok, tok), 0)
    query_pos = iota((tok, tok), 1)
    end0 = lengths[0:1, 0:1]
    end1 = end0 + lengths[0:1, 1:2]
    seg_k = (key_pos >= end0).astype(i32) + (key_pos >= end1).astype(i32)
    seg_q = (query_pos >= end0).astype(i32) + (query_pos >= end1).astype(i32)
    allowed = (seg_k == seg_q) & (key_pos <= query_pos)
    hot = bucket_hot(buckets, padded, table.shape[1])
    per_head = mm(table[...], hot, precision=highest)
    for h in range(table.shape[0]):
        full = skew(jnp.broadcast_to(per_head[h:h + 1], (tok, tok)), 1)
        bias[h] = jnp.where(allowed, full, big_negative)


def route_kernel(
    routes, router, gain, qkv_w, after, dest, gain_col, rw_own, qkv_wt, chunks,
    *, experts, cap, n_e, direct, n_t,
):
    tok = routes.shape[1]
    width = rw_own.shape[1]
    e = my_place()[1].astype(f32)
    rt = routes[...]
    x_of = iota((experts, tok), 0)
    m0 = (rt[0:1] == x_of).astype(f32)
    m1 = (rt[1:2] == x_of).astype(f32)
    earlier = (iota((tok, tok), 0) < iota((tok, tok), 1)).astype(f32).astype(bf16)
    counts = mm((m0 + m1).astype(bf16), earlier)
    send, back = [], []
    for i, m in enumerate((m0, m1)):
        slot = jnp.sum(m * counts, axis=0, keepdims=True)
        owner = rt[i:i + 1].astype(f32)
        if direct:
            ahead = owner - e
            behind = e - owner
            send.append(jnp.where(ahead < 0, ahead + n_e, ahead) * cap + slot)
            back.append(jnp.where(behind < 0, behind + n_e, behind) * cap + slot)
        else:
            send.append(owner * cap + slot)
            back.append(owner * cap + slot)
    dest[...] = row_block(send + back, 8)
    column_of(gain[...], gain_col)
    wide = router[...].astype(f32)
    for s in range(n_t):
        chunks[s] = wide[:, s * width:(s + 1) * width]
    rw_own[...] = chunks[my_place()[0]].astype(bf16)
    qkv_wt[...] = qkv_w[...].astype(f32).T.astype(bf16)


def chunk(ref, s, width):
    return ref.at[pl.ds(pl.multiple_of(s * width, 64), width)]


def attention_kernel(
    x0, x1, x2, x3, gain, qkv_w, out_wt, bias,
    own, p1, p2, p3, h1, inv1, heads, probs, attended,
    xs, parts, *, n_t,
):
    width, tok = x0.shape
    n_heads = bias.shape[0]
    size = width // n_heads
    model = n_t * width
    r, _ = my_place()
    for k, x in enumerate((x0, x1, x2, x3)):
        chunk(xs, lax.rem(r + n_t - k, n_t), width)[...] = x[...].astype(f32)
    inverse = lax.rsqrt(jnp.sum(xs[...] * xs[...], axis=0, keepdims=True) / model + epsilon)
    inv1[...] = inverse
    h1[...] = (xs[...] * inverse * gain[...]).astype(bf16)
    heads[...] = mm(qkv_w[...], h1[...]).astype(bf16)
    for h in range(n_heads):
        q, k, v = (heads[j * width + h * size:j * width + (h + 1) * size] for j in range(3))
        scores = mm(k, q, (0, 0)) * (size ** -0.5) + bias[h]
        weights = jnp.exp(scores - jnp.max(scores, axis=0, keepdims=True))
        prob = weights / jnp.sum(weights, axis=0, keepdims=True)
        probs[h] = prob
        attended[h * size:(h + 1) * size] = mm(v, prob.astype(bf16)).astype(bf16)
    parts[...] = mm(out_wt[...], attended[...])
    own[...] = chunk(parts, r, width)[...]
    for k, p in ((1, p1), (2, p2), (3, p3)):
        p[...] = chunk(parts, lax.rem(r + k, n_t), width)[...].astype(bf16)


def dispatch_kernel(
    own, p1, p2, p3, x, dy, gain, rw_own, routes, dest, *refs
):
    pieces = refs[:-3]
    token_pack, residual, pack = refs[-3:]
    width, tok = x.shape
    experts = rw_own.shape[0]
    r, _ = my_place()
    res = x[...].astype(f32) + own[...] + (
        p1[...].astype(f32) + p2[...].astype(f32) + p3[...].astype(f32)
    )
    residual[...] = res
    scaled = (res * chunk(gain, r, width)[...]).astype(bf16)
    square = jnp.sum(res * res, axis=0, keepdims=True)
    logits = mm(rw_own[...], scaled)
    x_of = iota((experts, tok), 0)
    c0 = jnp.sum(jnp.where(routes[0:1, :] == x_of, logits, 0.0), axis=0, keepdims=True)
    c1 = jnp.sum(jnp.where(routes[1:2, :] == x_of, logits, 0.0), axis=0, keepdims=True)
    stats = row_block(split_hi_lo(square) + split_hi_lo(c0 - c1)).astype(bf16)
    token_pack[0:width] = res.astype(bf16)
    token_pack[width:width + 16] = stats
    token_pack[width + 16:] = dy[...]
    pack[0:width] = scaled
    pack[width:width + 16] = stats
    pack[width + 16:] = dy[...]
    size = pieces[0].shape[0]
    row = iota((size * len(pieces), tok), 0).astype(f32)
    place0 = (row == dest[0:1, :]).astype(f32)
    place1 = (row == dest[1:2, :]).astype(f32)
    both = mm((place0 + place1).astype(bf16), pack[...], (1, 1))
    signed = mm((place0 - place1).astype(bf16), pack[...], (1, 1))
    lane = iota(both.shape, 1)
    full = jnp.where((lane == width + 2) | (lane == width + 3), signed, both)
    for k, piece in enumerate(pieces):
        piece[...] = full[k * size:(k + 1) * size].astype(bf16)


def gelu_pair(a):
    c = 0.7978845608028654
    t = jnp.tanh(c * (a + 0.044715 * a * a * a))
    value = 0.5 * a * (1.0 + t)
    slope = 0.5 * (1.0 + t) + 0.5 * a * (1.0 - t * t) * c * (1.0 + 3 * 0.044715 * a * a)
    return value, slope


def expert_kernel(
    h0, h1, h2, h3, up, down,
    c0, c1, c2, c3, u, z, de, da,
    hs, gs, chunks, *, n_t,
):
    width = c0.shape[1] // 2
    model = n_t * width
    r, _ = my_place()
    packs = (h0, h1, h2, h3)
    for k, h in enumerate(packs):
        s = lax.rem(r + n_t - k, n_t)
        hs[s] = h[:, 0:width].astype(f32)
        gs[s] = h[:, width + 16:].astype(f32)
    stats = h0[:, width:width + 16].astype(f32)
    for h in packs[1:]:
        stats += h[:, width:width + 16].astype(f32)
    inverse = lax.rsqrt((stats[:, 0:1] + stats[:, 1:2]) / model + epsilon)
    gate = 1.0 / (1.0 + jnp.exp(-inverse * (stats[:, 2:3] + stats[:, 3:4])))
    for s in range(n_t):
        cols = slice(s * width, (s + 1) * width)
        u[:, cols] = (hs[s] * inverse).astype(bf16)
        de[:, cols] = (gs[s] * gate).astype(bf16)
    value, slope = gelu_pair(mm(u[...], up[0]))
    z[...] = value.astype(bf16)
    da[...] = (mm(de[...], down[0], (1, 1)) * slope).astype(bf16)
    eo = mm(z[...], down[0]).astype(bf16)
    du = mm(da[...], up[0], (1, 1)).astype(bf16)
    for s in range(n_t):
        cols = slice(s * width, (s + 1) * width)
        chunks[s, :, 0:width] = eo[:, cols]
        chunks[s, :, width:] = du[:, cols]
    for k, c in enumerate((c0, c1, c2, c3)):
        c[...] = chunks[lax.rem(r + k, n_t)]


def expert_grad_kernel(u, z, de, da, up_grad, down_grad):
    up_grad[0] = mm(u[...], da[...], (0, 0))
    down_grad[0] = mm(z[...], de[...], (0, 0))


def join_kernel(*refs):
    pieces, out = refs[:-1], refs[-1]
    out[...] = jnp.concatenate([p[...].astype(f32) for p in pieces], axis=0).astype(bf16)


def expert_sum_kernel(c0, c1, c2, c3, *pieces):
    total = c0[...].astype(f32) + c1[...].astype(f32) + (c2[...].astype(f32) + c3[...].astype(f32))
    count = len(pieces)
    size = total.shape[0] // count
    for k, piece in enumerate(pieces):
        j = (count - k) % count
        piece[...] = total[j * size:(j + 1) * size].astype(bf16)


def total_stats(packs, width):
    total = packs[0][width:width + 16].astype(f32)
    for p in packs[1:]:
        total += p[width:width + 16].astype(f32)
    return total


def gates_of(stats, model):
    inverse = lax.rsqrt((stats[0:1] + stats[1:2]) / model + epsilon)
    delta = inverse * (stats[2:3] + stats[3:4])
    return inverse, 1.0 / (1.0 + jnp.exp(-delta)), 1.0 / (1.0 + jnp.exp(delta))


def combine_kernel(t0, t1, t2, t3, dest, dy, residual, *refs, n_t):
    pieces, (output, pack) = refs[:-2], refs[-2:]
    width, tok = dy.shape
    _, gate0, gate1 = gates_of(total_stats((t0, t1, t2, t3), width), n_t * width)
    back = jnp.concatenate([p[...].astype(f32) for p in pieces], axis=0).astype(bf16)
    row = iota((back.shape[0], tok), 0).astype(f32)
    pick0 = (row == dest[2:3, :]).astype(f32).astype(bf16)
    pick1 = (row == dest[3:4, :]).astype(f32).astype(bf16)
    got0 = mm(back, pick0, (0, 0))
    got1 = mm(back, pick1, (0, 0))
    e0, e1 = got0[0:width], got1[0:width]
    output[...] = (residual[...] + gate0 * e0 + gate1 * e1).astype(bf16)
    dy_own = dy[...].astype(f32)
    dg0 = jnp.sum(dy_own * e0, axis=0, keepdims=True)
    dg1 = jnp.sum(dy_own * e1, axis=0, keepdims=True)
    pack[0:width] = (got0[width:] + got1[width:]).astype(bf16)
    pack[width:] = row_block(split_hi_lo(dg0) + split_hi_lo(dg1)).astype(bf16)


def backward_kernel(
    b0, b1, b2, b3, t0, t1, t2, t3,
    routes, router, gain, out_w, qkv_wt, heads, probs,
    c0, c1, c2, c3, dr1_own, d_proj, d_att, d_logits, gain_terms, d_scores,
    bs, ts, ys, dr, *, n_t,
):
    width = dr1_own.shape[0]
    tok = b0.shape[1]
    experts = router.shape[0]
    n_heads = probs.shape[0]
    size = width // n_heads
    model = n_t * width
    r, _ = my_place()
    packs, tokens = (b0, b1, b2, b3), (t0, t1, t2, t3)
    for k in range(n_t):
        s = lax.rem(r + n_t - k, n_t)
        chunk(bs, s, width)[...] = packs[k][0:width].astype(f32)
        chunk(ts, s, width)[...] = tokens[k][0:width].astype(f32)
        chunk(ys, s, width)[...] = tokens[k][width + 16:].astype(f32)
    inverse, gate0, gate1 = gates_of(total_stats(tokens, width), model)
    back = total_stats(packs, width)
    dg0 = back[0:1] + back[1:2]
    dg1 = back[2:3] + back[3:4]
    mean_gate = gate0 * dg0 + gate1 * dg1
    x_of = iota((experts, tok), 0)
    dlog = jnp.where(routes[0:1, :] == x_of, gate0 * (dg0 - mean_gate), 0.0) + jnp.where(
        routes[1:2, :] == x_of, gate1 * (dg1 - mean_gate), 0.0
    )
    d_logits[...] = dlog
    dh2 = bs[...] + mm(router[...].astype(f32), dlog, (0, 0), precision=highest)
    res = ts[...]
    gain_terms[...] = dh2 * res * inverse
    weighted = dh2 * gain[...]
    dot = jnp.sum(weighted * res, axis=0, keepdims=True) * (inverse**3 / model)
    dr[...] = ys[...] + inverse * weighted - res * dot
    d_att[...] = dr[...].astype(bf16)
    dr1_own[...] = chunk(dr, r, width)[...]
    d_o = mm(out_w[...], d_att[...]).astype(bf16)
    scale = size ** -0.5
    for h in range(n_heads):
        q, k, v = (heads[j * width + h * size:j * width + (h + 1) * size] for j in range(3))
        d_oh = d_o[h * size:(h + 1) * size]
        prob = probs[h]
        d_prob = mm(v, d_oh, (0, 0))
        centre = jnp.sum(prob * d_prob, axis=0, keepdims=True)
        ds = (prob * (d_prob - centre)).astype(bf16)
        d_scores[h] = ds
        here = h * size
        d_proj[here:here + size] = (mm(k, ds) * scale).astype(bf16)
        here += width
        d_proj[here:here + size] = (mm(q, ds, (1, 1)) * scale).astype(bf16)
        here += width
        d_proj[here:here + size] = mm(d_oh, prob.astype(bf16), (1, 1)).astype(bf16)
    row_dot = jnp.sum(
        d_proj[...].astype(f32) * heads[...].astype(f32), axis=0, keepdims=True
    )
    stats = row_block(split_hi_lo(row_dot)).astype(bf16)
    dr[...] = mm(qkv_wt[...], d_proj[...])
    for k, c in enumerate((c0, c1, c2, c3)):
        c[0:width] = chunk(dr, lax.rem(r + k, n_t), width)[...].astype(bf16)
        c[width:] = stats


def small_grad_kernel(
    t0, t1, t2, t3, d_logits, gain_terms, gain1_row, gain2, h1, d_proj, attended, d_att,
    d_scores, buckets, qkv_w, small, last, ts, padded, *, n_t, n_buckets, direct,
):
    packs = (t0, t1, t2, t3)
    width = attended.shape[0]
    model = n_t * width
    inner = d_proj.shape[0]
    experts = d_logits.shape[0]
    tok = t0.shape[1]
    r, _ = my_place()
    for k, t in enumerate(packs):
        chunk(ts, lax.rem(r + n_t - k, n_t), width)[...] = t[0:width].astype(f32)
    inverse, _, _ = gates_of(total_stats(packs, width), model)
    normed = (ts[...] * inverse * gain2[...]).astype(bf16).astype(f32)
    small[0:experts] = mm(d_logits[...], normed, (1, 1), precision=highest)
    ones = jnp.ones((8, tok), f32)
    small[experts:] = jnp.zeros((small.shape[0] - experts, model), f32)
    small[experts:experts + 1] = mm(ones, gain_terms[...], (1, 1), precision=highest)[0:1]
    grad = mm(d_proj[...], h1[...], (1, 1))
    first = jnp.sum(grad * qkv_w[...].astype(f32), axis=0, keepdims=True)
    small[experts + 1:experts + 2] = first / gain1_row[...]
    hot = bucket_hot(buckets, padded, n_buckets)
    for h in range(d_scores.shape[0]):
        diagonal = jnp.sum(skew(d_scores[h].astype(f32), -1), axis=0, keepdims=True)
        per_bucket = mm(jnp.broadcast_to(diagonal, (8, tok)), hot, (1, 1), precision=highest)
        here = experts + 2 + h
        small[here:here + 1, 0:n_buckets] = per_bucket[0:1]
    if direct:
        last[0:inner] = d_proj[...]
        last[inner:inner + width] = chunk(d_att, r, width)[...]
        height = small.shape[0]
        for c in range(model // tok):
            here = inner + width + c * height
            last[here:here + height] = small[:, c * tok:(c + 1) * tok].astype(bf16)
    else:
        last[...] = mm(attended[...], d_att[...], (1, 1)).astype(last.dtype)


def senders(n_e):
    _, e = my_place()
    other = e + 1 - 2 * lax.rem(e, 2)
    half = n_e // 2
    return [lax.rem((e, other)[j // half] + n_e - 2 * (j % half), n_e) for j in range(n_e)]


def late_sum_kernel(att_all, *refs, n_t, n_e, inner):
    lasts, (small, own, q1, q2, q3, blocks) = refs[:n_e], refs[n_e:]
    model = small.shape[1]
    width = model // n_t
    stride, tok = lasts[0].shape
    height = small.shape[0]
    r, _ = my_place()
    total, grad = 0.0, 0.0
    for last, sender in zip(lasts, senders(n_e)):
        total += last[inner + width:].astype(f32)
        grad += mm(chunk(att_all, sender, model)[...], last[inner:inner + width], (1, 1))
    for c in range(model // tok):
        small[:, c * tok:(c + 1) * tok] = total[c * height:(c + 1) * height]
    for s in range(n_t):
        blocks[s] = grad[s * width:(s + 1) * width]
    own[...] = blocks[r]
    for k, q in ((1, q1), (2, q2), (3, q3)):
        q[...] = blocks[lax.rem(r + k, n_t)].astype(bf16)


def out_grad_kernel(own, q1, q2, q3, f0, f1, f2, f3, out, first, blocks, *, n_t):
    width = own.shape[0]
    r, _ = my_place()
    blocks[r] = own[...]
    for k, q in ((1, q1), (2, q2), (3, q3)):
        blocks[lax.rem(r + n_t - k, n_t)] = q[...].astype(f32)
    for s in range(n_t):
        out[:, s * width:(s + 1) * width] = blocks[s]
    first[...] = f0[...] + f1[...] + (f2[...] + f3[...])


def input_grad_kernel(c0, c1, c2, c3, dr1, inv1, x, gain, out, *, n_t):
    width = x.shape[0]
    total = c0[...].astype(f32) + c1[...].astype(f32) + (c2[...].astype(f32) + c3[...].astype(f32))
    row_dot = (total[width:width + 1] + total[width + 1:width + 2]) / (n_t * width)
    inverse = inv1[...]
    weighted = total[0:width] * chunk(gain, my_place()[0], width)[...]
    out[...] = dr1[...] + inverse * weighted - x[...].astype(f32) * (inverse * inverse * row_dot)


def qkv_grad_kernel(h1_all, *refs):
    lasts, out = refs[:-1], refs[-1]
    inner, model = out.shape
    if len(lasts) == 1:
        out[...] = mm(lasts[0][0:inner], h1_all[...], (1, 1))
        return
    total = 0.0
    for last, sender in zip(lasts, senders(len(lasts))):
        total += mm(last[0:inner], chunk(h1_all, sender, model)[...], (1, 1))
    out[...] = total


def per_device(
    tokens,
    first_gain,
    second_gain,
    qkv_weight,
    out_weight,
    rel_table,
    router_weight,
    up_weight,
    down_weight,
    routes,
    lengths,
    bucket_ids,
    cotangent,
    *,
    n_t,
    n_e,
):
    tok, width = tokens.shape
    model = n_t * width
    inner = 3 * width
    experts = router_weight.shape[1]
    cap = 5 * tok // (2 * experts)
    rows = experts * cap
    n_heads = rel_table.shape[1]
    n_buckets = rel_table.shape[0]
    direct = n_e == 8 and cap % 8 == 0
    n_pieces = n_e if direct else 1
    padded = pltpu.VMEM((1, tok), i32)

    def shift(v, k, axis="tensor", n=n_t):
        return lax.ppermute(v, axis, [(i, (i + k) % n) for i in range(n)])

    def around(v):
        return [v] + [shift(v, k) for k in range(1, n_t)]

    def gather(v, axes):
        return lax.all_gather(v, axes, axis=0, tiled=True)

    def exchange(pieces):
        if direct:
            return list(pieces[:1]) + [
                shift(p, k, "expert", n_e) for k, p in enumerate(pieces) if k
            ]
        w = pieces[0].shape[-1]
        v = pieces[0].reshape(n_e, rows // n_e, w)
        v = lax.all_to_all(v, "expert", split_axis=0, concat_axis=0, tiled=True)
        return [v.reshape(rows, w)]

    def join(pieces):
        if len(pieces) == 1:
            return pieces[0]
        return run(join_kernel, [((rows, pieces[0].shape[1]), bf16)], *pieces)[0]

    def piece_shapes(w):
        return [((rows // n_pieces, w), bf16)] * n_pieces

    x = tokens.T
    dy = cotangent.T
    qkv_w = qkv_weight.transpose(0, 2, 1).reshape(inner, model)
    router = router_weight.T
    table = rel_table.T
    routes_t = routes.T
    gain1_row = first_gain.reshape(1, model)
    gain2_row = second_gain.reshape(1, model)
    buckets = bucket_ids.reshape(1, -1)

    xs = around(x)
    gain1, out_wt, bias = run(
        prepare_kernel,
        [((model, 1), f32), ((model, width), bf16), ((n_heads, tok, tok), f32)],
        lengths, gain1_row, out_weight, table, buckets,
        fetch=(0, 1, 2, 3, 4),
        scratch=[padded],
    )
    own, p1, p2, p3, h1, inv1, heads, probs, attended = run(
        functools.partial(attention_kernel, n_t=n_t),
        [((width, tok), f32)]
        + [((width, tok), bf16)] * 3
        + [
            ((model, tok), bf16),
            ((1, tok), f32),
            ((inner, tok), bf16),
            ((n_heads, tok, tok), f32),
            ((width, tok), bf16),
        ],
        *xs, gain1, qkv_w, out_wt, bias,
        fetch=(n_t + 1,),
        scratch=[pltpu.VMEM((model, tok), f32), pltpu.VMEM((model, tok), f32)],
    )
    got = [shift(p, k) for k, p in ((1, p1), (2, p2), (3, p3))]
    dest, gain2, rw_own, qkv_wt = run(
        functools.partial(
            route_kernel, experts=experts, cap=cap, n_e=n_e, direct=direct, n_t=n_t
        ),
        [
            ((8, tok), f32),
            ((model, 1), f32),
            ((experts, width), bf16),
            ((model, inner), bf16),
        ],
        routes_t, router, gain2_row, qkv_w, inv1,
        fetch=(0, 1, 2, 3),
        scratch=[pltpu.VMEM((n_t, experts, width), f32)],
    )
    if direct:
        h1_all = gather(h1, "expert")
        att_all = gather(attended, ("expert", "tensor"))
    *row_pieces, token_pack, residual = run(
        dispatch_kernel,
        piece_shapes(2 * width + 16) + [((2 * width + 16, tok), bf16), ((width, tok), f32)],
        own, *got, x, dy, gain2, rw_own, routes_t, dest,
        fetch=(4, 5, 8),
        scratch=[pltpu.VMEM((2 * width + 16, tok), bf16)],
    )
    in_rows = around(join(exchange(row_pieces)))
    token_packs = around(token_pack)

    c0, c1, c2, c3, u, z, de, da = run(
        functools.partial(expert_kernel, n_t=n_t),
        [((rows, 2 * width), bf16)] * 4 + [((rows, model), bf16)] * 4,
        *in_rows, up_weight, down_weight,
        fetch=(4, 5),
        scratch=[
            pltpu.VMEM((n_t, rows, width), f32),
            pltpu.VMEM((n_t, rows, width), f32),
            pltpu.VMEM((n_t, rows, 2 * width), bf16),
        ],
    )
    got = [shift(c, k) for k, c in ((1, c1), (2, c2), (3, c3))]
    up_grad, down_grad = run(
        expert_grad_kernel,
        [(up_weight.shape, f32), (down_weight.shape, f32)],
        u, z, de, da,
    )
    back = exchange(run(expert_sum_kernel, piece_shapes(2 * width), c0, *got))
    output, back_pack = run(
        functools.partial(combine_kernel, n_t=n_t),
        [((width, tok), bf16), ((width + 16, tok), bf16)],
        *token_packs, dest, dy, residual, *back,
        fetch=(5,),
    )
    back_packs = around(back_pack)

    c0, c1, c2, c3, dr1, d_proj, d_att, d_logits, gain_terms, d_scores = run(
        functools.partial(backward_kernel, n_t=n_t),
        [((width + 16, tok), bf16)] * 4
        + [
            ((width, tok), f32),
            ((inner, tok), bf16),
            ((model, tok), bf16),
            ((experts, tok), f32),
            ((model, tok), f32),
            ((n_heads, tok, tok), bf16),
        ],
        *back_packs, *token_packs, routes_t, router, gain2, out_weight, qkv_wt, heads, probs,
        fetch=(8, 9, 11),
        scratch=[pltpu.VMEM((model, tok), f32)] * 4,
    )
    got = [shift(c, k) for k, c in ((1, c1), (2, c2), (3, c3))]
    height = experts + 8
    if direct:
        last_shape = (inner + width + height * (model // tok), tok)
    else:
        last_shape = out_weight.shape
    small, last = run(
        functools.partial(small_grad_kernel, n_t=n_t, n_buckets=n_buckets, direct=direct),
        [((height, model), f32), (last_shape, bf16)],
        *token_packs, d_logits, gain_terms, gain1_row, gain2, h1, d_proj, attended, d_att,
        d_scores, buckets, qkv_w,
        fetch=(6, 13, 14),
        scratch=[pltpu.VMEM((model, tok), f32), padded],
    )
    (input_grad,) = run(
        functools.partial(input_grad_kernel, n_t=n_t),
        [((width, tok), f32)],
        c0, *got, dr1, inv1, x, gain1,
        fetch=(6,),
    )
    if direct:
        lasts = [last] + [shift(last, 2 * k, "expert", n_e) for k in range(1, n_e // 2)]
        lasts = lasts + [
            lax.ppermute(v, "expert", [(i, i ^ 1) for i in range(n_e)]) for v in lasts
        ]
        small, own, q1, q2, q3 = run(
            functools.partial(late_sum_kernel, n_t=n_t, n_e=n_e, inner=inner),
            [((height, model), f32), ((width, width), f32)] + [((width, width), bf16)] * 3,
            att_all, *lasts,
            scratch=[pltpu.VMEM((n_t, width, width), f32)],
        )
        firsts = around(small[experts + 1:experts + 2])
        got = [shift(q, k) for k, q in ((1, q1), (2, q2), (3, q3))]
        (qkv_grad,) = run(qkv_grad_kernel, [((inner, model), f32)], h1_all, *lasts)
        out_grad, first = run(
            functools.partial(out_grad_kernel, n_t=n_t),
            [(out_weight.shape, f32), ((1, model), f32)],
            own, *got, *firsts,
            scratch=[pltpu.VMEM((n_t, width, width), f32)],
        )
    else:
        small, out_grad = lax.psum((small, last.astype(f32)), "expert")
        (qkv_grad,) = run(qkv_grad_kernel, [((inner, model), f32)], h1, d_proj)
        qkv_grad = lax.psum(qkv_grad, "expert")
        first = lax.psum(small[experts + 1], "tensor")
    return (
        output.T,
        input_grad.T,
        first.reshape(model),
        small[experts].reshape(model),
        qkv_grad.reshape(3, width, model).transpose(0, 2, 1),
        out_grad,
        small[experts + 2:experts + 2 + n_heads, :n_buckets].T,
        small[:experts].T,
        up_grad,
        down_grad,
    )


def solution(mesh):
    placed = (
        P("expert", "tensor"),
        P(),
        P(),
        P(None, None, "tensor"),
        P("tensor", None),
        P(None, "tensor"),
        P(),
        P("expert", None, "tensor"),
        P("expert", "tensor", None),
        P("expert", None),
        P("expert", None),
        P(),
        P("expert", "tensor"),
    )
    return jax.shard_map(
        functools.partial(per_device, n_t=mesh.shape["tensor"], n_e=mesh.shape["expert"]),
        mesh=mesh,
        in_specs=placed,
        out_specs=(
            P("expert", "tensor"),
            P("expert", "tensor"),
            P(),
            P(),
            P(None, None, "tensor"),
            P("tensor", None),
            P(None, "tensor"),
            P(),
            P("expert", None, "tensor"),
            P("expert", "tensor", None),
        ),
        check_vma=False,
    )
```

```python
import functools
import math

import jax
import jax.numpy as jnp
from jax import lax
from jax.experimental import pallas as pl
from jax.experimental.pallas import tpu as pltpu
from jax.sharding import PartitionSpec as P

epsilon = 1e-06
highest = lax.Precision.HIGHEST
big_negative = -1e30
bf16 = jnp.bfloat16
f32 = jnp.float32
i32 = jnp.int32


def mm(a, b, contract=(1, 0), precision=None):
    return lax.dot_general(
        a,
        b,
        (((contract[0],), (contract[1],)), ((), ())),
        preferred_element_type=f32,
        precision=precision,
    )


def iota(shape, dim):
    return lax.broadcasted_iota(i32, shape, dim)


def split_hi_lo(v):
    hi = v.astype(bf16).astype(f32)
    return hi, v - hi


def row_block(values, rows=16):
    lanes = values[0].shape[1]
    row = iota((rows, lanes), 0)
    block = jnp.zeros((rows, lanes), f32)
    for i, v in enumerate(values):
        block = jnp.where(row == i, v, block)
    return block


def run(body, outs, *args, fetch=(), scratch=(), limit=32):
    n, m, f = len(args), len(outs), len(fetch)
    moved = sum(a.size * a.dtype.itemsize for a in args)
    moved += sum(math.prod(s) * jnp.dtype(d).itemsize for s, d in outs)
    held = [pltpu.VMEM(args[i].shape, args[i].dtype) for i in fetch]
    sems = [pltpu.SemaphoreType.DMA((f,))] if f else []

    def whole(*refs):
        ins, rest = list(refs[:n]), refs[n + m:]
        copies = [
            pltpu.make_async_copy(ins[i], rest[j], rest[f].at[j]) for j, i in enumerate(fetch)
        ]
        for copy in copies:
            copy.start()
        for copy in copies:
            copy.wait()
        for j, i in enumerate(fetch):
            ins[i] = rest[j]
        body(*ins, *refs[n:n + m], *rest[f + len(sems):])

    return pl.pallas_call(
        whole,
        out_shape=[jax.ShapeDtypeStruct(s, d) for s, d in outs],
        in_specs=[
            pl.BlockSpec(memory_space=pltpu.HBM) if i in fetch else pl.BlockSpec()
            for i in range(n)
        ],
        out_specs=[pl.BlockSpec()] * m,
        scratch_shapes=held + sems + list(scratch),
        compiler_params=pltpu.CompilerParams(vmem_limit_bytes=limit * 2**20),
        cost_estimate=pl.CostEstimate(flops=0, bytes_accessed=moved, transcendentals=0),
    )(*args)


def my_place():
    return lax.axis_index("tensor"), lax.axis_index("expert")


def column_of(row, out):
    for c in range(row.shape[1] // 128):
        part = jnp.broadcast_to(row[:, c * 128:(c + 1) * 128], (128, 128))
        part = jnp.where(iota((128, 128), 0) == iota((128, 128), 1), part, 0.0)
        out[c * 128:(c + 1) * 128, :] = jnp.sum(part, axis=1, keepdims=True)


def skew(values, sign):
    n = values.shape[0]
    row = iota(values.shape, 0)
    bit = 1
    while bit < n:
        moved = pltpu.roll(values, bit if sign > 0 else n - bit, 1)
        values = jnp.where((row & bit) != 0, moved, values)
        bit *= 2
    return values


def bucket_hot(buckets, padded, count):
    padded[...] = jnp.full(padded.shape, -1, i32)
    padded[:, 0:buckets.shape[1]] = buckets[...]
    return (padded[...] == iota((count, padded.shape[1]), 0)).astype(f32)


def prepare_kernel(lengths, gain, out_w, table, buckets, gain_col, out_wt, bias, padded):
    tok = bias.shape[1]
    column_of(gain[...], gain_col)
    out_wt[...] = out_w[...].astype(f32).T.astype(bf16)
    key_pos = iota((tok, tok), 0)
    query_pos = iota((tok, tok), 1)
    end0 = lengths[0:1, 0:1]
    end1 = end0 + lengths[0:1, 1:2]
    seg_k = (key_pos >= end0).astype(i32) + (key_pos >= end1).astype(i32)
    seg_q = (query_pos >= end0).astype(i32) + (query_pos >= end1).astype(i32)
    allowed = (seg_k == seg_q) & (key_pos <= query_pos)
    hot = bucket_hot(buckets, padded, table.shape[1])
    per_head = mm(table[...], hot, precision=highest)
    for h in range(table.shape[0]):
        full = skew(jnp.broadcast_to(per_head[h:h + 1], (tok, tok)), 1)
        bias[h] = jnp.where(allowed, full, big_negative)


def route_kernel(
    routes, router, gain, qkv_w, after, dest, gain_col, rw_own, qkv_wt, chunks,
    *, experts, cap, n_t,
):
    tok = routes.shape[1]
    width = rw_own.shape[1]
    rt = routes[...]
    x_of = iota((experts, tok), 0)
    m0 = (rt[0:1] == x_of).astype(f32)
    m1 = (rt[1:2] == x_of).astype(f32)
    earlier = (iota((tok, tok), 0) < iota((tok, tok), 1)).astype(f32).astype(bf16)
    counts = mm((m0 + m1).astype(bf16), earlier)
    rows = [
        rt[i:i + 1].astype(f32) * cap + jnp.sum(m * counts, axis=0, keepdims=True)
        for i, m in enumerate((m0, m1))
    ]
    dest[...] = row_block(rows, 8)
    column_of(gain[...], gain_col)
    wide = router[...].astype(f32)
    for s in range(n_t):
        chunks[s] = wide[:, s * width:(s + 1) * width]
    rw_own[...] = chunks[my_place()[0]].astype(bf16)
    qkv_wt[...] = qkv_w[...].astype(f32).T.astype(bf16)


def chunk(ref, s, width):
    return ref.at[pl.ds(pl.multiple_of(s * width, 64), width)]


def attention_kernel(
    x0, x1, x2, x3, gain, qkv_w, out_wt, bias,
    own, p1, p2, p3, inv1, heads, probs, saved,
    xs, parts, *, n_t,
):
    width, tok = x0.shape
    n_heads = bias.shape[0]
    size = width // n_heads
    model = n_t * width
    r, _ = my_place()
    for k, x in enumerate((x0, x1, x2, x3)):
        chunk(xs, r ^ k, width)[...] = x[...].astype(f32)
    inverse = lax.rsqrt(jnp.sum(xs[...] * xs[...], axis=0, keepdims=True) / model + epsilon)
    inv1[...] = inverse
    saved[0:model] = (xs[...] * inverse * gain[...]).astype(bf16)
    heads[...] = mm(qkv_w[...], saved[0:model]).astype(bf16)
    for h in range(n_heads):
        q, k, v = (heads[j * width + h * size:j * width + (h + 1) * size] for j in range(3))
        scores = mm(k, q, (0, 0)) * (size ** -0.5) + bias[h]
        weights = jnp.exp(scores - jnp.max(scores, axis=0, keepdims=True))
        prob = weights / jnp.sum(weights, axis=0, keepdims=True)
        probs[h] = prob
        here = model + h * size
        saved[here:here + size] = mm(v, prob.astype(bf16)).astype(bf16)
    parts[...] = mm(out_wt[...], saved[model:])
    own[...] = chunk(parts, r, width)[...]
    for k, p in ((1, p1), (2, p2), (3, p3)):
        p[...] = chunk(parts, r ^ k, width)[...].astype(bf16)


def dispatch_kernel(
    own, p1, p2, p3, x, dy, gain, rw_own, routes, dest, *refs
):
    pieces = refs[:-3]
    token_pack, residual, pack = refs[-3:]
    width, tok = x.shape
    experts = rw_own.shape[0]
    r, _ = my_place()
    res = x[...].astype(f32) + own[...] + (
        p1[...].astype(f32) + p2[...].astype(f32) + p3[...].astype(f32)
    )
    residual[...] = res
    scaled = (res * chunk(gain, r, width)[...]).astype(bf16)
    square = jnp.sum(res * res, axis=0, keepdims=True)
    logits = mm(rw_own[...], scaled)
    x_of = iota((experts, tok), 0)
    c0 = jnp.sum(jnp.where(routes[0:1, :] == x_of, logits, 0.0), axis=0, keepdims=True)
    c1 = jnp.sum(jnp.where(routes[1:2, :] == x_of, logits, 0.0), axis=0, keepdims=True)
    stats = row_block(split_hi_lo(square) + split_hi_lo(c0 - c1)).astype(bf16)
    token_pack[0:width] = res.astype(bf16)
    token_pack[width:width + 16] = stats
    token_pack[width + 16:] = dy[...]
    pack[0:width] = scaled
    pack[width:width + 16] = stats
    pack[width + 16:] = dy[...]
    size = pieces[0].shape[0]
    row = iota((size * len(pieces), tok), 0).astype(f32)
    place0 = (row == dest[0:1, :]).astype(f32)
    place1 = (row == dest[1:2, :]).astype(f32)
    both = mm((place0 + place1).astype(bf16), pack[...], (1, 1))
    signed = mm((place0 - place1).astype(bf16), pack[...], (1, 1))
    lane = iota(both.shape, 1)
    full = jnp.where((lane == width + 2) | (lane == width + 3), signed, both)
    for k, piece in enumerate(pieces):
        piece[...] = full[k * size:(k + 1) * size].astype(bf16)


def gelu_pair(a):
    c = 0.7978845608028654
    t = jnp.tanh(c * (a + 0.044715 * a * a * a))
    value = 0.5 * a * (1.0 + t)
    slope = 0.5 * (1.0 + t) + 0.5 * a * (1.0 - t * t) * c * (1.0 + 3 * 0.044715 * a * a)
    return value, slope


def expert_kernel(
    h0, h1, h2, h3, up, down,
    own, across, mate, u, z, de, da,
    hs, gs, chunks, *, n_t,
):
    width = own.shape[1] // 2
    model = n_t * width
    r, _ = my_place()
    packs = (h0, h1, h2, h3)
    for k, h in enumerate(packs):
        s = r ^ k
        hs[s] = h[:, 0:width].astype(f32)
        gs[s] = h[:, width + 16:].astype(f32)
    stats = h0[:, width:width + 16].astype(f32)
    for h in packs[1:]:
        stats += h[:, width:width + 16].astype(f32)
    inverse = lax.rsqrt((stats[:, 0:1] + stats[:, 1:2]) / model + epsilon)
    gate = 1.0 / (1.0 + jnp.exp(-inverse * (stats[:, 2:3] + stats[:, 3:4])))
    for s in range(n_t):
        cols = slice(s * width, (s + 1) * width)
        u[:, cols] = (hs[s] * inverse).astype(bf16)
        de[:, cols] = (gs[s] * gate).astype(bf16)
    value, slope = gelu_pair(mm(u[...], up[0]))
    z[...] = value.astype(bf16)
    da[...] = (mm(de[...], down[0], (1, 1)) * slope).astype(bf16)
    eo = mm(z[...], down[0]).astype(bf16)
    du = mm(da[...], up[0], (1, 1)).astype(bf16)
    for s in range(n_t):
        cols = slice(s * width, (s + 1) * width)
        chunks[s, :, 0:width] = eo[:, cols]
        chunks[s, :, width:] = du[:, cols]
    rows = own.shape[0]
    own[...] = chunks[r]
    across[...] = chunks[r ^ 2]
    mate[0:rows] = chunks[r ^ 1]
    mate[rows:] = chunks[r ^ 3]


def expert_grad_kernel(u, z, de, da, up_grad, down_grad):
    up_grad[0] = mm(u[...], da[...], (0, 0))
    down_grad[0] = mm(z[...], de[...], (0, 0))


def join_kernel(gathered, out, *, n_e):
    stride, height = gathered.shape[0] // n_e, out.shape[0] // n_e
    for j in range(n_e):
        out[j * height:(j + 1) * height] = gathered[(j + 1) * stride - height:(j + 1) * stride]


def pair_sum_kernel(across, got, out):
    rows = across.shape[0]
    out[...] = (across[...].astype(f32) + got[rows:].astype(f32)).astype(bf16)


def expert_sum_kernel(own, got, far, out):
    rows = own.shape[0]
    total = own[...].astype(f32) + got[0:rows].astype(f32) + far[...].astype(f32)
    out[...] = total.astype(bf16)


def total_stats(packs, width):
    total = packs[0][width:width + 16].astype(f32)
    for p in packs[1:]:
        total += p[width:width + 16].astype(f32)
    return total


def gates_of(stats, model):
    inverse = lax.rsqrt((stats[0:1] + stats[1:2]) / model + epsilon)
    delta = inverse * (stats[2:3] + stats[3:4])
    return inverse, 1.0 / (1.0 + jnp.exp(-delta)), 1.0 / (1.0 + jnp.exp(delta))


def combine_kernel(t0, t1, t2, t3, dest, dy, residual, *refs, n_t):
    pieces, (output, pack) = refs[:-2], refs[-2:]
    width, tok = dy.shape
    _, gate0, gate1 = gates_of(total_stats((t0, t1, t2, t3), width), n_t * width)
    back = pieces[0][...]
    row = iota((back.shape[0], tok), 0).astype(f32)
    pick0 = (row == dest[0:1, :]).astype(f32).astype(bf16)
    pick1 = (row == dest[1:2, :]).astype(f32).astype(bf16)
    got0 = mm(back, pick0, (0, 0))
    got1 = mm(back, pick1, (0, 0))
    e0, e1 = got0[0:width], got1[0:width]
    output[...] = (residual[...] + gate0 * e0 + gate1 * e1).astype(bf16)
    dy_own = dy[...].astype(f32)
    dg0 = jnp.sum(dy_own * e0, axis=0, keepdims=True)
    dg1 = jnp.sum(dy_own * e1, axis=0, keepdims=True)
    pack[0:width] = (got0[width:] + got1[width:]).astype(bf16)
    pack[width:] = row_block(split_hi_lo(dg0) + split_hi_lo(dg1)).astype(bf16)


def backward_kernel(
    b0, b1, b2, b3, t0, t1, t2, t3,
    routes, router, gain, out_w, qkv_wt, heads, probs,
    c0, c1, c2, c3, dr1_own, d_proj, d_att, d_logits, gain_terms, d_scores,
    bs, ts, ys, dr, *, n_t,
):
    width = dr1_own.shape[0]
    tok = b0.shape[1]
    experts = router.shape[0]
    n_heads = probs.shape[0]
    size = width // n_heads
    model = n_t * width
    r, _ = my_place()
    packs, tokens = (b0, b1, b2, b3), (t0, t1, t2, t3)
    for k in range(n_t):
        s = r ^ k
        chunk(bs, s, width)[...] = packs[k][0:width].astype(f32)
        chunk(ts, s, width)[...] = tokens[k][0:width].astype(f32)
        chunk(ys, s, width)[...] = tokens[k][width + 16:].astype(f32)
    inverse, gate0, gate1 = gates_of(total_stats(tokens, width), model)
    back = total_stats(packs, width)
    dg0 = back[0:1] + back[1:2]
    dg1 = back[2:3] + back[3:4]
    mean_gate = gate0 * dg0 + gate1 * dg1
    x_of = iota((experts, tok), 0)
    dlog = jnp.where(routes[0:1, :] == x_of, gate0 * (dg0 - mean_gate), 0.0) + jnp.where(
        routes[1:2, :] == x_of, gate1 * (dg1 - mean_gate), 0.0
    )
    d_logits[...] = dlog
    dh2 = bs[...] + mm(router[...].astype(f32), dlog, (0, 0), precision=highest)
    res = ts[...]
    gain_terms[...] = dh2 * res * inverse
    weighted = dh2 * gain[...]
    dot = jnp.sum(weighted * res, axis=0, keepdims=True) * (inverse**3 / model)
    dr[...] = ys[...] + inverse * weighted - res * dot
    d_att[...] = dr[...].astype(bf16)
    dr1_own[...] = chunk(dr, r, width)[...]
    d_o = mm(out_w[...], d_att[...]).astype(bf16)
    scale = size ** -0.5
    for h in range(n_heads):
        q, k, v = (heads[j * width + h * size:j * width + (h + 1) * size] for j in range(3))
        d_oh = d_o[h * size:(h + 1) * size]
        prob = probs[h]
        d_prob = mm(v, d_oh, (0, 0))
        centre = jnp.sum(prob * d_prob, axis=0, keepdims=True)
        ds = (prob * (d_prob - centre)).astype(bf16)
        d_scores[h] = ds
        here = h * size
        d_proj[here:here + size] = (mm(k, ds) * scale).astype(bf16)
        here += width
        d_proj[here:here + size] = (mm(q, ds, (1, 1)) * scale).astype(bf16)
        here += width
        d_proj[here:here + size] = mm(d_oh, prob.astype(bf16), (1, 1)).astype(bf16)
    row_dot = jnp.sum(
        d_proj[...].astype(f32) * heads[...].astype(f32), axis=0, keepdims=True
    )
    stats = row_block(split_hi_lo(row_dot)).astype(bf16)
    dr[...] = mm(qkv_wt[...], d_proj[...])
    for k, c in enumerate((c0, c1, c2, c3)):
        c[0:width] = chunk(dr, r ^ k, width)[...].astype(bf16)
        c[width:] = stats


def small_grad_kernel(
    t0, t1, t2, t3, d_logits, gain_terms, gain1_row, gain2, saved, d_proj, d_att,
    d_scores, buckets, qkv_w, small, last, ts, padded, *, n_t, n_buckets, direct,
):
    packs = (t0, t1, t2, t3)
    width = d_proj.shape[0] // 3
    model = n_t * width
    inner = d_proj.shape[0]
    experts = d_logits.shape[0]
    tok = t0.shape[1]
    r, _ = my_place()
    for k, t in enumerate(packs):
        chunk(ts, r ^ k, width)[...] = t[0:width].astype(f32)
    inverse, _, _ = gates_of(total_stats(packs, width), model)
    normed = (ts[...] * inverse * gain2[...]).astype(bf16).astype(f32)
    small[0:experts] = mm(d_logits[...], normed, (1, 1), precision=highest)
    ones = jnp.ones((8, tok), f32)
    small[experts:] = jnp.zeros((small.shape[0] - experts, model), f32)
    small[experts:experts + 1] = mm(ones, gain_terms[...], (1, 1), precision=highest)[0:1]
    grad = mm(d_proj[...], saved[0:model], (1, 1))
    first = jnp.sum(grad * qkv_w[...].astype(f32), axis=0, keepdims=True)
    small[experts + 1:experts + 2] = first / gain1_row[...]
    hot = bucket_hot(buckets, padded, n_buckets)
    for h in range(d_scores.shape[0]):
        diagonal = jnp.sum(skew(d_scores[h].astype(f32), -1), axis=0, keepdims=True)
        per_bucket = mm(jnp.broadcast_to(diagonal, (8, tok)), hot, (1, 1), precision=highest)
        here = experts + 2 + h
        small[here:here + 1, 0:n_buckets] = per_bucket[0:1]
    if direct:
        last[0:inner] = d_proj[...]
        last[inner:inner + width] = chunk(d_att, r, width)[...]
        height = small.shape[0]
        for c in range(model // tok):
            here = inner + width + c * height
            last[here:here + height] = small[:, c * tok:(c + 1) * tok].astype(bf16)
    else:
        last[...] = mm(saved[model:], d_att[...], (1, 1)).astype(last.dtype)


def senders(n_e):
    _, e = my_place()
    half = n_e // 2
    return [lax.rem((e ^ (j // half)) + n_e - 2 * (j % half), n_e) for j in range(n_e)]


def late_sum_kernel(o0, o1, o2, o3, *refs, n_e, inner):
    lasts, (small, own, q1, q2, q3) = refs[:n_e], refs[n_e:]
    width = own.shape[0]
    stride, tok = lasts[0].shape
    height, model = small.shape
    total = lasts[0][inner + width:].astype(f32)
    for last in lasts[1:]:
        total += last[inner + width:].astype(f32)
    for c in range(model // tok):
        small[:, c * tok:(c + 1) * tok] = total[c * height:(c + 1) * height]
    first = small[height - 7:height - 6]
    hi, lo = split_hi_lo(first)
    wide = row_block(
        [v[:, s * width:(s + 1) * width] for v in (hi, lo) for s in range(model // width)]
    )
    for o, q in ((o0, own), (o1, q1), (o2, q2), (o3, q3)):
        grad = 0.0
        for last, sender in zip(lasts, senders(n_e)):
            grad += mm(chunk(o, sender, width)[...], last[inner:inner + width], (1, 1))
        q[0:width] = grad.astype(q.dtype)
        if q is not own:
            q[width:] = wide.astype(bf16)


def out_grad_kernel(
    own, q1, q2, q3, small, out, first, second, router, rel, blocks, line, *, n_t
):
    width = own.shape[0]
    experts, buckets = router.shape[0], rel.shape[1]
    r, _ = my_place()
    blocks[r] = own[...]
    for k, q in ((1, q1), (2, q2), (3, q3)):
        blocks[r ^ k] = q[0:width].astype(f32)
    for s in range(n_t):
        cols = slice(s * width, (s + 1) * width)
        out[:, cols] = blocks[s]
        total = small[experts + 1:experts + 2, cols]
        for q in (q1, q2, q3):
            parts = q[width:].astype(f32)
            total += parts[s:s + 1] + parts[n_t + s:n_t + s + 1]
        line[:, cols] = total
    first[...] = line[0]
    second[...] = small[experts]
    router[...] = small[0:experts]
    rel[...] = small[experts + 2:experts + 2 + rel.shape[0], 0:buckets]


def input_grad_kernel(c0, c1, c2, c3, dr1, inv1, x, gain, out, *, n_t):
    width = x.shape[0]
    total = c0[...].astype(f32) + c1[...].astype(f32) + (c2[...].astype(f32) + c3[...].astype(f32))
    row_dot = (total[width:width + 1] + total[width + 1:width + 2]) / (n_t * width)
    inverse = inv1[...]
    weighted = total[0:width] * chunk(gain, my_place()[0], width)[...]
    out[...] = dr1[...] + inverse * weighted - x[...].astype(f32) * (inverse * inverse * row_dot)


def qkv_grad_kernel(gathered, *refs, pieces, n_e, inner):
    lasts, rest = refs[:len(pieces)], refs[len(pieces):]
    out = rest[-1]
    model = out.shape[1]
    stride = gathered.shape[0] // n_e
    total = 0.0 if len(rest) == 1 else rest[0][...]
    for j, last in zip(pieces, lasts):
        sender = senders(n_e)[j] if n_e > 1 else 0
        h1 = chunk(gathered, sender, stride)[...][0:model]
        total += mm(last[0:inner], h1, (1, 1))
    out[...] = total


def per_device(
    tokens,
    first_gain,
    second_gain,
    qkv_weight,
    out_weight,
    rel_table,
    router_weight,
    up_weight,
    down_weight,
    routes,
    lengths,
    bucket_ids,
    cotangent,
    *,
    n_t,
    n_e,
):
    tok, width = tokens.shape
    model = n_t * width
    inner = 3 * width
    experts = router_weight.shape[1]
    cap = 5 * tok // (2 * experts)
    rows = experts * cap
    n_heads = rel_table.shape[1]
    n_buckets = rel_table.shape[0]
    direct = n_e == 8
    padded = pltpu.VMEM((1, tok), i32)

    def swap(v, k, axis="tensor", n=n_t):
        return lax.ppermute(v, axis, [(i, i ^ k) for i in range(n)])

    def around(v):
        return [v] + [swap(v, k) for k in range(1, n_t)]

    def around_large(v):
        far = swap(v, 2)
        return [v, swap(v, 1), far, swap(far, 1)]

    def exchange(v):
        w = v.shape[-1]
        v = v.reshape(n_e, rows // n_e, w)
        v = lax.all_to_all(v, "expert", split_axis=0, concat_axis=0, tiled=True)
        return v.reshape(rows, w)

    def over_pairs(v):
        return [
            lax.ppermute(v, "expert", [(i, (i + 2 * k) % n_e) for i in range(n_e)])
            for k in range(1, n_e // 2)
        ]

    def after(values, *others):
        return list(lax.optimization_barrier((tuple(values), others))[0])

    x = tokens.T
    dy = cotangent.T
    qkv_w = qkv_weight.transpose(0, 2, 1).reshape(inner, model)
    router = router_weight.T
    table = rel_table.T
    routes_t = routes.T
    gain1_row = first_gain.reshape(1, model)
    gain2_row = second_gain.reshape(1, model)
    buckets = bucket_ids.reshape(1, -1)

    xs = around(x)
    gain1, out_wt, bias = run(
        prepare_kernel,
        [((model, 1), f32), ((model, width), bf16), ((n_heads, tok, tok), f32)],
        lengths, gain1_row, out_weight, table, buckets,
        fetch=(0, 1, 2, 3, 4),
        scratch=[padded],
    )
    own, p1, p2, p3, inv1, heads, probs, saved = run(
        functools.partial(attention_kernel, n_t=n_t),
        [((width, tok), f32)]
        + [((width, tok), bf16)] * 3
        + [
            ((1, tok), f32),
            ((inner, tok), bf16),
            ((n_heads, tok, tok), f32),
            ((model + width, tok), bf16),
        ],
        *xs, gain1, qkv_w, out_wt, bias,
        fetch=(n_t + 1,),
        scratch=[pltpu.VMEM((model, tok), f32), pltpu.VMEM((model, tok), f32)],
    )
    got = [swap(p, k) for k, p in ((1, p1), (2, p2), (3, p3))]
    if direct:
        saved_all = lax.all_gather(saved, "expert", axis=0, tiled=True)
    dest, gain2, rw_own, qkv_wt = run(
        functools.partial(route_kernel, experts=experts, cap=cap, n_t=n_t),
        [
            ((8, tok), f32),
            ((model, 1), f32),
            ((experts, width), bf16),
            ((model, inner), bf16),
        ],
        routes_t, router, gain2_row, qkv_w, inv1,
        fetch=(0, 1, 2, 3),
        scratch=[pltpu.VMEM((n_t, experts, width), f32)],
    )
    send_rows, token_pack, residual = run(
        dispatch_kernel,
        [
            ((rows, 2 * width + 16), bf16),
            ((2 * width + 16, tok), bf16),
            ((width, tok), f32),
        ],
        own, *got, x, dy, gain2, rw_own, routes_t, dest,
        fetch=(4, 5, 8),
        scratch=[pltpu.VMEM((2 * width + 16, tok), bf16)],
    )
    in_rows = around_large(exchange(send_rows))
    token_packs = around(after([token_pack], in_rows[1])[0])

    own, across, mate, u, z, de, da = run(
        functools.partial(expert_kernel, n_t=n_t),
        [((rows, 2 * width), bf16)] * 2
        + [((2 * rows, 2 * width), bf16)]
        + [((rows, model), bf16)] * 4,
        *in_rows, up_weight, down_weight,
        fetch=(4, 5),
        scratch=[
            pltpu.VMEM((n_t, rows, width), f32),
            pltpu.VMEM((n_t, rows, width), f32),
            pltpu.VMEM((n_t, rows, 2 * width), bf16),
        ],
    )
    got = swap(mate, 1)
    (across,) = run(pair_sum_kernel, [((rows, 2 * width), bf16)], across, got)
    far = swap(across, 2)
    up_grad, down_grad = run(
        expert_grad_kernel,
        [(up_weight.shape, f32), (down_weight.shape, f32)],
        *after([u, z, de, da], across),
    )
    (far,) = after([far], up_grad, *token_packs[1:])
    (summed,) = run(expert_sum_kernel, [((rows, 2 * width), bf16)], own, got, far)
    back = exchange(summed)
    output, back_pack = run(
        functools.partial(combine_kernel, n_t=n_t),
        [((width, tok), bf16), ((width + 16, tok), bf16)],
        *token_packs, dest, dy, residual, back,
        fetch=(5,),
    )
    back_packs = around(back_pack)

    c0, c1, c2, c3, dr1, d_proj, d_att, d_logits, gain_terms, d_scores = run(
        functools.partial(backward_kernel, n_t=n_t),
        [((width + 16, tok), bf16)] * 4
        + [
            ((width, tok), f32),
            ((inner, tok), bf16),
            ((model, tok), bf16),
            ((experts, tok), f32),
            ((model, tok), f32),
            ((n_heads, tok, tok), bf16),
        ],
        *back_packs, *token_packs, routes_t, router, gain2, out_weight, qkv_wt, heads, probs,
        fetch=(8, 9, 11),
        scratch=[pltpu.VMEM((model, tok), f32)] * 4,
    )
    height = experts + 8
    if direct:
        last_shape = (inner + width + height * (model // tok), tok)
    else:
        last_shape = out_weight.shape
    small, last = run(
        functools.partial(small_grad_kernel, n_t=n_t, n_buckets=n_buckets, direct=direct),
        [((height, model), f32), (last_shape, bf16)],
        *token_packs, d_logits, gain_terms, gain1_row, gain2, saved, d_proj, d_att,
        d_scores, buckets, qkv_w,
        fetch=(6, 12, 13),
        scratch=[pltpu.VMEM((model, tok), f32), padded],
    )
    if direct:
        lasts = [last] + over_pairs(last)
    got = [swap(c, k) for k, c in ((1, c1), (2, c2), (3, c3))]
    (input_grad,) = run(
        functools.partial(input_grad_kernel, n_t=n_t),
        [((width, tok), f32)],
        c0, *got, dr1, inv1, x, gain1,
        fetch=(6,),
    )
    if direct:
        (att,) = run(
            functools.partial(join_kernel, n_e=n_e),
            [((n_e * width, tok), bf16)],
            *after([saved_all], last),
        )
        atts = around_large(att)
        half = n_e // 2
        (part,) = run(
            functools.partial(qkv_grad_kernel, pieces=range(half), n_e=n_e, inner=inner),
            [((inner, model), f32)],
            saved_all, *lasts,
        )
        lasts = lasts + [swap(v, 1, "expert", n_e) for v in lasts]
        lasts[half:] = after(lasts[half:], part, input_grad)
        small, own, q1, q2, q3 = run(
            functools.partial(late_sum_kernel, n_e=n_e, inner=inner),
            [((height, model), f32), ((width, width), f32)]
            + [((width + 16, width), bf16)] * 3,
            *atts, *lasts,
        )
        got = [swap(q, k) for k, q in ((1, q1), (2, q2), (3, q3))]
        (part,) = after([part], own)
        (qkv_grad,) = run(
            functools.partial(qkv_grad_kernel, pieces=range(half, n_e), n_e=n_e, inner=inner),
            [((inner, model), f32)],
            saved_all, *lasts[half:], part,
        )
        out_grad, first, second, router_grad, rel_grad = run(
            functools.partial(out_grad_kernel, n_t=n_t),
            [
                (out_weight.shape, f32),
                ((model,), f32),
                ((model,), f32),
                ((experts, model), f32),
                ((n_heads, n_buckets), f32),
            ],
            own, *got, small,
            scratch=[pltpu.VMEM((n_t, width, width), f32), pltpu.VMEM((1, model), f32)],
        )
    else:
        small, out_grad = lax.psum((small, last.astype(f32)), "expert")
        (qkv_grad,) = run(
            functools.partial(qkv_grad_kernel, pieces=range(1), n_e=1, inner=inner),
            [((inner, model), f32)],
            saved, d_proj,
        )
        qkv_grad = lax.psum(qkv_grad, "expert")
        first = lax.psum(small[experts + 1], "tensor")
        second = small[experts]
        router_grad = small[:experts]
        rel_grad = small[experts + 2:experts + 2 + n_heads, :n_buckets]
    return (
        output.T,
        input_grad.T,
        first.reshape(model),
        second.reshape(model),
        qkv_grad.reshape(3, width, model).transpose(0, 2, 1),
        out_grad,
        rel_grad.T,
        router_grad.T,
        up_grad,
        down_grad,
    )


def solution(mesh):
    placed = (
        P("expert", "tensor"),
        P(),
        P(),
        P(None, None, "tensor"),
        P("tensor", None),
        P(None, "tensor"),
        P(),
        P("expert", None, "tensor"),
        P("expert", "tensor", None),
        P("expert", None),
        P("expert", None),
        P(),
        P("expert", "tensor"),
    )
    return jax.shard_map(
        functools.partial(per_device, n_t=mesh.shape["tensor"], n_e=mesh.shape["expert"]),
        mesh=mesh,
        in_specs=placed,
        out_specs=(
            P("expert", "tensor"),
            P("expert", "tensor"),
            P(),
            P(),
            P(None, None, "tensor"),
            P("tensor", None),
            P(None, "tensor"),
            P(),
            P("expert", None, "tensor"),
            P("expert", "tensor", None),
        ),
        check_vma=False,
    )
```

```python
import functools
import math

import jax
import jax.numpy as jnp
from jax import lax
from jax.experimental import pallas as pl
from jax.experimental.pallas import tpu as pltpu
from jax.sharding import PartitionSpec as P

epsilon = 1e-06
highest = lax.Precision.HIGHEST
big_negative = -1e30
bf16 = jnp.bfloat16
f32 = jnp.float32
i32 = jnp.int32


def mm(a, b, contract=(1, 0), precision=None):
    return lax.dot_general(
        a,
        b,
        (((contract[0],), (contract[1],)), ((), ())),
        preferred_element_type=f32,
        precision=precision,
    )


def iota(shape, dim):
    return lax.broadcasted_iota(i32, shape, dim)


def split_hi_lo(v):
    hi = v.astype(bf16).astype(f32)
    return hi, v - hi


def row_block(values, rows=16):
    lanes = values[0].shape[1]
    row = iota((rows, lanes), 0)
    block = jnp.zeros((rows, lanes), f32)
    for i, v in enumerate(values):
        block = jnp.where(row == i, v, block)
    return block


def run(body, outs, *args, fetch=(), scratch=(), limit=32):
    n, m, f = len(args), len(outs), len(fetch)
    moved = sum(a.size * a.dtype.itemsize for a in args)
    moved += sum(math.prod(s) * jnp.dtype(d).itemsize for s, d in outs)
    held = [pltpu.VMEM(args[i].shape, args[i].dtype) for i in fetch]
    sems = [pltpu.SemaphoreType.DMA((f,))] if f else []

    def whole(*refs):
        ins, rest = list(refs[:n]), refs[n + m:]
        copies = [
            pltpu.make_async_copy(ins[i], rest[j], rest[f].at[j]) for j, i in enumerate(fetch)
        ]
        for copy in copies:
            copy.start()
        for copy in copies:
            copy.wait()
        for j, i in enumerate(fetch):
            ins[i] = rest[j]
        body(*ins, *refs[n:n + m], *rest[f + len(sems):])

    return pl.pallas_call(
        whole,
        out_shape=[jax.ShapeDtypeStruct(s, d) for s, d in outs],
        in_specs=[
            pl.BlockSpec(memory_space=pltpu.HBM) if i in fetch else pl.BlockSpec()
            for i in range(n)
        ],
        out_specs=[pl.BlockSpec()] * m,
        scratch_shapes=held + sems + list(scratch),
        compiler_params=pltpu.CompilerParams(vmem_limit_bytes=limit * 2**20),
        cost_estimate=pl.CostEstimate(flops=0, bytes_accessed=moved, transcendentals=0),
    )(*args)


def my_place():
    return lax.axis_index("tensor"), lax.axis_index("expert")


def column_of(row, out):
    for c in range(row.shape[1] // 128):
        part = jnp.broadcast_to(row[:, c * 128:(c + 1) * 128], (128, 128))
        part = jnp.where(iota((128, 128), 0) == iota((128, 128), 1), part, 0.0)
        out[c * 128:(c + 1) * 128, :] = jnp.sum(part, axis=1, keepdims=True)


def skew(values, sign):
    n = values.shape[0]
    row = iota(values.shape, 0)
    bit = 1
    while bit < n:
        moved = pltpu.roll(values, bit if sign > 0 else n - bit, 1)
        values = jnp.where((row & bit) != 0, moved, values)
        bit *= 2
    return values


def bucket_hot(buckets, padded, count):
    padded[...] = jnp.full(padded.shape, -1, i32)
    padded[:, 0:buckets.shape[1]] = buckets[...]
    return (padded[...] == iota((count, padded.shape[1]), 0)).astype(f32)


def prepare_kernel(lengths, gain, out_w, table, buckets, gain_col, out_wt, bias, padded):
    tok = bias.shape[1]
    column_of(gain[...], gain_col)
    out_wt[...] = out_w[...].astype(f32).T.astype(bf16)
    key_pos = iota((tok, tok), 0)
    query_pos = iota((tok, tok), 1)
    end0 = lengths[0:1, 0:1]
    end1 = end0 + lengths[0:1, 1:2]
    seg_k = (key_pos >= end0).astype(i32) + (key_pos >= end1).astype(i32)
    seg_q = (query_pos >= end0).astype(i32) + (query_pos >= end1).astype(i32)
    allowed = (seg_k == seg_q) & (key_pos <= query_pos)
    hot = bucket_hot(buckets, padded, table.shape[1])
    per_head = mm(table[...], hot, precision=highest)
    for h in range(table.shape[0]):
        full = skew(jnp.broadcast_to(per_head[h:h + 1], (tok, tok)), 1)
        bias[h] = jnp.where(allowed, full, big_negative)


def route_kernel(
    routes, router, gain, qkv_w, after, dest, gain_col, rw_own, qkv_wt, chunks,
    *, experts, cap, n_t,
):
    tok = routes.shape[1]
    width = rw_own.shape[1]
    rt = routes[...]
    x_of = iota((experts, tok), 0)
    m0 = (rt[0:1] == x_of).astype(f32)
    m1 = (rt[1:2] == x_of).astype(f32)
    earlier = (iota((tok, tok), 0) < iota((tok, tok), 1)).astype(f32).astype(bf16)
    counts = mm((m0 + m1).astype(bf16), earlier)
    rows = [
        rt[i:i + 1].astype(f32) * cap + jnp.sum(m * counts, axis=0, keepdims=True)
        for i, m in enumerate((m0, m1))
    ]
    dest[...] = row_block(rows, 8)
    column_of(gain[...], gain_col)
    wide = router[...].astype(f32)
    for s in range(n_t):
        chunks[s] = wide[:, s * width:(s + 1) * width]
    rw_own[...] = chunks[my_place()[0]].astype(bf16)
    qkv_wt[...] = qkv_w[...].astype(f32).T.astype(bf16)


def chunk(ref, s, width):
    return ref.at[pl.ds(pl.multiple_of(s * width, 64), width)]


def attention_kernel(
    x0, x1, x2, x3, gain, qkv_w, out_wt, bias,
    own, p1, p2, p3, inv1, heads, probs, saved,
    xs, parts, *, n_t,
):
    width, tok = x0.shape
    n_heads = bias.shape[0]
    size = width // n_heads
    model = n_t * width
    r, _ = my_place()
    for k, x in enumerate((x0, x1, x2, x3)):
        chunk(xs, r ^ k, width)[...] = x[...].astype(f32)
    inverse = lax.rsqrt(jnp.sum(xs[...] * xs[...], axis=0, keepdims=True) / model + epsilon)
    inv1[...] = inverse
    saved[0:model] = (xs[...] * inverse * gain[...]).astype(bf16)
    heads[...] = mm(qkv_w[...], saved[0:model]).astype(bf16)
    for h in range(n_heads):
        q, k, v = (heads[j * width + h * size:j * width + (h + 1) * size] for j in range(3))
        scores = mm(k, q, (0, 0)) * (size ** -0.5) + bias[h]
        weights = jnp.exp(scores - jnp.max(scores, axis=0, keepdims=True))
        prob = weights / jnp.sum(weights, axis=0, keepdims=True)
        probs[h] = prob
        here = model + h * size
        saved[here:here + size] = mm(v, prob.astype(bf16)).astype(bf16)
    parts[...] = mm(out_wt[...], saved[model:])
    own[...] = chunk(parts, r, width)[...]
    for k, p in ((1, p1), (2, p2), (3, p3)):
        p[...] = chunk(parts, r ^ k, width)[...].astype(bf16)


def dispatch_kernel(
    own, p1, p2, p3, x, dy, gain, rw_own, routes, dest, *refs
):
    pieces = refs[:-3]
    token_pack, residual, pack = refs[-3:]
    width, tok = x.shape
    experts = rw_own.shape[0]
    r, _ = my_place()
    res = x[...].astype(f32) + own[...] + (
        p1[...].astype(f32) + p2[...].astype(f32) + p3[...].astype(f32)
    )
    residual[...] = res
    scaled = (res * chunk(gain, r, width)[...]).astype(bf16)
    square = jnp.sum(res * res, axis=0, keepdims=True)
    logits = mm(rw_own[...], scaled)
    x_of = iota((experts, tok), 0)
    c0 = jnp.sum(jnp.where(routes[0:1, :] == x_of, logits, 0.0), axis=0, keepdims=True)
    c1 = jnp.sum(jnp.where(routes[1:2, :] == x_of, logits, 0.0), axis=0, keepdims=True)
    stats = row_block(split_hi_lo(square) + split_hi_lo(c0 - c1)).astype(bf16)
    token_pack[0:width] = res.astype(bf16)
    token_pack[width:width + 16] = stats
    token_pack[width + 16:] = dy[...]
    pack[0:width] = scaled
    pack[width:width + 16] = stats
    pack[width + 16:] = dy[...]
    size = pieces[0].shape[0]
    row = iota((size * len(pieces), tok), 0).astype(f32)
    place0 = (row == dest[0:1, :]).astype(f32)
    place1 = (row == dest[1:2, :]).astype(f32)
    both = mm((place0 + place1).astype(bf16), pack[...], (1, 1))
    signed = mm((place0 - place1).astype(bf16), pack[...], (1, 1))
    lane = iota(both.shape, 1)
    full = jnp.where((lane == width + 2) | (lane == width + 3), signed, both)
    for k, piece in enumerate(pieces):
        piece[...] = full[k * size:(k + 1) * size].astype(bf16)


def gelu_pair(a):
    c = 0.7978845608028654
    t = jnp.tanh(c * (a + 0.044715 * a * a * a))
    value = 0.5 * a * (1.0 + t)
    slope = 0.5 * (1.0 + t) + 0.5 * a * (1.0 - t * t) * c * (1.0 + 3 * 0.044715 * a * a)
    return value, slope


def expert_kernel(
    h0, h1, h2, h3, up, down,
    own, across, mate, u, z, de, da,
    hs, gs, chunks, *, n_t,
):
    width = own.shape[1] // 2
    model = n_t * width
    r, _ = my_place()
    packs = (h0, h1, h2, h3)
    for k, h in enumerate(packs):
        s = r ^ k
        hs[s] = h[:, 0:width].astype(f32)
        gs[s] = h[:, width + 16:].astype(f32)
    stats = h0[:, width:width + 16].astype(f32)
    for h in packs[1:]:
        stats += h[:, width:width + 16].astype(f32)
    inverse = lax.rsqrt((stats[:, 0:1] + stats[:, 1:2]) / model + epsilon)
    gate = 1.0 / (1.0 + jnp.exp(-inverse * (stats[:, 2:3] + stats[:, 3:4])))
    for s in range(n_t):
        cols = slice(s * width, (s + 1) * width)
        u[:, cols] = (hs[s] * inverse).astype(bf16)
        de[:, cols] = (gs[s] * gate).astype(bf16)
    value, slope = gelu_pair(mm(u[...], up[0]))
    z[...] = value.astype(bf16)
    da[...] = (mm(de[...], down[0], (1, 1)) * slope).astype(bf16)
    eo = mm(z[...], down[0]).astype(bf16)
    du = mm(da[...], up[0], (1, 1)).astype(bf16)
    for s in range(n_t):
        cols = slice(s * width, (s + 1) * width)
        chunks[s, :, 0:width] = eo[:, cols]
        chunks[s, :, width:] = du[:, cols]
    rows = own.shape[0]
    own[...] = chunks[r]
    across[...] = chunks[r ^ 2]
    mate[0:rows] = chunks[r ^ 1]
    mate[rows:] = chunks[r ^ 3]


def expert_grad_kernel(u, z, de, da, up_grad, down_grad):
    up_grad[0] = mm(u[...], da[...], (0, 0))
    down_grad[0] = mm(z[...], de[...], (0, 0))


def join_kernel(*refs):
    parts, out = refs[:-1], refs[-1]
    height = out.shape[0] // len(parts)
    for j, part in enumerate(parts):
        out[j * height:(j + 1) * height] = part[part.shape[0] - height:]


def pair_sum_kernel(across, got, out):
    rows = across.shape[0]
    out[...] = (across[...].astype(f32) + got[rows:].astype(f32)).astype(bf16)


def expert_sum_kernel(own, got, far, out):
    rows = own.shape[0]
    total = own[...].astype(f32) + got[0:rows].astype(f32) + far[...].astype(f32)
    out[...] = total.astype(bf16)


def total_stats(packs, width):
    total = packs[0][width:width + 16].astype(f32)
    for p in packs[1:]:
        total += p[width:width + 16].astype(f32)
    return total


def gates_of(stats, model):
    inverse = lax.rsqrt((stats[0:1] + stats[1:2]) / model + epsilon)
    delta = inverse * (stats[2:3] + stats[3:4])
    return inverse, 1.0 / (1.0 + jnp.exp(-delta)), 1.0 / (1.0 + jnp.exp(delta))


def combine_kernel(t0, t1, t2, t3, dest, dy, residual, *refs, n_t):
    pieces, (output, pack) = refs[:-2], refs[-2:]
    width, tok = dy.shape
    _, gate0, gate1 = gates_of(total_stats((t0, t1, t2, t3), width), n_t * width)
    back = pieces[0][...]
    row = iota((back.shape[0], tok), 0).astype(f32)
    pick0 = (row == dest[0:1, :]).astype(f32).astype(bf16)
    pick1 = (row == dest[1:2, :]).astype(f32).astype(bf16)
    got0 = mm(back, pick0, (0, 0))
    got1 = mm(back, pick1, (0, 0))
    e0, e1 = got0[0:width], got1[0:width]
    output[...] = (residual[...] + gate0 * e0 + gate1 * e1).astype(bf16)
    dy_own = dy[...].astype(f32)
    dg0 = jnp.sum(dy_own * e0, axis=0, keepdims=True)
    dg1 = jnp.sum(dy_own * e1, axis=0, keepdims=True)
    pack[0:width] = (got0[width:] + got1[width:]).astype(bf16)
    pack[width:] = row_block(split_hi_lo(dg0) + split_hi_lo(dg1)).astype(bf16)


def backward_kernel(
    b0, b1, b2, b3, t0, t1, t2, t3,
    routes, router, gain, out_w, qkv_wt, heads, probs,
    c0, c1, c2, c3, dr1_own, d_proj, d_att, d_logits, gain_terms, d_scores,
    bs, ts, ys, dr, *, n_t,
):
    width = dr1_own.shape[0]
    tok = b0.shape[1]
    experts = router.shape[0]
    n_heads = probs.shape[0]
    size = width // n_heads
    model = n_t * width
    r, _ = my_place()
    packs, tokens = (b0, b1, b2, b3), (t0, t1, t2, t3)
    for k in range(n_t):
        s = r ^ k
        chunk(bs, s, width)[...] = packs[k][0:width].astype(f32)
        chunk(ts, s, width)[...] = tokens[k][0:width].astype(f32)
        chunk(ys, s, width)[...] = tokens[k][width + 16:].astype(f32)
    inverse, gate0, gate1 = gates_of(total_stats(tokens, width), model)
    back = total_stats(packs, width)
    dg0 = back[0:1] + back[1:2]
    dg1 = back[2:3] + back[3:4]
    mean_gate = gate0 * dg0 + gate1 * dg1
    x_of = iota((experts, tok), 0)
    dlog = jnp.where(routes[0:1, :] == x_of, gate0 * (dg0 - mean_gate), 0.0) + jnp.where(
        routes[1:2, :] == x_of, gate1 * (dg1 - mean_gate), 0.0
    )
    d_logits[...] = dlog
    dh2 = bs[...] + mm(router[...].astype(f32), dlog, (0, 0), precision=highest)
    res = ts[...]
    gain_terms[...] = dh2 * res * inverse
    weighted = dh2 * gain[...]
    dot = jnp.sum(weighted * res, axis=0, keepdims=True) * (inverse**3 / model)
    dr[...] = ys[...] + inverse * weighted - res * dot
    d_att[...] = dr[...].astype(bf16)
    dr1_own[...] = chunk(dr, r, width)[...]
    d_o = mm(out_w[...], d_att[...]).astype(bf16)
    scale = size ** -0.5
    for h in range(n_heads):
        q, k, v = (heads[j * width + h * size:j * width + (h + 1) * size] for j in range(3))
        d_oh = d_o[h * size:(h + 1) * size]
        prob = probs[h]
        d_prob = mm(v, d_oh, (0, 0))
        centre = jnp.sum(prob * d_prob, axis=0, keepdims=True)
        ds = (prob * (d_prob - centre)).astype(bf16)
        d_scores[h] = ds
        here = h * size
        d_proj[here:here + size] = (mm(k, ds) * scale).astype(bf16)
        here += width
        d_proj[here:here + size] = (mm(q, ds, (1, 1)) * scale).astype(bf16)
        here += width
        d_proj[here:here + size] = mm(d_oh, prob.astype(bf16), (1, 1)).astype(bf16)
    row_dot = jnp.sum(
        d_proj[...].astype(f32) * heads[...].astype(f32), axis=0, keepdims=True
    )
    stats = row_block(split_hi_lo(row_dot)).astype(bf16)
    dr[...] = mm(qkv_wt[...], d_proj[...])
    for k, c in enumerate((c0, c1, c2, c3)):
        c[0:width] = chunk(dr, r ^ k, width)[...].astype(bf16)
        c[width:] = stats


def small_grad_kernel(
    t0, t1, t2, t3, d_logits, gain_terms, gain1_row, gain2, saved, d_proj, d_att,
    d_scores, buckets, qkv_w, small, last, ts, padded, *, n_t, n_buckets, direct,
):
    packs = (t0, t1, t2, t3)
    width = d_proj.shape[0] // 3
    model = n_t * width
    inner = d_proj.shape[0]
    experts = d_logits.shape[0]
    tok = t0.shape[1]
    r, _ = my_place()
    for k, t in enumerate(packs):
        chunk(ts, r ^ k, width)[...] = t[0:width].astype(f32)
    inverse, _, _ = gates_of(total_stats(packs, width), model)
    normed = (ts[...] * inverse * gain2[...]).astype(bf16).astype(f32)
    small[0:experts] = mm(d_logits[...], normed, (1, 1), precision=highest)
    ones = jnp.ones((8, tok), f32)
    small[experts:] = jnp.zeros((small.shape[0] - experts, model), f32)
    small[experts:experts + 1] = mm(ones, gain_terms[...], (1, 1), precision=highest)[0:1]
    grad = mm(d_proj[...], saved[0:model], (1, 1))
    first = jnp.sum(grad * qkv_w[...].astype(f32), axis=0, keepdims=True)
    small[experts + 1:experts + 2] = first / gain1_row[...]
    hot = bucket_hot(buckets, padded, n_buckets)
    for h in range(d_scores.shape[0]):
        diagonal = jnp.sum(skew(d_scores[h].astype(f32), -1), axis=0, keepdims=True)
        per_bucket = mm(jnp.broadcast_to(diagonal, (8, tok)), hot, (1, 1), precision=highest)
        here = experts + 2 + h
        small[here:here + 1, 0:n_buckets] = per_bucket[0:1]
    if direct:
        last[0:inner] = d_proj[...]
        last[inner:inner + width] = chunk(d_att, r, width)[...]
        height = small.shape[0]
        for c in range(model // tok):
            here = inner + width + c * height
            last[here:here + height] = small[:, c * tok:(c + 1) * tok].astype(bf16)
    else:
        last[...] = mm(saved[model:], d_att[...], (1, 1)).astype(last.dtype)


def late_sum_kernel(o0, o1, o2, o3, *refs, n_e, inner):
    lasts, (small, own, q1, q2, q3) = refs[:n_e], refs[n_e:]
    width = own.shape[0]
    stride, tok = lasts[0].shape
    height, model = small.shape
    total = lasts[0][inner + width:].astype(f32)
    for last in lasts[1:]:
        total += last[inner + width:].astype(f32)
    for c in range(model // tok):
        small[:, c * tok:(c + 1) * tok] = total[c * height:(c + 1) * height]
    first = small[height - 7:height - 6]
    hi, lo = split_hi_lo(first)
    wide = row_block(
        [v[:, s * width:(s + 1) * width] for v in (hi, lo) for s in range(model // width)]
    )
    for o, q in ((o0, own), (o1, q1), (o2, q2), (o3, q3)):
        grad = 0.0
        for j, last in enumerate(lasts):
            grad += mm(o[j * width:(j + 1) * width], last[inner:inner + width], (1, 1))
        q[0:width] = grad.astype(q.dtype)
        if q is not own:
            q[width:] = wide.astype(bf16)


def out_grad_kernel(
    own, q1, q2, q3, small, out, first, second, router, rel, blocks, line, *, n_t
):
    width = own.shape[0]
    experts, buckets = router.shape[0], rel.shape[1]
    r, _ = my_place()
    blocks[r] = own[...]
    for k, q in ((1, q1), (2, q2), (3, q3)):
        blocks[r ^ k] = q[0:width].astype(f32)
    for s in range(n_t):
        cols = slice(s * width, (s + 1) * width)
        out[:, cols] = blocks[s]
        total = small[experts + 1:experts + 2, cols]
        for q in (q1, q2, q3):
            parts = q[width:].astype(f32)
            total += parts[s:s + 1] + parts[n_t + s:n_t + s + 1]
        line[:, cols] = total
    first[...] = line[0]
    second[...] = small[experts]
    router[...] = small[0:experts]
    rel[...] = small[experts + 2:experts + 2 + rel.shape[0], 0:buckets]


def input_grad_kernel(c0, c1, c2, c3, dr1, inv1, x, gain, out, *, n_t):
    width = x.shape[0]
    total = c0[...].astype(f32) + c1[...].astype(f32) + (c2[...].astype(f32) + c3[...].astype(f32))
    row_dot = (total[width:width + 1] + total[width + 1:width + 2]) / (n_t * width)
    inverse = inv1[...]
    weighted = total[0:width] * chunk(gain, my_place()[0], width)[...]
    out[...] = dr1[...] + inverse * weighted - x[...].astype(f32) * (inverse * inverse * row_dot)


def qkv_grad_kernel(*refs, count, inner):
    lasts, saved, rest = refs[:count], refs[count:2 * count], refs[2 * count:]
    out = rest[-1]
    model = out.shape[1]
    total = 0.0 if len(rest) == 1 else rest[0][...]
    for last, h in zip(lasts, saved):
        total += mm(last[0:inner], h[0:model], (1, 1))
    out[...] = total


def per_device(
    tokens,
    first_gain,
    second_gain,
    qkv_weight,
    out_weight,
    rel_table,
    router_weight,
    up_weight,
    down_weight,
    routes,
    lengths,
    bucket_ids,
    cotangent,
    *,
    n_t,
    n_e,
):
    tok, width = tokens.shape
    model = n_t * width
    inner = 3 * width
    experts = router_weight.shape[1]
    cap = 5 * tok // (2 * experts)
    rows = experts * cap
    n_heads = rel_table.shape[1]
    n_buckets = rel_table.shape[0]
    direct = n_e == 8
    padded = pltpu.VMEM((1, tok), i32)

    def swap(v, k, axis="tensor", n=n_t):
        return lax.ppermute(v, axis, [(i, i ^ k) for i in range(n)])

    def around(v):
        return [v] + [swap(v, k) for k in range(1, n_t)]

    def around_large(v):
        far = swap(v, 2)
        return [v, swap(v, 1), far, swap(far, 1)]

    def exchange(v):
        w = v.shape[-1]
        v = v.reshape(n_e, rows // n_e, w)
        v = lax.all_to_all(v, "expert", split_axis=0, concat_axis=0, tiled=True)
        return v.reshape(rows, w)

    def step(v, k):
        return lax.ppermute(v, "expert", [(i, (i + k) % n_e) for i in range(n_e)])

    def after(values, *others):
        return list(lax.optimization_barrier((tuple(values), others))[0])

    x = tokens.T
    dy = cotangent.T
    qkv_w = qkv_weight.transpose(0, 2, 1).reshape(inner, model)
    router = router_weight.T
    table = rel_table.T
    routes_t = routes.T
    gain1_row = first_gain.reshape(1, model)
    gain2_row = second_gain.reshape(1, model)
    buckets = bucket_ids.reshape(1, -1)

    xs = around(x)
    gain1, out_wt, bias = run(
        prepare_kernel,
        [((model, 1), f32), ((model, width), bf16), ((n_heads, tok, tok), f32)],
        lengths, gain1_row, out_weight, table, buckets,
        fetch=(0, 1, 2, 3, 4),
        scratch=[padded],
    )
    own, p1, p2, p3, inv1, heads, probs, saved = run(
        functools.partial(attention_kernel, n_t=n_t),
        [((width, tok), f32)]
        + [((width, tok), bf16)] * 3
        + [
            ((1, tok), f32),
            ((inner, tok), bf16),
            ((n_heads, tok, tok), f32),
            ((model + width, tok), bf16),
        ],
        *xs, gain1, qkv_w, out_wt, bias,
        fetch=(n_t + 1,),
        scratch=[pltpu.VMEM((model, tok), f32), pltpu.VMEM((model, tok), f32)],
    )
    got = [swap(p, k) for k, p in ((1, p1), (2, p2), (3, p3))]
    dest, gain2, rw_own, qkv_wt = run(
        functools.partial(route_kernel, experts=experts, cap=cap, n_t=n_t),
        [
            ((8, tok), f32),
            ((model, 1), f32),
            ((experts, width), bf16),
            ((model, inner), bf16),
        ],
        routes_t, router, gain2_row, qkv_w, inv1,
        fetch=(0, 1, 2, 3),
        scratch=[pltpu.VMEM((n_t, experts, width), f32)],
    )
    send_rows, token_pack, residual = run(
        dispatch_kernel,
        [
            ((rows, 2 * width + 16), bf16),
            ((2 * width + 16, tok), bf16),
            ((width, tok), f32),
        ],
        own, *got, x, dy, gain2, rw_own, routes_t, dest,
        fetch=(4, 5, 8),
        scratch=[pltpu.VMEM((2 * width + 16, tok), bf16)],
    )
    in_rows = exchange(send_rows)
    if direct:
        (early,) = after([saved], in_rows)
        in_rows = around_large(in_rows)
        behind1, behind3 = step(early, 2), step(early, 6)
        beside = swap(early, 1, "expert", n_e)
        in_rows = after(in_rows, behind1, behind3, beside)
    else:
        in_rows = around_large(in_rows)

    own, across, mate, u, z, de, da = run(
        functools.partial(expert_kernel, n_t=n_t),
        [((rows, 2 * width), bf16)] * 2
        + [((2 * rows, 2 * width), bf16)]
        + [((rows, model), bf16)] * 4,
        *in_rows, up_weight, down_weight,
        fetch=(4, 5),
        scratch=[
            pltpu.VMEM((n_t, rows, width), f32),
            pltpu.VMEM((n_t, rows, width), f32),
            pltpu.VMEM((n_t, rows, 2 * width), bf16),
        ],
    )
    got = swap(mate, 1)
    if direct:
        early, behind1 = after([early, behind1], mate)
        behind2, beside1 = step(early, 4), swap(behind1, 1, "expert", n_e)
    (across,) = run(pair_sum_kernel, [((rows, 2 * width), bf16)], across, got)
    far = swap(across, 2)
    up_grad, down_grad = run(
        expert_grad_kernel,
        [(up_weight.shape, f32), (down_weight.shape, f32)],
        *after([u, z, de, da], across),
    )
    token_packs = around(after([token_pack], up_grad)[0])
    if direct:
        beside3 = swap(after([behind3], across)[0], 1, "expert", n_e)
        (far,) = after([far], behind2, beside1, beside3)
    (far,) = after([far], up_grad)
    (summed,) = run(expert_sum_kernel, [((rows, 2 * width), bf16)], own, got, far)
    back = exchange(summed)
    output, back_pack = run(
        functools.partial(combine_kernel, n_t=n_t),
        [((width, tok), bf16), ((width + 16, tok), bf16)],
        *token_packs, dest, dy, residual, back,
        fetch=(5,),
    )
    back_packs = around(back_pack)
    if direct:
        beside2 = swap(after([behind2], back_pack)[0], 1, "expert", n_e)
        saved_all = [saved, behind1, behind2, behind3, beside, beside1, beside2, beside3]

    c0, c1, c2, c3, dr1, d_proj, d_att, d_logits, gain_terms, d_scores = run(
        functools.partial(backward_kernel, n_t=n_t),
        [((width + 16, tok), bf16)] * 4
        + [
            ((width, tok), f32),
            ((inner, tok), bf16),
            ((model, tok), bf16),
            ((experts, tok), f32),
            ((model, tok), f32),
            ((n_heads, tok, tok), bf16),
        ],
        *back_packs, *token_packs, routes_t, router, gain2, out_weight, qkv_wt, heads, probs,
        fetch=(8, 9, 11),
        scratch=[pltpu.VMEM((model, tok), f32)] * 4,
    )
    height = experts + 8
    if direct:
        last_shape = (inner + width + height * (model // tok), tok)
    else:
        last_shape = out_weight.shape
    small, last = run(
        functools.partial(small_grad_kernel, n_t=n_t, n_buckets=n_buckets, direct=direct),
        [((height, model), f32), (last_shape, bf16)],
        *token_packs, d_logits, gain_terms, gain1_row, gain2, saved, d_proj, d_att,
        d_scores, buckets, qkv_w,
        fetch=(6, 12, 13),
        scratch=[pltpu.VMEM((model, tok), f32), padded],
    )
    if direct:
        lasts = [last] + [step(last, k) for k in (2, 4, 6)]
    if direct:
        (att,) = run(
            join_kernel, [((n_e * width, tok), bf16)], *after(saved_all, last)
        )
        half = n_e // 2
        (part,) = run(
            functools.partial(qkv_grad_kernel, count=half, inner=inner),
            [((inner, model), f32)],
            *lasts, *saved_all[:half],
        )
        lasts = lasts + [swap(v, 1, "expert", n_e) for v in lasts]
        atts = [att, swap(att, 1), swap(att, 2)]
        atts.append(swap(after(atts[2:], lasts[half + 1])[0], 1))
        lasts[half:] = after(lasts[half:], part)
        small, own, q1, q2, q3 = run(
            functools.partial(late_sum_kernel, n_e=n_e, inner=inner),
            [((height, model), f32), ((width, width), f32)]
            + [((width + 16, width), bf16)] * 3,
            *atts, *lasts,
        )
        got = [swap(q, k) for k, q in ((1, q1), (2, q2), (3, q3))]
        c1, c2, c3, part = after([c1, c2, c3, part], own)
        (qkv_grad,) = run(
            functools.partial(qkv_grad_kernel, count=half, inner=inner),
            [((inner, model), f32)],
            *lasts[half:], *saved_all[half:], part,
        )
        out_grad, first, second, router_grad, rel_grad = run(
            functools.partial(out_grad_kernel, n_t=n_t),
            [
                (out_weight.shape, f32),
                ((model,), f32),
                ((model,), f32),
                ((experts, model), f32),
                ((n_heads, n_buckets), f32),
            ],
            own, *got, small,
            scratch=[pltpu.VMEM((n_t, width, width), f32), pltpu.VMEM((1, model), f32)],
        )
    else:
        small, out_grad = lax.psum((small, last.astype(f32)), "expert")
        (qkv_grad,) = run(
            functools.partial(qkv_grad_kernel, count=1, inner=inner),
            [((inner, model), f32)],
            d_proj, saved,
        )
        qkv_grad = lax.psum(qkv_grad, "expert")
        first = lax.psum(small[experts + 1], "tensor")
        second = small[experts]
        router_grad = small[:experts]
        rel_grad = small[experts + 2:experts + 2 + n_heads, :n_buckets]
    got = [swap(c, k) for k, c in ((1, c1), (2, c2), (3, c3))]
    (input_grad,) = run(
        functools.partial(input_grad_kernel, n_t=n_t),
        [((width, tok), f32)],
        c0, *got, dr1, inv1, x, gain1,
        fetch=(6,),
    )
    return (
        output.T,
        input_grad.T,
        first.reshape(model),
        second.reshape(model),
        qkv_grad.reshape(3, width, model).transpose(0, 2, 1),
        out_grad,
        rel_grad.T,
        router_grad.T,
        up_grad,
        down_grad,
    )


def solution(mesh):
    placed = (
        P("expert", "tensor"),
        P(),
        P(),
        P(None, None, "tensor"),
        P("tensor", None),
        P(None, "tensor"),
        P(),
        P("expert", None, "tensor"),
        P("expert", "tensor", None),
        P("expert", None),
        P("expert", None),
        P(),
        P("expert", "tensor"),
    )
    return jax.shard_map(
        functools.partial(per_device, n_t=mesh.shape["tensor"], n_e=mesh.shape["expert"]),
        mesh=mesh,
        in_specs=placed,
        out_specs=(
            P("expert", "tensor"),
            P("expert", "tensor"),
            P(),
            P(),
            P(None, None, "tensor"),
            P("tensor", None),
            P(None, "tensor"),
            P(),
            P("expert", None, "tensor"),
            P("expert", "tensor", None),
        ),
        check_vma=False,
    )
```

```python
import functools
import math

import jax
import jax.numpy as jnp
from jax import lax
from jax.experimental import pallas as pl
from jax.experimental.pallas import tpu as pltpu
from jax.sharding import PartitionSpec as P

epsilon = 1e-06
highest = lax.Precision.HIGHEST
big_negative = -1e30
bf16 = jnp.bfloat16
f32 = jnp.float32
i32 = jnp.int32


def mm(a, b, contract=(1, 0), precision=None):
    return lax.dot_general(
        a,
        b,
        (((contract[0],), (contract[1],)), ((), ())),
        preferred_element_type=f32,
        precision=precision,
    )


def iota(shape, dim):
    return lax.broadcasted_iota(i32, shape, dim)


def split_hi_lo(v):
    hi = v.astype(bf16).astype(f32)
    return hi, v - hi


def row_block(values, rows=16):
    lanes = values[0].shape[1]
    row = iota((rows, lanes), 0)
    block = jnp.zeros((rows, lanes), f32)
    for i, v in enumerate(values):
        block = jnp.where(row == i, v, block)
    return block


def run(body, outs, *args, fetch=(), scratch=(), limit=32):
    n, m, f = len(args), len(outs), len(fetch)
    moved = sum(a.size * a.dtype.itemsize for a in args)
    moved += sum(math.prod(s) * jnp.dtype(d).itemsize for s, d in outs)
    held = [pltpu.VMEM(args[i].shape, args[i].dtype) for i in fetch]
    sems = [pltpu.SemaphoreType.DMA((f,))] if f else []

    def whole(*refs):
        ins, rest = list(refs[:n]), refs[n + m:]
        copies = [
            pltpu.make_async_copy(ins[i], rest[j], rest[f].at[j]) for j, i in enumerate(fetch)
        ]
        for copy in copies:
            copy.start()
        for copy in copies:
            copy.wait()
        for j, i in enumerate(fetch):
            ins[i] = rest[j]
        body(*ins, *refs[n:n + m], *rest[f + len(sems):])

    return pl.pallas_call(
        whole,
        out_shape=[jax.ShapeDtypeStruct(s, d) for s, d in outs],
        in_specs=[
            pl.BlockSpec(memory_space=pltpu.HBM) if i in fetch else pl.BlockSpec()
            for i in range(n)
        ],
        out_specs=[pl.BlockSpec()] * m,
        scratch_shapes=held + sems + list(scratch),
        compiler_params=pltpu.CompilerParams(vmem_limit_bytes=limit * 2**20),
        cost_estimate=pl.CostEstimate(flops=0, bytes_accessed=moved, transcendentals=0),
    )(*args)


def my_place():
    return lax.axis_index("tensor"), lax.axis_index("expert")


def column_of(row, out):
    for c in range(row.shape[1] // 128):
        part = jnp.broadcast_to(row[:, c * 128:(c + 1) * 128], (128, 128))
        part = jnp.where(iota((128, 128), 0) == iota((128, 128), 1), part, 0.0)
        out[c * 128:(c + 1) * 128, :] = jnp.sum(part, axis=1, keepdims=True)


def skew(values, sign):
    n = values.shape[0]
    row = iota(values.shape, 0)
    bit = 1
    while bit < n:
        moved = pltpu.roll(values, bit if sign > 0 else n - bit, 1)
        values = jnp.where((row & bit) != 0, moved, values)
        bit *= 2
    return values


def bucket_hot(buckets, padded, count):
    padded[...] = jnp.full(padded.shape, -1, i32)
    padded[:, 0:buckets.shape[1]] = buckets[...]
    return (padded[...] == iota((count, padded.shape[1]), 0)).astype(f32)


def prepare_kernel(lengths, gain, out_w, table, buckets, gain_col, out_wt, bias, padded):
    tok = bias.shape[1]
    column_of(gain[...], gain_col)
    out_wt[...] = out_w[...].astype(f32).T.astype(bf16)
    key_pos = iota((tok, tok), 0)
    query_pos = iota((tok, tok), 1)
    end0 = lengths[0:1, 0:1]
    end1 = end0 + lengths[0:1, 1:2]
    seg_k = (key_pos >= end0).astype(i32) + (key_pos >= end1).astype(i32)
    seg_q = (query_pos >= end0).astype(i32) + (query_pos >= end1).astype(i32)
    allowed = (seg_k == seg_q) & (key_pos <= query_pos)
    hot = bucket_hot(buckets, padded, table.shape[1])
    per_head = mm(table[...], hot, precision=highest)
    for h in range(table.shape[0]):
        full = skew(jnp.broadcast_to(per_head[h:h + 1], (tok, tok)), 1)
        bias[h] = jnp.where(allowed, full, big_negative)


def route_kernel(
    routes, router, gain, qkv_w, after, dest, gain_col, rw_own, qkv_wt, chunks,
    *, experts, cap, n_t,
):
    tok = routes.shape[1]
    width = rw_own.shape[1]
    rt = routes[...]
    x_of = iota((experts, tok), 0)
    m0 = (rt[0:1] == x_of).astype(f32)
    m1 = (rt[1:2] == x_of).astype(f32)
    earlier = (iota((tok, tok), 0) < iota((tok, tok), 1)).astype(f32).astype(bf16)
    counts = mm((m0 + m1).astype(bf16), earlier)
    rows = [
        rt[i:i + 1].astype(f32) * cap + jnp.sum(m * counts, axis=0, keepdims=True)
        for i, m in enumerate((m0, m1))
    ]
    dest[...] = row_block(rows, 8)
    column_of(gain[...], gain_col)
    wide = router[...].astype(f32)
    for s in range(n_t):
        chunks[s] = wide[:, s * width:(s + 1) * width]
    rw_own[...] = chunks[my_place()[0]].astype(bf16)
    qkv_wt[...] = qkv_w[...].astype(f32).T.astype(bf16)


def chunk(ref, s, width):
    return ref.at[pl.ds(pl.multiple_of(s * width, 64), width)]


def attention_kernel(
    x0, x1, x2, x3, gain, qkv_w, out_wt, bias,
    own, p1, p2, p3, inv1, heads, probs, saved,
    xs, parts, *, n_t,
):
    width, tok = x0.shape
    n_heads = bias.shape[0]
    size = width // n_heads
    model = n_t * width
    r, _ = my_place()
    for k, x in enumerate((x0, x1, x2, x3)):
        chunk(xs, r ^ k, width)[...] = x[...].astype(f32)
    inverse = lax.rsqrt(jnp.sum(xs[...] * xs[...], axis=0, keepdims=True) / model + epsilon)
    inv1[...] = inverse
    saved[0:model] = (xs[...] * inverse * gain[...]).astype(bf16)
    heads[...] = mm(qkv_w[...], saved[0:model]).astype(bf16)
    for h in range(n_heads):
        q, k, v = (heads[j * width + h * size:j * width + (h + 1) * size] for j in range(3))
        scores = mm(k, q, (0, 0)) * (size ** -0.5) + bias[h]
        weights = jnp.exp(scores - jnp.max(scores, axis=0, keepdims=True))
        prob = weights / jnp.sum(weights, axis=0, keepdims=True)
        probs[h] = prob
        here = model + h * size
        saved[here:here + size] = mm(v, prob.astype(bf16)).astype(bf16)
    parts[...] = mm(out_wt[...], saved[model:])
    own[...] = chunk(parts, r, width)[...]
    for k, p in ((1, p1), (2, p2), (3, p3)):
        p[...] = chunk(parts, r ^ k, width)[...].astype(bf16)


def dispatch_kernel(
    own, p1, p2, p3, x, dy, gain, rw_own, routes, dest, *refs
):
    pieces = refs[:-3]
    token_pack, residual, pack = refs[-3:]
    width, tok = x.shape
    experts = rw_own.shape[0]
    r, _ = my_place()
    res = x[...].astype(f32) + own[...] + (
        p1[...].astype(f32) + p2[...].astype(f32) + p3[...].astype(f32)
    )
    residual[...] = res
    scaled = (res * chunk(gain, r, width)[...]).astype(bf16)
    square = jnp.sum(res * res, axis=0, keepdims=True)
    logits = mm(rw_own[...], scaled)
    x_of = iota((experts, tok), 0)
    c0 = jnp.sum(jnp.where(routes[0:1, :] == x_of, logits, 0.0), axis=0, keepdims=True)
    c1 = jnp.sum(jnp.where(routes[1:2, :] == x_of, logits, 0.0), axis=0, keepdims=True)
    stats = row_block(split_hi_lo(square) + split_hi_lo(c0 - c1)).astype(bf16)
    token_pack[0:width] = res.astype(bf16)
    token_pack[width:width + 16] = stats
    token_pack[width + 16:] = dy[...]
    pack[0:width] = scaled
    pack[width:width + 16] = stats
    pack[width + 16:] = dy[...]
    size = pieces[0].shape[0]
    row = iota((size * len(pieces), tok), 0).astype(f32)
    place0 = (row == dest[0:1, :]).astype(f32)
    place1 = (row == dest[1:2, :]).astype(f32)
    both = mm((place0 + place1).astype(bf16), pack[...], (1, 1))
    signed = mm((place0 - place1).astype(bf16), pack[...], (1, 1))
    lane = iota(both.shape, 1)
    full = jnp.where((lane == width + 2) | (lane == width + 3), signed, both)
    for k, piece in enumerate(pieces):
        piece[...] = full[k * size:(k + 1) * size].astype(bf16)


def gelu_pair(a):
    c = 0.7978845608028654
    t = jnp.tanh(c * (a + 0.044715 * a * a * a))
    value = 0.5 * a * (1.0 + t)
    slope = 0.5 * (1.0 + t) + 0.5 * a * (1.0 - t * t) * c * (1.0 + 3 * 0.044715 * a * a)
    return value, slope


def expert_kernel(
    h0, h1, h2, h3, up, down,
    own, across, mate, u, z, de, da,
    hs, gs, chunks, *, n_t,
):
    width = own.shape[1] // 2
    model = n_t * width
    r, _ = my_place()
    packs = (h0, h1, h2, h3)
    for k, h in enumerate(packs):
        s = r ^ k
        hs[s] = h[:, 0:width].astype(f32)
        gs[s] = h[:, width + 16:].astype(f32)
    stats = h0[:, width:width + 16].astype(f32)
    for h in packs[1:]:
        stats += h[:, width:width + 16].astype(f32)
    inverse = lax.rsqrt((stats[:, 0:1] + stats[:, 1:2]) / model + epsilon)
    gate = 1.0 / (1.0 + jnp.exp(-inverse * (stats[:, 2:3] + stats[:, 3:4])))
    for s in range(n_t):
        cols = slice(s * width, (s + 1) * width)
        u[:, cols] = (hs[s] * inverse).astype(bf16)
        de[:, cols] = (gs[s] * gate).astype(bf16)
    value, slope = gelu_pair(mm(u[...], up[0]))
    z[...] = value.astype(bf16)
    da[...] = (mm(de[...], down[0], (1, 1)) * slope).astype(bf16)
    eo = mm(z[...], down[0]).astype(bf16)
    du = mm(da[...], up[0], (1, 1)).astype(bf16)
    for s in range(n_t):
        cols = slice(s * width, (s + 1) * width)
        chunks[s, :, 0:width] = eo[:, cols]
        chunks[s, :, width:] = du[:, cols]
    rows = own.shape[0]
    own[...] = chunks[r]
    across[...] = chunks[r ^ 2]
    mate[0:rows] = chunks[r ^ 1]
    mate[rows:] = chunks[r ^ 3]


def expert_grad_kernel(u, z, de, da, up_grad, down_grad):
    up_grad[0] = mm(u[...], da[...], (0, 0))
    down_grad[0] = mm(z[...], de[...], (0, 0))


def join_kernel(*refs):
    parts, out = refs[:-1], refs[-1]
    height = out.shape[0] // len(parts)
    for j, part in enumerate(parts):
        out[j * height:(j + 1) * height] = part[part.shape[0] - height:]


def pair_sum_kernel(across, got, out):
    rows = across.shape[0]
    out[...] = (across[...].astype(f32) + got[rows:].astype(f32)).astype(bf16)


def expert_sum_kernel(own, got, far, out):
    rows = own.shape[0]
    total = own[...].astype(f32) + got[0:rows].astype(f32) + far[...].astype(f32)
    out[...] = total.astype(bf16)


def total_stats(packs, width):
    total = packs[0][width:width + 16].astype(f32)
    for p in packs[1:]:
        total += p[width:width + 16].astype(f32)
    return total


def gates_of(stats, model):
    inverse = lax.rsqrt((stats[0:1] + stats[1:2]) / model + epsilon)
    delta = inverse * (stats[2:3] + stats[3:4])
    return inverse, 1.0 / (1.0 + jnp.exp(-delta)), 1.0 / (1.0 + jnp.exp(delta))


def combine_kernel(t0, t1, t2, t3, dest, dy, residual, *refs, n_t):
    pieces, (output, pack) = refs[:-2], refs[-2:]
    width, tok = dy.shape
    _, gate0, gate1 = gates_of(total_stats((t0, t1, t2, t3), width), n_t * width)
    back = pieces[0][...]
    row = iota((back.shape[0], tok), 0).astype(f32)
    pick0 = (row == dest[0:1, :]).astype(f32).astype(bf16)
    pick1 = (row == dest[1:2, :]).astype(f32).astype(bf16)
    got0 = mm(back, pick0, (0, 0))
    got1 = mm(back, pick1, (0, 0))
    e0, e1 = got0[0:width], got1[0:width]
    output[...] = (residual[...] + gate0 * e0 + gate1 * e1).astype(bf16)
    dy_own = dy[...].astype(f32)
    dg0 = jnp.sum(dy_own * e0, axis=0, keepdims=True)
    dg1 = jnp.sum(dy_own * e1, axis=0, keepdims=True)
    pack[0:width] = (got0[width:] + got1[width:]).astype(bf16)
    pack[width:] = row_block(split_hi_lo(dg0) + split_hi_lo(dg1)).astype(bf16)


def backward_kernel(
    b0, b1, b2, b3, t0, t1, t2, t3,
    routes, router, gain, out_w, qkv_wt, heads, probs,
    c0, c1, c2, c3, dr1_own, d_proj, d_att, d_logits, gain_terms, d_scores,
    bs, ts, ys, dr, *, n_t,
):
    width = dr1_own.shape[0]
    tok = b0.shape[1]
    experts = router.shape[0]
    n_heads = probs.shape[0]
    size = width // n_heads
    model = n_t * width
    r, _ = my_place()
    packs, tokens = (b0, b1, b2, b3), (t0, t1, t2, t3)
    for k in range(n_t):
        s = r ^ k
        chunk(bs, s, width)[...] = packs[k][0:width].astype(f32)
        chunk(ts, s, width)[...] = tokens[k][0:width].astype(f32)
        chunk(ys, s, width)[...] = tokens[k][width + 16:].astype(f32)
    inverse, gate0, gate1 = gates_of(total_stats(tokens, width), model)
    back = total_stats(packs, width)
    dg0 = back[0:1] + back[1:2]
    dg1 = back[2:3] + back[3:4]
    mean_gate = gate0 * dg0 + gate1 * dg1
    x_of = iota((experts, tok), 0)
    dlog = jnp.where(routes[0:1, :] == x_of, gate0 * (dg0 - mean_gate), 0.0) + jnp.where(
        routes[1:2, :] == x_of, gate1 * (dg1 - mean_gate), 0.0
    )
    d_logits[...] = dlog
    dh2 = bs[...] + mm(router[...].astype(f32), dlog, (0, 0), precision=highest)
    res = ts[...]
    gain_terms[...] = dh2 * res * inverse
    weighted = dh2 * gain[...]
    dot = jnp.sum(weighted * res, axis=0, keepdims=True) * (inverse**3 / model)
    dr[...] = ys[...] + inverse * weighted - res * dot
    d_att[...] = dr[...].astype(bf16)
    dr1_own[...] = chunk(dr, r, width)[...]
    d_o = mm(out_w[...], d_att[...]).astype(bf16)
    scale = size ** -0.5
    for h in range(n_heads):
        q, k, v = (heads[j * width + h * size:j * width + (h + 1) * size] for j in range(3))
        d_oh = d_o[h * size:(h + 1) * size]
        prob = probs[h]
        d_prob = mm(v, d_oh, (0, 0))
        centre = jnp.sum(prob * d_prob, axis=0, keepdims=True)
        ds = (prob * (d_prob - centre)).astype(bf16)
        d_scores[h] = ds
        here = h * size
        d_proj[here:here + size] = (mm(k, ds) * scale).astype(bf16)
        here += width
        d_proj[here:here + size] = (mm(q, ds, (1, 1)) * scale).astype(bf16)
        here += width
        d_proj[here:here + size] = mm(d_oh, prob.astype(bf16), (1, 1)).astype(bf16)
    row_dot = jnp.sum(
        d_proj[...].astype(f32) * heads[...].astype(f32), axis=0, keepdims=True
    )
    stats = row_block(split_hi_lo(row_dot)).astype(bf16)
    dr[...] = mm(qkv_wt[...], d_proj[...])
    for k, c in enumerate((c0, c1, c2, c3)):
        c[0:width] = chunk(dr, r ^ k, width)[...].astype(bf16)
        c[width:] = stats


def small_grad_kernel(
    t0, t1, t2, t3, d_logits, gain_terms, gain1_row, gain2, saved, d_proj, d_att,
    d_scores, buckets, qkv_w, small, last, ts, padded, *, n_t, n_buckets, direct,
):
    packs = (t0, t1, t2, t3)
    width = d_proj.shape[0] // 3
    model = n_t * width
    inner = d_proj.shape[0]
    experts = d_logits.shape[0]
    tok = t0.shape[1]
    r, _ = my_place()
    for k, t in enumerate(packs):
        chunk(ts, r ^ k, width)[...] = t[0:width].astype(f32)
    inverse, _, _ = gates_of(total_stats(packs, width), model)
    normed = (ts[...] * inverse * gain2[...]).astype(bf16).astype(f32)
    small[0:experts] = mm(d_logits[...], normed, (1, 1), precision=highest)
    ones = jnp.ones((8, tok), f32)
    small[experts:] = jnp.zeros((small.shape[0] - experts, model), f32)
    small[experts:experts + 1] = mm(ones, gain_terms[...], (1, 1), precision=highest)[0:1]
    grad = mm(d_proj[...], saved[0:model], (1, 1))
    first = jnp.sum(grad * qkv_w[...].astype(f32), axis=0, keepdims=True)
    small[experts + 1:experts + 2] = first / gain1_row[...]
    hot = bucket_hot(buckets, padded, n_buckets)
    for h in range(d_scores.shape[0]):
        diagonal = jnp.sum(skew(d_scores[h].astype(f32), -1), axis=0, keepdims=True)
        per_bucket = mm(jnp.broadcast_to(diagonal, (8, tok)), hot, (1, 1), precision=highest)
        here = experts + 2 + h
        small[here:here + 1, 0:n_buckets] = per_bucket[0:1]
    if direct:
        last[0:inner] = d_proj[...]
        last[inner:inner + width] = chunk(d_att, r, width)[...]
        height = small.shape[0]
        for c in range(model // tok):
            here = inner + width + c * height
            last[here:here + height] = small[:, c * tok:(c + 1) * tok].astype(bf16)
    else:
        last[...] = mm(saved[model:], d_att[...], (1, 1)).astype(last.dtype)


def late_sum_kernel(o0, o1, o2, o3, *refs, n_e, inner):
    lasts, (small, own, q1, q2, q3) = refs[:n_e], refs[n_e:]
    width = own.shape[0]
    stride, tok = lasts[0].shape
    height, model = small.shape
    total = lasts[0][inner + width:].astype(f32)
    for last in lasts[1:]:
        total += last[inner + width:].astype(f32)
    for c in range(model // tok):
        small[:, c * tok:(c + 1) * tok] = total[c * height:(c + 1) * height]
    first = small[height - 7:height - 6]
    hi, lo = split_hi_lo(first)
    wide = row_block(
        [v[:, s * width:(s + 1) * width] for v in (hi, lo) for s in range(model // width)]
    )
    for o, q in ((o0, own), (o1, q1), (o2, q2), (o3, q3)):
        grad = 0.0
        for j, last in enumerate(lasts):
            grad += mm(o[j * width:(j + 1) * width], last[inner:inner + width], (1, 1))
        q[0:width] = grad.astype(q.dtype)
        if q is not own:
            q[width:] = wide.astype(bf16)


def out_grad_kernel(
    own, q1, q2, q3, small, out, first, second, router, rel, blocks, line, *, n_t
):
    width = own.shape[0]
    experts, buckets = router.shape[0], rel.shape[1]
    r, _ = my_place()
    blocks[r] = own[...]
    for k, q in ((1, q1), (2, q2), (3, q3)):
        blocks[r ^ k] = q[0:width].astype(f32)
    for s in range(n_t):
        cols = slice(s * width, (s + 1) * width)
        out[:, cols] = blocks[s]
        total = small[experts + 1:experts + 2, cols]
        for q in (q1, q2, q3):
            parts = q[width:].astype(f32)
            total += parts[s:s + 1] + parts[n_t + s:n_t + s + 1]
        line[:, cols] = total
    first[...] = line[0]
    second[...] = small[experts]
    router[...] = small[0:experts]
    rel[...] = small[experts + 2:experts + 2 + rel.shape[0], 0:buckets]


def input_grad_kernel(c0, c1, c2, c3, dr1, inv1, x, gain, out, *, n_t):
    width = x.shape[0]
    total = c0[...].astype(f32) + c1[...].astype(f32) + (c2[...].astype(f32) + c3[...].astype(f32))
    row_dot = (total[width:width + 1] + total[width + 1:width + 2]) / (n_t * width)
    inverse = inv1[...]
    weighted = total[0:width] * chunk(gain, my_place()[0], width)[...]
    out[...] = dr1[...] + inverse * weighted - x[...].astype(f32) * (inverse * inverse * row_dot)


def qkv_grad_kernel(*refs, count, inner):
    lasts, saved, rest = refs[:count], refs[count:2 * count], refs[2 * count:]
    out = rest[-1]
    model = out.shape[1]
    total = 0.0 if len(rest) == 1 else rest[0][...]
    for last, h in zip(lasts, saved):
        total += mm(last[0:inner], h[0:model], (1, 1))
    out[...] = total


def per_device(
    tokens,
    first_gain,
    second_gain,
    qkv_weight,
    out_weight,
    rel_table,
    router_weight,
    up_weight,
    down_weight,
    routes,
    lengths,
    bucket_ids,
    cotangent,
    *,
    n_t,
    n_e,
):
    tok, width = tokens.shape
    model = n_t * width
    inner = 3 * width
    experts = router_weight.shape[1]
    cap = 5 * tok // (2 * experts)
    rows = experts * cap
    n_heads = rel_table.shape[1]
    n_buckets = rel_table.shape[0]
    direct = n_e == 8
    padded = pltpu.VMEM((1, tok), i32)

    def swap(v, k, axis="tensor", n=n_t):
        return lax.ppermute(v, axis, [(i, i ^ k) for i in range(n)])

    def around(v):
        return [v] + [swap(v, k) for k in range(1, n_t)]

    def around_large(v):
        far = swap(v, 2)
        return [v, swap(v, 1), far, swap(far, 1)]

    def exchange(v):
        w = v.shape[-1]
        v = v.reshape(n_e, rows // n_e, w)
        v = lax.all_to_all(v, "expert", split_axis=0, concat_axis=0, tiled=True)
        return v.reshape(rows, w)

    def step(v, k):
        return lax.ppermute(v, "expert", [(i, (i + k) % n_e) for i in range(n_e)])

    def after(values, *others):
        return list(lax.optimization_barrier((tuple(values), others))[0])

    x = tokens.T
    dy = cotangent.T
    qkv_w = qkv_weight.transpose(0, 2, 1).reshape(inner, model)
    router = router_weight.T
    table = rel_table.T
    routes_t = routes.T
    gain1_row = first_gain.reshape(1, model)
    gain2_row = second_gain.reshape(1, model)
    buckets = bucket_ids.reshape(1, -1)

    xs = around(x)
    gain1, out_wt, bias = run(
        prepare_kernel,
        [((model, 1), f32), ((model, width), bf16), ((n_heads, tok, tok), f32)],
        lengths, gain1_row, out_weight, table, buckets,
        fetch=(0, 1, 2, 3, 4),
        scratch=[padded],
    )
    own, p1, p2, p3, inv1, heads, probs, saved = run(
        functools.partial(attention_kernel, n_t=n_t),
        [((width, tok), f32)]
        + [((width, tok), bf16)] * 3
        + [
            ((1, tok), f32),
            ((inner, tok), bf16),
            ((n_heads, tok, tok), f32),
            ((model + width, tok), bf16),
        ],
        *xs, gain1, qkv_w, out_wt, bias,
        fetch=(n_t + 1,),
        scratch=[pltpu.VMEM((model, tok), f32), pltpu.VMEM((model, tok), f32)],
    )
    got = [swap(p, k) for k, p in ((1, p1), (2, p2), (3, p3))]
    dest, gain2, rw_own, qkv_wt = run(
        functools.partial(route_kernel, experts=experts, cap=cap, n_t=n_t),
        [
            ((8, tok), f32),
            ((model, 1), f32),
            ((experts, width), bf16),
            ((model, inner), bf16),
        ],
        routes_t, router, gain2_row, qkv_w, inv1,
        fetch=(0, 1, 2, 3),
        scratch=[pltpu.VMEM((n_t, experts, width), f32)],
    )
    send_rows, token_pack, residual = run(
        dispatch_kernel,
        [
            ((rows, 2 * width + 16), bf16),
            ((2 * width + 16, tok), bf16),
            ((width, tok), f32),
        ],
        own, *got, x, dy, gain2, rw_own, routes_t, dest,
        fetch=(4, 5, 8),
        scratch=[pltpu.VMEM((2 * width + 16, tok), bf16)],
    )
    in_rows = exchange(send_rows)
    if direct:
        (early,) = after([saved], in_rows)
        behind1, beside = step(early, 2), swap(early, 1, "expert", n_e)
        (far,) = after([swap(in_rows, 2)], behind1, beside)
        in_rows = [in_rows, swap(in_rows, 1), far, swap(far, 1)]
    else:
        in_rows = around_large(in_rows)

    own, across, mate, u, z, de, da = run(
        functools.partial(expert_kernel, n_t=n_t),
        [((rows, 2 * width), bf16)] * 2
        + [((2 * rows, 2 * width), bf16)]
        + [((rows, model), bf16)] * 4,
        *in_rows, up_weight, down_weight,
        fetch=(4, 5),
        scratch=[
            pltpu.VMEM((n_t, rows, width), f32),
            pltpu.VMEM((n_t, rows, width), f32),
            pltpu.VMEM((n_t, rows, 2 * width), bf16),
        ],
    )
    got = swap(mate, 1)
    if direct:
        early, behind1 = after([early, behind1], mate)
        behind2, behind3 = step(behind1, 2), step(early, 6)
        beside1 = swap(behind1, 1, "expert", n_e)
    (across,) = run(pair_sum_kernel, [((rows, 2 * width), bf16)], across, got)
    far = swap(across, 2)
    up_grad, down_grad = run(
        expert_grad_kernel,
        [(up_weight.shape, f32), (down_weight.shape, f32)],
        *after([u, z, de, da], across),
    )
    token_packs = around(after([token_pack], across)[0])
    if direct:
        (far,) = after([far], behind2, behind3, beside1)
    (far,) = after([far], up_grad, *token_packs[1:])
    (summed,) = run(expert_sum_kernel, [((rows, 2 * width), bf16)], own, got, far)
    back = exchange(summed)
    output, back_pack = run(
        functools.partial(combine_kernel, n_t=n_t),
        [((width, tok), bf16), ((width + 16, tok), bf16)],
        *token_packs, dest, dy, residual, back,
        fetch=(5,),
    )
    back_packs = around(back_pack)
    if direct:
        beside2, beside3 = (
            swap(v, 1, "expert", n_e) for v in after([behind2, behind3], back_pack)
        )
        saved_all = [saved, behind1, behind2, behind3, beside, beside1, beside2, beside3]

    c0, c1, c2, c3, dr1, d_proj, d_att, d_logits, gain_terms, d_scores = run(
        functools.partial(backward_kernel, n_t=n_t),
        [((width + 16, tok), bf16)] * 4
        + [
            ((width, tok), f32),
            ((inner, tok), bf16),
            ((model, tok), bf16),
            ((experts, tok), f32),
            ((model, tok), f32),
            ((n_heads, tok, tok), bf16),
        ],
        *back_packs, *token_packs, routes_t, router, gain2, out_weight, qkv_wt, heads, probs,
        fetch=(8, 9, 11),
        scratch=[pltpu.VMEM((model, tok), f32)] * 4,
    )
    height = experts + 8
    if direct:
        last_shape = (inner + width + height * (model // tok), tok)
    else:
        last_shape = out_weight.shape
    small, last = run(
        functools.partial(small_grad_kernel, n_t=n_t, n_buckets=n_buckets, direct=direct),
        [((height, model), f32), (last_shape, bf16)],
        *token_packs, d_logits, gain_terms, gain1_row, gain2, saved, d_proj, d_att,
        d_scores, buckets, qkv_w,
        fetch=(6, 12, 13),
        scratch=[pltpu.VMEM((model, tok), f32), padded],
    )
    if direct:
        lasts = [last, step(last, 2)]
        lasts += [step(lasts[1], 2), step(last, 6)]
        across1 = swap(lasts[1], 1, "expert", n_e)
        c1, c2, c3 = after([c1, c2, c3], across1)
    got = [swap(c, k) for k, c in ((1, c1), (2, c2), (3, c3))]
    (input_grad,) = run(
        functools.partial(input_grad_kernel, n_t=n_t),
        [((width, tok), f32)],
        c0, *got, dr1, inv1, x, gain1,
        fetch=(6,),
    )
    if direct:
        (att,) = run(
            join_kernel, [((n_e * width, tok), bf16)], *after(saved_all, lasts[1])
        )
        half = n_e // 2
        (part,) = run(
            functools.partial(qkv_grad_kernel, count=half, inner=inner),
            [((inner, model), f32)],
            *lasts, *saved_all[:half],
        )
        lasts[2:] = after(lasts[2:], input_grad)
        lasts += [
            across1 if j == 1 else swap(v, 1, "expert", n_e) for j, v in enumerate(lasts)
        ]
        atts = [att, swap(att, 1), swap(att, 2)]
        atts.append(swap(after(atts[2:], lasts[half + 1])[0], 1))
        lasts[half:] = after(lasts[half:], part)
        small, own, q1, q2, q3 = run(
            functools.partial(late_sum_kernel, n_e=n_e, inner=inner),
            [((height, model), f32), ((width, width), f32)]
            + [((width + 16, width), bf16)] * 3,
            *atts, *lasts,
        )
        got = [swap(q, k) for k, q in ((1, q1), (2, q2), (3, q3))]
        (part,) = after([part], own)
        (qkv_grad,) = run(
            functools.partial(qkv_grad_kernel, count=half, inner=inner),
            [((inner, model), f32)],
            *lasts[half:], *saved_all[half:], part,
        )
        out_grad, first, second, router_grad, rel_grad = run(
            functools.partial(out_grad_kernel, n_t=n_t),
            [
                (out_weight.shape, f32),
                ((model,), f32),
                ((model,), f32),
                ((experts, model), f32),
                ((n_heads, n_buckets), f32),
            ],
            own, *got, small,
            scratch=[pltpu.VMEM((n_t, width, width), f32), pltpu.VMEM((1, model), f32)],
        )
    else:
        small, out_grad = lax.psum((small, last.astype(f32)), "expert")
        (qkv_grad,) = run(
            functools.partial(qkv_grad_kernel, count=1, inner=inner),
            [((inner, model), f32)],
            d_proj, saved,
        )
        qkv_grad = lax.psum(qkv_grad, "expert")
        first = lax.psum(small[experts + 1], "tensor")
        second = small[experts]
        router_grad = small[:experts]
        rel_grad = small[experts + 2:experts + 2 + n_heads, :n_buckets]
    return (
        output.T,
        input_grad.T,
        first.reshape(model),
        second.reshape(model),
        qkv_grad.reshape(3, width, model).transpose(0, 2, 1),
        out_grad,
        rel_grad.T,
        router_grad.T,
        up_grad,
        down_grad,
    )


def solution(mesh):
    placed = (
        P("expert", "tensor"),
        P(),
        P(),
        P(None, None, "tensor"),
        P("tensor", None),
        P(None, "tensor"),
        P(),
        P("expert", None, "tensor"),
        P("expert", "tensor", None),
        P("expert", None),
        P("expert", None),
        P(),
        P("expert", "tensor"),
    )
    return jax.shard_map(
        functools.partial(per_device, n_t=mesh.shape["tensor"], n_e=mesh.shape["expert"]),
        mesh=mesh,
        in_specs=placed,
        out_specs=(
            P("expert", "tensor"),
            P("expert", "tensor"),
            P(),
            P(),
            P(None, None, "tensor"),
            P("tensor", None),
            P(None, "tensor"),
            P(),
            P("expert", None, "tensor"),
            P("expert", "tensor", None),
        ),
        check_vma=False,
    )
```

```python
import functools
import math

import jax
import jax.numpy as jnp
from jax import lax
from jax.experimental import pallas as pl
from jax.experimental.pallas import tpu as pltpu
from jax.sharding import PartitionSpec as P

epsilon = 1e-06
highest = lax.Precision.HIGHEST
big_negative = -1e30
bf16 = jnp.bfloat16
f32 = jnp.float32
i32 = jnp.int32


def mm(a, b, contract=(1, 0), precision=None):
    return lax.dot_general(
        a,
        b,
        (((contract[0],), (contract[1],)), ((), ())),
        preferred_element_type=f32,
        precision=precision,
    )


def iota(shape, dim):
    return lax.broadcasted_iota(i32, shape, dim)


def split_hi_lo(v):
    hi = v.astype(bf16).astype(f32)
    return hi, v - hi


def row_block(values, rows=16):
    lanes = values[0].shape[1]
    row = iota((rows, lanes), 0)
    block = jnp.zeros((rows, lanes), f32)
    for i, v in enumerate(values):
        block = jnp.where(row == i, v, block)
    return block


def run(body, outs, *args, fetch=(), scratch=(), limit=32):
    n, m, f = len(args), len(outs), len(fetch)
    moved = sum(a.size * a.dtype.itemsize for a in args)
    moved += sum(math.prod(s) * jnp.dtype(d).itemsize for s, d in outs)
    held = [pltpu.VMEM(args[i].shape, args[i].dtype) for i in fetch]
    sems = [pltpu.SemaphoreType.DMA((f,))] if f else []

    def whole(*refs):
        ins, rest = list(refs[:n]), refs[n + m:]
        copies = [
            pltpu.make_async_copy(ins[i], rest[j], rest[f].at[j]) for j, i in enumerate(fetch)
        ]
        for copy in copies:
            copy.start()
        for copy in copies:
            copy.wait()
        for j, i in enumerate(fetch):
            ins[i] = rest[j]
        body(*ins, *refs[n:n + m], *rest[f + len(sems):])

    return pl.pallas_call(
        whole,
        out_shape=[jax.ShapeDtypeStruct(s, d) for s, d in outs],
        in_specs=[
            pl.BlockSpec(memory_space=pltpu.HBM) if i in fetch else pl.BlockSpec()
            for i in range(n)
        ],
        out_specs=[pl.BlockSpec()] * m,
        scratch_shapes=held + sems + list(scratch),
        compiler_params=pltpu.CompilerParams(vmem_limit_bytes=limit * 2**20),
        cost_estimate=pl.CostEstimate(flops=0, bytes_accessed=moved, transcendentals=0),
    )(*args)


def my_place():
    return lax.axis_index("tensor"), lax.axis_index("expert")


def column_of(row, out):
    for c in range(row.shape[1] // 128):
        part = jnp.broadcast_to(row[:, c * 128:(c + 1) * 128], (128, 128))
        part = jnp.where(iota((128, 128), 0) == iota((128, 128), 1), part, 0.0)
        out[c * 128:(c + 1) * 128, :] = jnp.sum(part, axis=1, keepdims=True)


def skew(values, sign):
    n = values.shape[0]
    row = iota(values.shape, 0)
    bit = 1
    while bit < n:
        moved = pltpu.roll(values, bit if sign > 0 else n - bit, 1)
        values = jnp.where((row & bit) != 0, moved, values)
        bit *= 2
    return values


def bucket_hot(buckets, padded, count):
    padded[...] = jnp.full(padded.shape, -1, i32)
    padded[:, 0:buckets.shape[1]] = buckets[...]
    return (padded[...] == iota((count, padded.shape[1]), 0)).astype(f32)


def prepare_kernel(lengths, gain, out_w, table, buckets, gain_col, out_wt, bias, padded):
    tok = bias.shape[1]
    column_of(gain[...], gain_col)
    out_wt[...] = out_w[...].astype(f32).T.astype(bf16)
    key_pos = iota((tok, tok), 0)
    query_pos = iota((tok, tok), 1)
    end0 = lengths[0:1, 0:1]
    end1 = end0 + lengths[0:1, 1:2]
    seg_k = (key_pos >= end0).astype(i32) + (key_pos >= end1).astype(i32)
    seg_q = (query_pos >= end0).astype(i32) + (query_pos >= end1).astype(i32)
    allowed = (seg_k == seg_q) & (key_pos <= query_pos)
    hot = bucket_hot(buckets, padded, table.shape[1])
    per_head = mm(table[...], hot, precision=highest)
    for h in range(table.shape[0]):
        full = skew(jnp.broadcast_to(per_head[h:h + 1], (tok, tok)), 1)
        bias[h] = jnp.where(allowed, full, big_negative)


def route_kernel(
    routes, router, gain, qkv_w, after, dest, gain_col, rw_own, qkv_wt, chunks,
    *, experts, cap, n_t,
):
    tok = routes.shape[1]
    width = rw_own.shape[1]
    rt = routes[...]
    x_of = iota((experts, tok), 0)
    m0 = (rt[0:1] == x_of).astype(f32)
    m1 = (rt[1:2] == x_of).astype(f32)
    earlier = (iota((tok, tok), 0) < iota((tok, tok), 1)).astype(f32).astype(bf16)
    counts = mm((m0 + m1).astype(bf16), earlier)
    rows = [
        rt[i:i + 1].astype(f32) * cap + jnp.sum(m * counts, axis=0, keepdims=True)
        for i, m in enumerate((m0, m1))
    ]
    dest[...] = row_block(rows, 8)
    column_of(gain[...], gain_col)
    wide = router[...].astype(f32)
    for s in range(n_t):
        chunks[s] = wide[:, s * width:(s + 1) * width]
    rw_own[...] = chunks[my_place()[0]].astype(bf16)
    qkv_wt[...] = qkv_w[...].astype(f32).T.astype(bf16)


def chunk(ref, s, width):
    return ref.at[pl.ds(pl.multiple_of(s * width, 64), width)]


def attention_kernel(
    x0, x1, x2, x3, gain, qkv_w, out_wt, bias,
    own, p1, p2, p3, inv1, heads, probs, saved,
    xs, parts, *, n_t,
):
    width, tok = x0.shape
    n_heads = bias.shape[0]
    size = width // n_heads
    model = n_t * width
    r, _ = my_place()
    for k, x in enumerate((x0, x1, x2, x3)):
        chunk(xs, r ^ k, width)[...] = x[...].astype(f32)
    inverse = lax.rsqrt(jnp.sum(xs[...] * xs[...], axis=0, keepdims=True) / model + epsilon)
    inv1[...] = inverse
    saved[0:model] = (xs[...] * inverse * gain[...]).astype(bf16)
    heads[...] = mm(qkv_w[...], saved[0:model]).astype(bf16)
    for h in range(n_heads):
        q, k, v = (heads[j * width + h * size:j * width + (h + 1) * size] for j in range(3))
        scores = mm(k, q, (0, 0)) * (size ** -0.5) + bias[h]
        weights = jnp.exp(scores - jnp.max(scores, axis=0, keepdims=True))
        prob = weights / jnp.sum(weights, axis=0, keepdims=True)
        probs[h] = prob
        here = model + h * size
        saved[here:here + size] = mm(v, prob.astype(bf16)).astype(bf16)
    parts[...] = mm(out_wt[...], saved[model:])
    own[...] = chunk(parts, r, width)[...]
    for k, p in ((1, p1), (2, p2), (3, p3)):
        p[...] = chunk(parts, r ^ k, width)[...].astype(bf16)


def dispatch_kernel(
    own, p1, p2, p3, x, dy, gain, rw_own, routes, dest, *refs
):
    pieces = refs[:-3]
    token_pack, residual, pack = refs[-3:]
    width, tok = x.shape
    experts = rw_own.shape[0]
    r, _ = my_place()
    res = x[...].astype(f32) + own[...] + (
        p1[...].astype(f32) + p2[...].astype(f32) + p3[...].astype(f32)
    )
    residual[...] = res
    scaled = (res * chunk(gain, r, width)[...]).astype(bf16)
    square = jnp.sum(res * res, axis=0, keepdims=True)
    logits = mm(rw_own[...], scaled)
    x_of = iota((experts, tok), 0)
    c0 = jnp.sum(jnp.where(routes[0:1, :] == x_of, logits, 0.0), axis=0, keepdims=True)
    c1 = jnp.sum(jnp.where(routes[1:2, :] == x_of, logits, 0.0), axis=0, keepdims=True)
    stats = row_block(split_hi_lo(square) + split_hi_lo(c0 - c1)).astype(bf16)
    token_pack[0:width] = res.astype(bf16)
    token_pack[width:width + 16] = stats
    token_pack[width + 16:] = dy[...]
    pack[0:width] = scaled
    pack[width:width + 16] = stats
    pack[width + 16:] = dy[...]
    size = pieces[0].shape[0]
    row = iota((size * len(pieces), tok), 0).astype(f32)
    place0 = (row == dest[0:1, :]).astype(f32)
    place1 = (row == dest[1:2, :]).astype(f32)
    both = mm((place0 + place1).astype(bf16), pack[...], (1, 1))
    signed = mm((place0 - place1).astype(bf16), pack[...], (1, 1))
    lane = iota(both.shape, 1)
    full = jnp.where((lane == width + 2) | (lane == width + 3), signed, both)
    for k, piece in enumerate(pieces):
        piece[...] = full[k * size:(k + 1) * size].astype(bf16)


def gelu_pair(a):
    c = 0.7978845608028654
    t = jnp.tanh(c * (a + 0.044715 * a * a * a))
    value = 0.5 * a * (1.0 + t)
    slope = 0.5 * (1.0 + t) + 0.5 * a * (1.0 - t * t) * c * (1.0 + 3 * 0.044715 * a * a)
    return value, slope


def expert_kernel(
    h0, h1, h2, h3, up, down,
    own, across, mate, u, z, de, da,
    hs, gs, chunks, *, n_t,
):
    width = own.shape[1] // 2
    model = n_t * width
    r, _ = my_place()
    packs = (h0, h1, h2, h3)
    for k, h in enumerate(packs):
        s = r ^ k
        hs[s] = h[:, 0:width].astype(f32)
        gs[s] = h[:, width + 16:].astype(f32)
    stats = h0[:, width:width + 16].astype(f32)
    for h in packs[1:]:
        stats += h[:, width:width + 16].astype(f32)
    inverse = lax.rsqrt((stats[:, 0:1] + stats[:, 1:2]) / model + epsilon)
    gate = 1.0 / (1.0 + jnp.exp(-inverse * (stats[:, 2:3] + stats[:, 3:4])))
    for s in range(n_t):
        cols = slice(s * width, (s + 1) * width)
        u[:, cols] = (hs[s] * inverse).astype(bf16)
        de[:, cols] = (gs[s] * gate).astype(bf16)
    value, slope = gelu_pair(mm(u[...], up[0]))
    z[...] = value.astype(bf16)
    da[...] = (mm(de[...], down[0], (1, 1)) * slope).astype(bf16)
    eo = mm(z[...], down[0]).astype(bf16)
    du = mm(da[...], up[0], (1, 1)).astype(bf16)
    for s in range(n_t):
        cols = slice(s * width, (s + 1) * width)
        chunks[s, :, 0:width] = eo[:, cols]
        chunks[s, :, width:] = du[:, cols]
    rows = own.shape[0]
    own[...] = chunks[r]
    across[...] = chunks[r ^ 2]
    mate[0:rows] = chunks[r ^ 1]
    mate[rows:] = chunks[r ^ 3]


def expert_grad_kernel(u, z, de, da, up_grad, down_grad):
    up_grad[0] = mm(u[...], da[...], (0, 0))
    down_grad[0] = mm(z[...], de[...], (0, 0))


def join_kernel(*refs):
    parts, out = refs[:-1], refs[-1]
    height = out.shape[0] // len(parts)
    for j, part in enumerate(parts):
        out[j * height:(j + 1) * height] = part[part.shape[0] - height:]


def pair_sum_kernel(across, got, out):
    rows = across.shape[0]
    out[...] = (across[...].astype(f32) + got[rows:].astype(f32)).astype(bf16)


def expert_sum_kernel(own, got, far, out):
    rows = own.shape[0]
    total = own[...].astype(f32) + got[0:rows].astype(f32) + far[...].astype(f32)
    out[...] = total.astype(bf16)


def total_stats(packs, width):
    total = packs[0][width:width + 16].astype(f32)
    for p in packs[1:]:
        total += p[width:width + 16].astype(f32)
    return total


def gates_of(stats, model):
    inverse = lax.rsqrt((stats[0:1] + stats[1:2]) / model + epsilon)
    delta = inverse * (stats[2:3] + stats[3:4])
    return inverse, 1.0 / (1.0 + jnp.exp(-delta)), 1.0 / (1.0 + jnp.exp(delta))


def combine_kernel(t0, t1, t2, t3, dest, dy, residual, *refs, n_t):
    pieces, (output, pack) = refs[:-2], refs[-2:]
    width, tok = dy.shape
    _, gate0, gate1 = gates_of(total_stats((t0, t1, t2, t3), width), n_t * width)
    back = pieces[0][...]
    row = iota((back.shape[0], tok), 0).astype(f32)
    pick0 = (row == dest[0:1, :]).astype(f32).astype(bf16)
    pick1 = (row == dest[1:2, :]).astype(f32).astype(bf16)
    got0 = mm(back, pick0, (0, 0))
    got1 = mm(back, pick1, (0, 0))
    e0, e1 = got0[0:width], got1[0:width]
    output[...] = (residual[...] + gate0 * e0 + gate1 * e1).astype(bf16)
    dy_own = dy[...].astype(f32)
    dg0 = jnp.sum(dy_own * e0, axis=0, keepdims=True)
    dg1 = jnp.sum(dy_own * e1, axis=0, keepdims=True)
    pack[0:width] = (got0[width:] + got1[width:]).astype(bf16)
    pack[width:] = row_block(split_hi_lo(dg0) + split_hi_lo(dg1)).astype(bf16)


def backward_kernel(
    b0, b1, b2, b3, t0, t1, t2, t3,
    routes, router, gain, out_w, qkv_wt, heads, probs,
    c0, c1, c2, c3, dr1_own, d_proj, d_att, d_logits, gain_terms, d_scores,
    bs, ts, ys, dr, *, n_t,
):
    width = dr1_own.shape[0]
    tok = b0.shape[1]
    experts = router.shape[0]
    n_heads = probs.shape[0]
    size = width // n_heads
    model = n_t * width
    r, _ = my_place()
    packs, tokens = (b0, b1, b2, b3), (t0, t1, t2, t3)
    for k in range(n_t):
        s = r ^ k
        chunk(bs, s, width)[...] = packs[k][0:width].astype(f32)
        chunk(ts, s, width)[...] = tokens[k][0:width].astype(f32)
        chunk(ys, s, width)[...] = tokens[k][width + 16:].astype(f32)
    inverse, gate0, gate1 = gates_of(total_stats(tokens, width), model)
    back = total_stats(packs, width)
    dg0 = back[0:1] + back[1:2]
    dg1 = back[2:3] + back[3:4]
    mean_gate = gate0 * dg0 + gate1 * dg1
    x_of = iota((experts, tok), 0)
    dlog = jnp.where(routes[0:1, :] == x_of, gate0 * (dg0 - mean_gate), 0.0) + jnp.where(
        routes[1:2, :] == x_of, gate1 * (dg1 - mean_gate), 0.0
    )
    d_logits[...] = dlog
    dh2 = bs[...] + mm(router[...].astype(f32), dlog, (0, 0), precision=highest)
    res = ts[...]
    gain_terms[...] = dh2 * res * inverse
    weighted = dh2 * gain[...]
    dot = jnp.sum(weighted * res, axis=0, keepdims=True) * (inverse**3 / model)
    dr[...] = ys[...] + inverse * weighted - res * dot
    d_att[...] = dr[...].astype(bf16)
    dr1_own[...] = chunk(dr, r, width)[...]
    d_o = mm(out_w[...], d_att[...]).astype(bf16)
    scale = size ** -0.5
    for h in range(n_heads):
        q, k, v = (heads[j * width + h * size:j * width + (h + 1) * size] for j in range(3))
        d_oh = d_o[h * size:(h + 1) * size]
        prob = probs[h]
        d_prob = mm(v, d_oh, (0, 0))
        centre = jnp.sum(prob * d_prob, axis=0, keepdims=True)
        ds = (prob * (d_prob - centre)).astype(bf16)
        d_scores[h] = ds
        here = h * size
        d_proj[here:here + size] = (mm(k, ds) * scale).astype(bf16)
        here += width
        d_proj[here:here + size] = (mm(q, ds, (1, 1)) * scale).astype(bf16)
        here += width
        d_proj[here:here + size] = mm(d_oh, prob.astype(bf16), (1, 1)).astype(bf16)
    row_dot = jnp.sum(
        d_proj[...].astype(f32) * heads[...].astype(f32), axis=0, keepdims=True
    )
    stats = row_block(split_hi_lo(row_dot)).astype(bf16)
    dr[...] = mm(qkv_wt[...], d_proj[...])
    for k, c in enumerate((c0, c1, c2, c3)):
        c[0:width] = chunk(dr, r ^ k, width)[...].astype(bf16)
        c[width:] = stats


def small_grad_kernel(
    t0, t1, t2, t3, d_logits, gain_terms, gain1_row, gain2, saved, d_proj, d_att,
    d_scores, buckets, qkv_w, small, last, ts, padded, *, n_t, n_buckets, direct,
):
    packs = (t0, t1, t2, t3)
    width = d_proj.shape[0] // 3
    model = n_t * width
    inner = d_proj.shape[0]
    experts = d_logits.shape[0]
    tok = t0.shape[1]
    r, _ = my_place()
    for k, t in enumerate(packs):
        chunk(ts, r ^ k, width)[...] = t[0:width].astype(f32)
    inverse, _, _ = gates_of(total_stats(packs, width), model)
    normed = (ts[...] * inverse * gain2[...]).astype(bf16).astype(f32)
    small[0:experts] = mm(d_logits[...], normed, (1, 1), precision=highest)
    ones = jnp.ones((8, tok), f32)
    small[experts:] = jnp.zeros((small.shape[0] - experts, model), f32)
    small[experts:experts + 1] = mm(ones, gain_terms[...], (1, 1), precision=highest)[0:1]
    grad = mm(d_proj[...], saved[0:model], (1, 1))
    first = jnp.sum(grad * qkv_w[...].astype(f32), axis=0, keepdims=True)
    small[experts + 1:experts + 2] = first / gain1_row[...]
    hot = bucket_hot(buckets, padded, n_buckets)
    for h in range(d_scores.shape[0]):
        diagonal = jnp.sum(skew(d_scores[h].astype(f32), -1), axis=0, keepdims=True)
        per_bucket = mm(jnp.broadcast_to(diagonal, (8, tok)), hot, (1, 1), precision=highest)
        here = experts + 2 + h
        small[here:here + 1, 0:n_buckets] = per_bucket[0:1]
    if direct:
        last[0:inner] = d_proj[...]
        last[inner:inner + width] = chunk(d_att, r, width)[...]
        height = small.shape[0]
        for c in range(model // tok):
            here = inner + width + c * height
            last[here:here + height] = small[:, c * tok:(c + 1) * tok].astype(bf16)
    else:
        last[...] = mm(saved[model:], d_att[...], (1, 1)).astype(last.dtype)


def late_sum_kernel(o0, o1, o2, o3, *refs, n_e, inner):
    lasts, (small, own, q1, q2, q3) = refs[:n_e], refs[n_e:]
    width = own.shape[0]
    stride, tok = lasts[0].shape
    height, model = small.shape
    total = lasts[0][inner + width:].astype(f32)
    for last in lasts[1:]:
        total += last[inner + width:].astype(f32)
    for c in range(model // tok):
        small[:, c * tok:(c + 1) * tok] = total[c * height:(c + 1) * height]
    first = small[height - 7:height - 6]
    hi, lo = split_hi_lo(first)
    wide = row_block(
        [v[:, s * width:(s + 1) * width] for v in (hi, lo) for s in range(model // width)]
    )
    for o, q in ((o0, own), (o1, q1), (o2, q2), (o3, q3)):
        grad = 0.0
        for j, last in enumerate(lasts):
            grad += mm(o[j * width:(j + 1) * width], last[inner:inner + width], (1, 1))
        q[0:width] = grad.astype(q.dtype)
        if q is not own:
            q[width:] = wide.astype(bf16)


def out_grad_kernel(
    own, q1, q2, q3, small, out, first, second, router, rel, blocks, line, *, n_t
):
    width = own.shape[0]
    experts, buckets = router.shape[0], rel.shape[1]
    r, _ = my_place()
    blocks[r] = own[...]
    for k, q in ((1, q1), (2, q2), (3, q3)):
        blocks[r ^ k] = q[0:width].astype(f32)
    for s in range(n_t):
        cols = slice(s * width, (s + 1) * width)
        out[:, cols] = blocks[s]
        total = small[experts + 1:experts + 2, cols]
        for q in (q1, q2, q3):
            parts = q[width:].astype(f32)
            total += parts[s:s + 1] + parts[n_t + s:n_t + s + 1]
        line[:, cols] = total
    first[...] = line[0]
    second[...] = small[experts]
    router[...] = small[0:experts]
    rel[...] = small[experts + 2:experts + 2 + rel.shape[0], 0:buckets]


def input_grad_kernel(c0, c1, c2, c3, dr1, inv1, x, gain, out, *, n_t):
    width = x.shape[0]
    total = c0[...].astype(f32) + c1[...].astype(f32) + (c2[...].astype(f32) + c3[...].astype(f32))
    row_dot = (total[width:width + 1] + total[width + 1:width + 2]) / (n_t * width)
    inverse = inv1[...]
    weighted = total[0:width] * chunk(gain, my_place()[0], width)[...]
    out[...] = dr1[...] + inverse * weighted - x[...].astype(f32) * (inverse * inverse * row_dot)


def qkv_grad_kernel(*refs, count, inner):
    lasts, saved, rest = refs[:count], refs[count:2 * count], refs[2 * count:]
    out = rest[-1]
    model = out.shape[1]
    total = 0.0 if len(rest) == 1 else rest[0][...]
    for last, h in zip(lasts, saved):
        total += mm(last[0:inner], h[0:model], (1, 1))
    out[...] = total


def per_device(
    tokens,
    first_gain,
    second_gain,
    qkv_weight,
    out_weight,
    rel_table,
    router_weight,
    up_weight,
    down_weight,
    routes,
    lengths,
    bucket_ids,
    cotangent,
    *,
    n_t,
    n_e,
):
    tok, width = tokens.shape
    model = n_t * width
    inner = 3 * width
    experts = router_weight.shape[1]
    cap = 5 * tok // (2 * experts)
    rows = experts * cap
    n_heads = rel_table.shape[1]
    n_buckets = rel_table.shape[0]
    direct = n_e == 8
    padded = pltpu.VMEM((1, tok), i32)

    def swap(v, k, axis="tensor", n=n_t):
        return lax.ppermute(v, axis, [(i, i ^ k) for i in range(n)])

    def around(v):
        return [v] + [swap(v, k) for k in range(1, n_t)]

    def around_large(v):
        far = swap(v, 2)
        return [v, swap(v, 1), far, swap(far, 1)]

    def exchange(v):
        w = v.shape[-1]
        v = v.reshape(n_e, rows // n_e, w)
        v = lax.all_to_all(v, "expert", split_axis=0, concat_axis=0, tiled=True)
        return v.reshape(rows, w)

    def step(v, k):
        return lax.ppermute(v, "expert", [(i, (i + k) % n_e) for i in range(n_e)])

    def after(values, *others):
        return list(lax.optimization_barrier((tuple(values), others))[0])

    x = tokens.T
    dy = cotangent.T
    qkv_w = qkv_weight.transpose(0, 2, 1).reshape(inner, model)
    router = router_weight.T
    table = rel_table.T
    routes_t = routes.T
    gain1_row = first_gain.reshape(1, model)
    gain2_row = second_gain.reshape(1, model)
    buckets = bucket_ids.reshape(1, -1)

    xs = around(x)
    gain1, out_wt, bias = run(
        prepare_kernel,
        [((model, 1), f32), ((model, width), bf16), ((n_heads, tok, tok), f32)],
        lengths, gain1_row, out_weight, table, buckets,
        fetch=(0, 1, 2, 3, 4),
        scratch=[padded],
    )
    own, p1, p2, p3, inv1, heads, probs, saved = run(
        functools.partial(attention_kernel, n_t=n_t),
        [((width, tok), f32)]
        + [((width, tok), bf16)] * 3
        + [
            ((1, tok), f32),
            ((inner, tok), bf16),
            ((n_heads, tok, tok), f32),
            ((model + width, tok), bf16),
        ],
        *xs, gain1, qkv_w, out_wt, bias,
        fetch=(n_t + 1,),
        scratch=[pltpu.VMEM((model, tok), f32), pltpu.VMEM((model, tok), f32)],
    )
    got = [swap(p, k) for k, p in ((1, p1), (2, p2), (3, p3))]
    dest, gain2, rw_own, qkv_wt = run(
        functools.partial(route_kernel, experts=experts, cap=cap, n_t=n_t),
        [
            ((8, tok), f32),
            ((model, 1), f32),
            ((experts, width), bf16),
            ((model, inner), bf16),
        ],
        routes_t, router, gain2_row, qkv_w, inv1,
        fetch=(0, 1, 2, 3),
        scratch=[pltpu.VMEM((n_t, experts, width), f32)],
    )
    send_rows, token_pack, residual = run(
        dispatch_kernel,
        [
            ((rows, 2 * width + 16), bf16),
            ((2 * width + 16, tok), bf16),
            ((width, tok), f32),
        ],
        own, *got, x, dy, gain2, rw_own, routes_t, dest,
        fetch=(4, 5, 8),
        scratch=[pltpu.VMEM((2 * width + 16, tok), bf16)],
    )
    in_rows = exchange(send_rows)
    if direct:
        (early,) = after([saved], in_rows)
        behind1, beside = step(early, 2), swap(early, 1, "expert", n_e)
        (far,) = after([swap(in_rows, 2)], behind1, beside)
        in_rows = [in_rows, swap(in_rows, 1), far, swap(far, 1)]
    else:
        in_rows = around_large(in_rows)

    own, across, mate, u, z, de, da = run(
        functools.partial(expert_kernel, n_t=n_t),
        [((rows, 2 * width), bf16)] * 2
        + [((2 * rows, 2 * width), bf16)]
        + [((rows, model), bf16)] * 4,
        *in_rows, up_weight, down_weight,
        fetch=(4, 5),
        scratch=[
            pltpu.VMEM((n_t, rows, width), f32),
            pltpu.VMEM((n_t, rows, width), f32),
            pltpu.VMEM((n_t, rows, 2 * width), bf16),
        ],
    )
    got = swap(mate, 1)
    if direct:
        early, behind1 = after([early, behind1], mate)
        behind2, behind3 = step(behind1, 2), step(early, 6)
        beside1 = swap(behind1, 1, "expert", n_e)
    (across,) = run(pair_sum_kernel, [((rows, 2 * width), bf16)], across, got)
    far = swap(across, 2)
    up_grad, down_grad = run(
        expert_grad_kernel,
        [(up_weight.shape, f32), (down_weight.shape, f32)],
        *after([u, z, de, da], across),
    )
    token_packs = around(after([token_pack], across)[0])
    if direct:
        (far,) = after([far], behind2, behind3, beside1)
    (far,) = after([far], up_grad, *token_packs[1:])
    (summed,) = run(expert_sum_kernel, [((rows, 2 * width), bf16)], own, got, far)
    back = exchange(summed)
    output, back_pack = run(
        functools.partial(combine_kernel, n_t=n_t),
        [((width, tok), bf16), ((width + 16, tok), bf16)],
        *token_packs, dest, dy, residual, back,
        fetch=(5,),
    )
    back_packs = around(back_pack)
    if direct:
        beside2, beside3 = (
            swap(v, 1, "expert", n_e) for v in after([behind2, behind3], back_pack)
        )
        saved_all = [saved, behind1, behind2, behind3, beside, beside1, beside2, beside3]

    c0, c1, c2, c3, dr1, d_proj, d_att, d_logits, gain_terms, d_scores = run(
        functools.partial(backward_kernel, n_t=n_t),
        [((width + 16, tok), bf16)] * 4
        + [
            ((width, tok), f32),
            ((inner, tok), bf16),
            ((model, tok), bf16),
            ((experts, tok), f32),
            ((model, tok), f32),
            ((n_heads, tok, tok), bf16),
        ],
        *back_packs, *token_packs, routes_t, router, gain2, out_weight, qkv_wt, heads, probs,
        fetch=(8, 9, 11),
        scratch=[pltpu.VMEM((model, tok), f32)] * 4,
    )
    height = experts + 8
    if direct:
        last_shape = (inner + width + height * (model // tok), tok)
    else:
        last_shape = out_weight.shape
    small, last = run(
        functools.partial(small_grad_kernel, n_t=n_t, n_buckets=n_buckets, direct=direct),
        [((height, model), f32), (last_shape, bf16)],
        *token_packs, d_logits, gain_terms, gain1_row, gain2, saved, d_proj, d_att,
        d_scores, buckets, qkv_w,
        fetch=(6, 12, 13),
        scratch=[pltpu.VMEM((model, tok), f32), padded],
    )
    if direct:
        got = [swap(c, k) for k, c in ((1, c1), (2, c2), (3, c3))]
        (last,) = after([last], *got)
        next_to = swap(last, 1, "expert", n_e)
        last1, last3 = after([step(last, 2), step(last, 6)], next_to)
        lasts = [last, last1, step(last1, 2), last3]
    else:
        got = [swap(c, k) for k, c in ((1, c1), (2, c2), (3, c3))]
    (input_grad,) = run(
        functools.partial(input_grad_kernel, n_t=n_t),
        [((width, tok), f32)],
        c0, *got, dr1, inv1, x, gain1,
        fetch=(6,),
    )
    if direct:
        (att,) = run(
            join_kernel, [((n_e * width, tok), bf16)], *after(saved_all, lasts[1])
        )
        half = n_e // 2
        (part,) = run(
            functools.partial(qkv_grad_kernel, count=half, inner=inner),
            [((inner, model), f32)],
            *lasts, *saved_all[:half],
        )
        lasts += [next_to] + [swap(v, 1, "expert", n_e) for v in lasts[1:]]
        atts = [att, swap(att, 1), swap(att, 2)]
        atts.append(swap(after(atts[2:], lasts[half + 1])[0], 1))
        lasts[half:] = after(lasts[half:], part)
        small, own, q1, q2, q3 = run(
            functools.partial(late_sum_kernel, n_e=n_e, inner=inner),
            [((height, model), f32), ((width, width), f32)]
            + [((width + 16, width), bf16)] * 3,
            *atts, *lasts,
        )
        got = [swap(q, k) for k, q in ((1, q1), (2, q2), (3, q3))]
        (part,) = after([part], own)
        (qkv_grad,) = run(
            functools.partial(qkv_grad_kernel, count=half, inner=inner),
            [((inner, model), f32)],
            *lasts[half:], *saved_all[half:], part,
        )
        out_grad, first, second, router_grad, rel_grad = run(
            functools.partial(out_grad_kernel, n_t=n_t),
            [
                (out_weight.shape, f32),
                ((model,), f32),
                ((model,), f32),
                ((experts, model), f32),
                ((n_heads, n_buckets), f32),
            ],
            own, *got, small,
            scratch=[pltpu.VMEM((n_t, width, width), f32), pltpu.VMEM((1, model), f32)],
        )
    else:
        small, out_grad = lax.psum((small, last.astype(f32)), "expert")
        (qkv_grad,) = run(
            functools.partial(qkv_grad_kernel, count=1, inner=inner),
            [((inner, model), f32)],
            d_proj, saved,
        )
        qkv_grad = lax.psum(qkv_grad, "expert")
        first = lax.psum(small[experts + 1], "tensor")
        second = small[experts]
        router_grad = small[:experts]
        rel_grad = small[experts + 2:experts + 2 + n_heads, :n_buckets]
    return (
        output.T,
        input_grad.T,
        first.reshape(model),
        second.reshape(model),
        qkv_grad.reshape(3, width, model).transpose(0, 2, 1),
        out_grad,
        rel_grad.T,
        router_grad.T,
        up_grad,
        down_grad,
    )


def solution(mesh):
    placed = (
        P("expert", "tensor"),
        P(),
        P(),
        P(None, None, "tensor"),
        P("tensor", None),
        P(None, "tensor"),
        P(),
        P("expert", None, "tensor"),
        P("expert", "tensor", None),
        P("expert", None),
        P("expert", None),
        P(),
        P("expert", "tensor"),
    )
    return jax.shard_map(
        functools.partial(per_device, n_t=mesh.shape["tensor"], n_e=mesh.shape["expert"]),
        mesh=mesh,
        in_specs=placed,
        out_specs=(
            P("expert", "tensor"),
            P("expert", "tensor"),
            P(),
            P(),
            P(None, None, "tensor"),
            P("tensor", None),
            P(None, "tensor"),
            P(),
            P("expert", None, "tensor"),
            P("expert", "tensor", None),
        ),
        check_vma=False,
    )
```

```python
import functools
import math

import jax
import jax.numpy as jnp
from jax import lax
from jax.experimental import pallas as pl
from jax.experimental.pallas import tpu as pltpu
from jax.sharding import PartitionSpec as P

epsilon = 1e-06
highest = lax.Precision.HIGHEST
big_negative = -1e30
bf16 = jnp.bfloat16
f32 = jnp.float32
i32 = jnp.int32


def mm(a, b, contract=(1, 0), precision=None):
    return lax.dot_general(
        a,
        b,
        (((contract[0],), (contract[1],)), ((), ())),
        preferred_element_type=f32,
        precision=precision,
    )


def iota(shape, dim):
    return lax.broadcasted_iota(i32, shape, dim)


def split_hi_lo(v):
    hi = v.astype(bf16).astype(f32)
    return hi, v - hi


def row_block(values, rows=16):
    lanes = values[0].shape[1]
    row = iota((rows, lanes), 0)
    block = jnp.zeros((rows, lanes), f32)
    for i, v in enumerate(values):
        block = jnp.where(row == i, v, block)
    return block


def run(body, outs, *args, fetch=(), scratch=(), limit=32):
    n, m, f = len(args), len(outs), len(fetch)
    moved = sum(a.size * a.dtype.itemsize for a in args)
    moved += sum(math.prod(s) * jnp.dtype(d).itemsize for s, d in outs)
    held = [pltpu.VMEM(args[i].shape, args[i].dtype) for i in fetch]
    sems = [pltpu.SemaphoreType.DMA((f,))] if f else []

    def whole(*refs):
        ins, rest = list(refs[:n]), refs[n + m:]
        copies = [
            pltpu.make_async_copy(ins[i], rest[j], rest[f].at[j]) for j, i in enumerate(fetch)
        ]
        for copy in copies:
            copy.start()
        for copy in copies:
            copy.wait()
        for j, i in enumerate(fetch):
            ins[i] = rest[j]
        body(*ins, *refs[n:n + m], *rest[f + len(sems):])

    return pl.pallas_call(
        whole,
        out_shape=[jax.ShapeDtypeStruct(s, d) for s, d in outs],
        in_specs=[
            pl.BlockSpec(memory_space=pltpu.HBM) if i in fetch else pl.BlockSpec()
            for i in range(n)
        ],
        out_specs=[pl.BlockSpec()] * m,
        scratch_shapes=held + sems + list(scratch),
        compiler_params=pltpu.CompilerParams(vmem_limit_bytes=limit * 2**20),
        cost_estimate=pl.CostEstimate(flops=0, bytes_accessed=moved, transcendentals=0),
    )(*args)


def my_place():
    return lax.axis_index("tensor"), lax.axis_index("expert")


def column_of(row, out):
    for c in range(row.shape[1] // 128):
        part = jnp.broadcast_to(row[:, c * 128:(c + 1) * 128], (128, 128))
        part = jnp.where(iota((128, 128), 0) == iota((128, 128), 1), part, 0.0)
        out[c * 128:(c + 1) * 128, :] = jnp.sum(part, axis=1, keepdims=True)


def skew(values, sign):
    n = values.shape[0]
    row = iota(values.shape, 0)
    bit = 1
    while bit < n:
        moved = pltpu.roll(values, bit if sign > 0 else n - bit, 1)
        values = jnp.where((row & bit) != 0, moved, values)
        bit *= 2
    return values


def bucket_hot(buckets, padded, count):
    padded[...] = jnp.full(padded.shape, -1, i32)
    padded[:, 0:buckets.shape[1]] = buckets[...]
    return (padded[...] == iota((count, padded.shape[1]), 0)).astype(f32)


def prepare_kernel(lengths, gain, out_w, table, buckets, gain_col, out_wt, bias, padded):
    tok = bias.shape[1]
    column_of(gain[...], gain_col)
    out_wt[...] = out_w[...].astype(f32).T.astype(bf16)
    key_pos = iota((tok, tok), 0)
    query_pos = iota((tok, tok), 1)
    end0 = lengths[0:1, 0:1]
    end1 = end0 + lengths[0:1, 1:2]
    seg_k = (key_pos >= end0).astype(i32) + (key_pos >= end1).astype(i32)
    seg_q = (query_pos >= end0).astype(i32) + (query_pos >= end1).astype(i32)
    allowed = (seg_k == seg_q) & (key_pos <= query_pos)
    hot = bucket_hot(buckets, padded, table.shape[1])
    per_head = mm(table[...], hot, precision=highest)
    for h in range(table.shape[0]):
        full = skew(jnp.broadcast_to(per_head[h:h + 1], (tok, tok)), 1)
        bias[h] = jnp.where(allowed, full, big_negative)


def route_kernel(
    routes, router, gain, qkv_w, after, dest, gain_col, rw_own, qkv_wt, chunks,
    *, experts, cap, n_t,
):
    tok = routes.shape[1]
    width = rw_own.shape[1]
    rt = routes[...]
    x_of = iota((experts, tok), 0)
    m0 = (rt[0:1] == x_of).astype(f32)
    m1 = (rt[1:2] == x_of).astype(f32)
    earlier = (iota((tok, tok), 0) < iota((tok, tok), 1)).astype(f32).astype(bf16)
    counts = mm((m0 + m1).astype(bf16), earlier)
    rows = [
        rt[i:i + 1].astype(f32) * cap + jnp.sum(m * counts, axis=0, keepdims=True)
        for i, m in enumerate((m0, m1))
    ]
    dest[...] = row_block(rows, 8)
    column_of(gain[...], gain_col)
    wide = router[...].astype(f32)
    for s in range(n_t):
        chunks[s] = wide[:, s * width:(s + 1) * width]
    rw_own[...] = chunks[my_place()[0]].astype(bf16)
    qkv_wt[...] = qkv_w[...].astype(f32).T.astype(bf16)


def chunk(ref, s, width):
    return ref.at[pl.ds(pl.multiple_of(s * width, 64), width)]


def attention_kernel(
    x0, x1, x2, x3, gain, qkv_w, out_wt, bias,
    own, p1, p2, p3, inv1, heads, probs, saved,
    xs, parts, *, n_t,
):
    width, tok = x0.shape
    n_heads = bias.shape[0]
    size = width // n_heads
    model = n_t * width
    r, _ = my_place()
    for k, x in enumerate((x0, x1, x2, x3)):
        chunk(xs, r ^ k, width)[...] = x[...].astype(f32)
    inverse = lax.rsqrt(jnp.sum(xs[...] * xs[...], axis=0, keepdims=True) / model + epsilon)
    inv1[...] = inverse
    saved[0:model] = (xs[...] * inverse * gain[...]).astype(bf16)
    heads[...] = mm(qkv_w[...], saved[0:model]).astype(bf16)
    for h in range(n_heads):
        q, k, v = (heads[j * width + h * size:j * width + (h + 1) * size] for j in range(3))
        scores = mm(k, q, (0, 0)) * (size ** -0.5) + bias[h]
        weights = jnp.exp(scores - jnp.max(scores, axis=0, keepdims=True))
        prob = weights / jnp.sum(weights, axis=0, keepdims=True)
        probs[h] = prob
        here = model + h * size
        saved[here:here + size] = mm(v, prob.astype(bf16)).astype(bf16)
    parts[...] = mm(out_wt[...], saved[model:])
    own[...] = chunk(parts, r, width)[...]
    for k, p in ((1, p1), (2, p2), (3, p3)):
        p[...] = chunk(parts, r ^ k, width)[...].astype(bf16)


def dispatch_kernel(
    own, p1, p2, p3, x, dy, gain, rw_own, routes, dest, *refs
):
    pieces = refs[:-3]
    token_pack, residual, pack = refs[-3:]
    width, tok = x.shape
    experts = rw_own.shape[0]
    r, _ = my_place()
    res = x[...].astype(f32) + own[...] + (
        p1[...].astype(f32) + p2[...].astype(f32) + p3[...].astype(f32)
    )
    residual[...] = res
    scaled = (res * chunk(gain, r, width)[...]).astype(bf16)
    square = jnp.sum(res * res, axis=0, keepdims=True)
    logits = mm(rw_own[...], scaled)
    x_of = iota((experts, tok), 0)
    c0 = jnp.sum(jnp.where(routes[0:1, :] == x_of, logits, 0.0), axis=0, keepdims=True)
    c1 = jnp.sum(jnp.where(routes[1:2, :] == x_of, logits, 0.0), axis=0, keepdims=True)
    stats = row_block(split_hi_lo(square) + split_hi_lo(c0 - c1)).astype(bf16)
    token_pack[0:width] = res.astype(bf16)
    token_pack[width:width + 16] = stats
    token_pack[width + 16:] = dy[...]
    pack[0:width] = scaled
    pack[width:width + 16] = stats
    pack[width + 16:] = dy[...]
    size = pieces[0].shape[0]
    row = iota((size * len(pieces), tok), 0).astype(f32)
    place0 = (row == dest[0:1, :]).astype(f32)
    place1 = (row == dest[1:2, :]).astype(f32)
    both = mm((place0 + place1).astype(bf16), pack[...], (1, 1))
    signed = mm((place0 - place1).astype(bf16), pack[...], (1, 1))
    lane = iota(both.shape, 1)
    full = jnp.where((lane == width + 2) | (lane == width + 3), signed, both)
    for k, piece in enumerate(pieces):
        piece[...] = full[k * size:(k + 1) * size].astype(bf16)


def gelu_pair(a):
    c = 0.7978845608028654
    t = jnp.tanh(c * (a + 0.044715 * a * a * a))
    value = 0.5 * a * (1.0 + t)
    slope = 0.5 * (1.0 + t) + 0.5 * a * (1.0 - t * t) * c * (1.0 + 3 * 0.044715 * a * a)
    return value, slope


def expert_kernel(
    h0, h1, h2, h3, up, down,
    own, across, mate, u, z, de, da,
    hs, gs, chunks, *, n_t,
):
    width = own.shape[1] // 2
    model = n_t * width
    r, _ = my_place()
    packs = (h0, h1, h2, h3)
    for k, h in enumerate(packs):
        s = r ^ k
        hs[s] = h[:, 0:width].astype(f32)
        gs[s] = h[:, width + 16:].astype(f32)
    stats = h0[:, width:width + 16].astype(f32)
    for h in packs[1:]:
        stats += h[:, width:width + 16].astype(f32)
    inverse = lax.rsqrt((stats[:, 0:1] + stats[:, 1:2]) / model + epsilon)
    gate = 1.0 / (1.0 + jnp.exp(-inverse * (stats[:, 2:3] + stats[:, 3:4])))
    for s in range(n_t):
        cols = slice(s * width, (s + 1) * width)
        u[:, cols] = (hs[s] * inverse).astype(bf16)
        de[:, cols] = (gs[s] * gate).astype(bf16)
    value, slope = gelu_pair(mm(u[...], up[0]))
    z[...] = value.astype(bf16)
    da[...] = (mm(de[...], down[0], (1, 1)) * slope).astype(bf16)
    eo = mm(z[...], down[0]).astype(bf16)
    du = mm(da[...], up[0], (1, 1)).astype(bf16)
    for s in range(n_t):
        cols = slice(s * width, (s + 1) * width)
        chunks[s, :, 0:width] = eo[:, cols]
        chunks[s, :, width:] = du[:, cols]
    rows = own.shape[0]
    own[...] = chunks[r]
    across[...] = chunks[r ^ 2]
    mate[0:rows] = chunks[r ^ 1]
    mate[rows:] = chunks[r ^ 3]


def expert_grad_kernel(u, z, de, da, up_grad, down_grad):
    up_grad[0] = mm(u[...], da[...], (0, 0))
    down_grad[0] = mm(z[...], de[...], (0, 0))


def join_kernel(*refs):
    parts, out = refs[:-1], refs[-1]
    height = out.shape[0] // len(parts)
    for j, part in enumerate(parts):
        out[j * height:(j + 1) * height] = part[part.shape[0] - height:]


def pair_sum_kernel(across, got, out):
    rows = across.shape[0]
    out[...] = (across[...].astype(f32) + got[rows:].astype(f32)).astype(bf16)


def expert_sum_kernel(own, got, far, out):
    rows = own.shape[0]
    total = own[...].astype(f32) + got[0:rows].astype(f32) + far[...].astype(f32)
    out[...] = total.astype(bf16)


def total_stats(packs, width):
    total = packs[0][width:width + 16].astype(f32)
    for p in packs[1:]:
        total += p[width:width + 16].astype(f32)
    return total


def gates_of(stats, model):
    inverse = lax.rsqrt((stats[0:1] + stats[1:2]) / model + epsilon)
    delta = inverse * (stats[2:3] + stats[3:4])
    return inverse, 1.0 / (1.0 + jnp.exp(-delta)), 1.0 / (1.0 + jnp.exp(delta))


def combine_kernel(t0, t1, t2, t3, dest, dy, residual, *refs, n_t):
    pieces, (output, pack) = refs[:-2], refs[-2:]
    width, tok = dy.shape
    _, gate0, gate1 = gates_of(total_stats((t0, t1, t2, t3), width), n_t * width)
    back = pieces[0][...]
    row = iota((back.shape[0], tok), 0).astype(f32)
    pick0 = (row == dest[0:1, :]).astype(f32).astype(bf16)
    pick1 = (row == dest[1:2, :]).astype(f32).astype(bf16)
    got0 = mm(back, pick0, (0, 0))
    got1 = mm(back, pick1, (0, 0))
    e0, e1 = got0[0:width], got1[0:width]
    output[...] = (residual[...] + gate0 * e0 + gate1 * e1).astype(bf16)
    dy_own = dy[...].astype(f32)
    dg0 = jnp.sum(dy_own * e0, axis=0, keepdims=True)
    dg1 = jnp.sum(dy_own * e1, axis=0, keepdims=True)
    pack[0:width] = (got0[width:] + got1[width:]).astype(bf16)
    pack[width:] = row_block(split_hi_lo(dg0) + split_hi_lo(dg1)).astype(bf16)


def backward_kernel(
    b0, b1, b2, b3, t0, t1, t2, t3,
    routes, router, gain, out_w, qkv_wt, heads, probs,
    c0, c1, c2, c3, dr1_own, d_proj, d_att, d_logits, gain_terms, d_scores,
    bs, ts, ys, dr, *, n_t,
):
    width = dr1_own.shape[0]
    tok = b0.shape[1]
    experts = router.shape[0]
    n_heads = probs.shape[0]
    size = width // n_heads
    model = n_t * width
    r, _ = my_place()
    packs, tokens = (b0, b1, b2, b3), (t0, t1, t2, t3)
    for k in range(n_t):
        s = r ^ k
        chunk(bs, s, width)[...] = packs[k][0:width].astype(f32)
        chunk(ts, s, width)[...] = tokens[k][0:width].astype(f32)
        chunk(ys, s, width)[...] = tokens[k][width + 16:].astype(f32)
    inverse, gate0, gate1 = gates_of(total_stats(tokens, width), model)
    back = total_stats(packs, width)
    dg0 = back[0:1] + back[1:2]
    dg1 = back[2:3] + back[3:4]
    mean_gate = gate0 * dg0 + gate1 * dg1
    x_of = iota((experts, tok), 0)
    dlog = jnp.where(routes[0:1, :] == x_of, gate0 * (dg0 - mean_gate), 0.0) + jnp.where(
        routes[1:2, :] == x_of, gate1 * (dg1 - mean_gate), 0.0
    )
    d_logits[...] = dlog
    dh2 = bs[...] + mm(router[...].astype(f32), dlog, (0, 0), precision=highest)
    res = ts[...]
    gain_terms[...] = dh2 * res * inverse
    weighted = dh2 * gain[...]
    dot = jnp.sum(weighted * res, axis=0, keepdims=True) * (inverse**3 / model)
    dr[...] = ys[...] + inverse * weighted - res * dot
    d_att[...] = dr[...].astype(bf16)
    dr1_own[...] = chunk(dr, r, width)[...]
    d_o = mm(out_w[...], d_att[...]).astype(bf16)
    scale = size ** -0.5
    for h in range(n_heads):
        q, k, v = (heads[j * width + h * size:j * width + (h + 1) * size] for j in range(3))
        d_oh = d_o[h * size:(h + 1) * size]
        prob = probs[h]
        d_prob = mm(v, d_oh, (0, 0))
        centre = jnp.sum(prob * d_prob, axis=0, keepdims=True)
        ds = (prob * (d_prob - centre)).astype(bf16)
        d_scores[h] = ds
        here = h * size
        d_proj[here:here + size] = (mm(k, ds) * scale).astype(bf16)
        here += width
        d_proj[here:here + size] = (mm(q, ds, (1, 1)) * scale).astype(bf16)
        here += width
        d_proj[here:here + size] = mm(d_oh, prob.astype(bf16), (1, 1)).astype(bf16)
    row_dot = jnp.sum(
        d_proj[...].astype(f32) * heads[...].astype(f32), axis=0, keepdims=True
    )
    stats = row_block(split_hi_lo(row_dot)).astype(bf16)
    dr[...] = mm(qkv_wt[...], d_proj[...])
    for k, c in enumerate((c0, c1, c2, c3)):
        c[0:width] = chunk(dr, r ^ k, width)[...].astype(bf16)
        c[width:] = stats


def small_grad_kernel(
    t0, t1, t2, t3, d_logits, gain_terms, gain1_row, gain2, saved, d_proj, d_att,
    d_scores, buckets, qkv_w, small, last, ts, padded, *, n_t, n_buckets, direct,
):
    packs = (t0, t1, t2, t3)
    width = d_proj.shape[0] // 3
    model = n_t * width
    inner = d_proj.shape[0]
    experts = d_logits.shape[0]
    tok = t0.shape[1]
    r, _ = my_place()
    for k, t in enumerate(packs):
        chunk(ts, r ^ k, width)[...] = t[0:width].astype(f32)
    inverse, _, _ = gates_of(total_stats(packs, width), model)
    normed = (ts[...] * inverse * gain2[...]).astype(bf16).astype(f32)
    small[0:experts] = mm(d_logits[...], normed, (1, 1), precision=highest)
    ones = jnp.ones((8, tok), f32)
    small[experts:] = jnp.zeros((small.shape[0] - experts, model), f32)
    small[experts:experts + 1] = mm(ones, gain_terms[...], (1, 1), precision=highest)[0:1]
    grad = mm(d_proj[...], saved[0:model], (1, 1))
    first = jnp.sum(grad * qkv_w[...].astype(f32), axis=0, keepdims=True)
    small[experts + 1:experts + 2] = first / gain1_row[...]
    hot = bucket_hot(buckets, padded, n_buckets)
    for h in range(d_scores.shape[0]):
        diagonal = jnp.sum(skew(d_scores[h].astype(f32), -1), axis=0, keepdims=True)
        per_bucket = mm(jnp.broadcast_to(diagonal, (8, tok)), hot, (1, 1), precision=highest)
        here = experts + 2 + h
        small[here:here + 1, 0:n_buckets] = per_bucket[0:1]
    if direct:
        last[0:inner] = d_proj[...]
        last[inner:inner + width] = chunk(d_att, r, width)[...]
        height = small.shape[0]
        for c in range(model // tok):
            here = inner + width + c * height
            last[here:here + height] = small[:, c * tok:(c + 1) * tok].astype(bf16)
    else:
        last[...] = mm(saved[model:], d_att[...], (1, 1)).astype(last.dtype)


def late_sum_kernel(o0, o1, o2, o3, *refs, n_e, inner):
    lasts, (small, own, q1, q2, q3) = refs[:n_e], refs[n_e:]
    width = own.shape[0]
    stride, tok = lasts[0].shape
    height, model = small.shape
    total = lasts[0][inner + width:].astype(f32)
    for last in lasts[1:]:
        total += last[inner + width:].astype(f32)
    for c in range(model // tok):
        small[:, c * tok:(c + 1) * tok] = total[c * height:(c + 1) * height]
    first = small[height - 7:height - 6]
    hi, lo = split_hi_lo(first)
    wide = row_block(
        [v[:, s * width:(s + 1) * width] for v in (hi, lo) for s in range(model // width)]
    )
    for o, q in ((o0, own), (o1, q1), (o2, q2), (o3, q3)):
        grad = 0.0
        for j, last in enumerate(lasts):
            grad += mm(o[j * width:(j + 1) * width], last[inner:inner + width], (1, 1))
        q[0:width] = grad.astype(q.dtype)
        if q is not own:
            q[width:] = wide.astype(bf16)


def out_grad_kernel(
    own, q1, q2, q3, small, out, first, second, router, rel, blocks, line, *, n_t
):
    width = own.shape[0]
    experts, buckets = router.shape[0], rel.shape[1]
    r, _ = my_place()
    blocks[r] = own[...]
    for k, q in ((1, q1), (2, q2), (3, q3)):
        blocks[r ^ k] = q[0:width].astype(f32)
    for s in range(n_t):
        cols = slice(s * width, (s + 1) * width)
        out[:, cols] = blocks[s]
        total = small[experts + 1:experts + 2, cols]
        for q in (q1, q2, q3):
            parts = q[width:].astype(f32)
            total += parts[s:s + 1] + parts[n_t + s:n_t + s + 1]
        line[:, cols] = total
    first[...] = line[0]
    second[...] = small[experts]
    router[...] = small[0:experts]
    rel[...] = small[experts + 2:experts + 2 + rel.shape[0], 0:buckets]


def input_grad_kernel(c0, c1, c2, c3, dr1, inv1, x, gain, out, *, n_t):
    width = x.shape[0]
    total = c0[...].astype(f32) + c1[...].astype(f32) + (c2[...].astype(f32) + c3[...].astype(f32))
    row_dot = (total[width:width + 1] + total[width + 1:width + 2]) / (n_t * width)
    inverse = inv1[...]
    weighted = total[0:width] * chunk(gain, my_place()[0], width)[...]
    out[...] = dr1[...] + inverse * weighted - x[...].astype(f32) * (inverse * inverse * row_dot)


def qkv_grad_kernel(*refs, count, inner):
    lasts, saved, rest = refs[:count], refs[count:2 * count], refs[2 * count:]
    out = rest[-1]
    model = out.shape[1]
    total = 0.0 if len(rest) == 1 else rest[0][...]
    for last, h in zip(lasts, saved):
        total += mm(last[0:inner], h[0:model], (1, 1))
    out[...] = total


def per_device(
    tokens,
    first_gain,
    second_gain,
    qkv_weight,
    out_weight,
    rel_table,
    router_weight,
    up_weight,
    down_weight,
    routes,
    lengths,
    bucket_ids,
    cotangent,
    *,
    n_t,
    n_e,
):
    tok, width = tokens.shape
    model = n_t * width
    inner = 3 * width
    experts = router_weight.shape[1]
    cap = 5 * tok // (2 * experts)
    rows = experts * cap
    n_heads = rel_table.shape[1]
    n_buckets = rel_table.shape[0]
    direct = n_e == 8
    padded = pltpu.VMEM((1, tok), i32)

    def swap(v, k, axis="tensor", n=n_t):
        return lax.ppermute(v, axis, [(i, i ^ k) for i in range(n)])

    def around(v):
        return [v] + [swap(v, k) for k in range(1, n_t)]

    def around_large(v):
        far = swap(v, 2)
        return [v, swap(v, 1), far, swap(far, 1)]

    def exchange(v):
        w = v.shape[-1]
        v = v.reshape(n_e, rows // n_e, w)
        v = lax.all_to_all(v, "expert", split_axis=0, concat_axis=0, tiled=True)
        return v.reshape(rows, w)

    def step(v, k):
        return lax.ppermute(v, "expert", [(i, (i + k) % n_e) for i in range(n_e)])

    def after(values, *others):
        return list(lax.optimization_barrier((tuple(values), others))[0])

    x = tokens.T
    dy = cotangent.T
    qkv_w = qkv_weight.transpose(0, 2, 1).reshape(inner, model)
    router = router_weight.T
    table = rel_table.T
    routes_t = routes.T
    gain1_row = first_gain.reshape(1, model)
    gain2_row = second_gain.reshape(1, model)
    buckets = bucket_ids.reshape(1, -1)

    xs = around(x)
    gain1, out_wt, bias = run(
        prepare_kernel,
        [((model, 1), f32), ((model, width), bf16), ((n_heads, tok, tok), f32)],
        lengths, gain1_row, out_weight, table, buckets,
        fetch=(0, 1, 2, 3, 4),
        scratch=[padded],
    )
    own, p1, p2, p3, inv1, heads, probs, saved = run(
        functools.partial(attention_kernel, n_t=n_t),
        [((width, tok), f32)]
        + [((width, tok), bf16)] * 3
        + [
            ((1, tok), f32),
            ((inner, tok), bf16),
            ((n_heads, tok, tok), f32),
            ((model + width, tok), bf16),
        ],
        *xs, gain1, qkv_w, out_wt, bias,
        fetch=(n_t + 1,),
        scratch=[pltpu.VMEM((model, tok), f32), pltpu.VMEM((model, tok), f32)],
    )
    got = [swap(p, k) for k, p in ((1, p1), (2, p2), (3, p3))]
    dest, gain2, rw_own, qkv_wt = run(
        functools.partial(route_kernel, experts=experts, cap=cap, n_t=n_t),
        [
            ((8, tok), f32),
            ((model, 1), f32),
            ((experts, width), bf16),
            ((model, inner), bf16),
        ],
        routes_t, router, gain2_row, qkv_w, inv1,
        fetch=(0, 1, 2, 3),
        scratch=[pltpu.VMEM((n_t, experts, width), f32)],
    )
    send_rows, token_pack, residual = run(
        dispatch_kernel,
        [
            ((rows, 2 * width + 16), bf16),
            ((2 * width + 16, tok), bf16),
            ((width, tok), f32),
        ],
        own, *got, x, dy, gain2, rw_own, routes_t, dest,
        fetch=(4, 5, 8),
        scratch=[pltpu.VMEM((2 * width + 16, tok), bf16)],
    )
    in_rows = exchange(send_rows)
    if direct:
        (early,) = after([saved], in_rows)
        behind1, beside = step(early, 2), swap(early, 1, "expert", n_e)
        (far,) = after([swap(in_rows, 2)], behind1, beside)
        in_rows = [in_rows, swap(in_rows, 1), far, swap(far, 1)]
    else:
        in_rows = around_large(in_rows)

    own, across, mate, u, z, de, da = run(
        functools.partial(expert_kernel, n_t=n_t),
        [((rows, 2 * width), bf16)] * 2
        + [((2 * rows, 2 * width), bf16)]
        + [((rows, model), bf16)] * 4,
        *in_rows, up_weight, down_weight,
        fetch=(4, 5),
        scratch=[
            pltpu.VMEM((n_t, rows, width), f32),
            pltpu.VMEM((n_t, rows, width), f32),
            pltpu.VMEM((n_t, rows, 2 * width), bf16),
        ],
    )
    got = swap(mate, 1)
    if direct:
        early, behind1 = after([early, behind1], mate)
        behind2, behind3 = step(behind1, 2), step(early, 6)
        beside1 = swap(behind1, 1, "expert", n_e)
    (across,) = run(pair_sum_kernel, [((rows, 2 * width), bf16)], across, got)
    far = swap(across, 2)
    up_grad, down_grad = run(
        expert_grad_kernel,
        [(up_weight.shape, f32), (down_weight.shape, f32)],
        *after([u, z, de, da], across),
    )
    token_packs = around(after([token_pack], up_grad)[0])
    if direct:
        (far,) = after([far], behind2, behind3, beside1)
    (far,) = after([far], up_grad, *token_packs[1:])
    (summed,) = run(expert_sum_kernel, [((rows, 2 * width), bf16)], own, got, far)
    back = exchange(summed)
    output, back_pack = run(
        functools.partial(combine_kernel, n_t=n_t),
        [((width, tok), bf16), ((width + 16, tok), bf16)],
        *token_packs, dest, dy, residual, back,
        fetch=(5,),
    )
    back_packs = around(back_pack)
    if direct:
        beside2, beside3 = (
            swap(v, 1, "expert", n_e) for v in after([behind2, behind3], back_pack)
        )
        saved_all = [saved, behind1, behind2, behind3, beside, beside1, beside2, beside3]

    c0, c1, c2, c3, dr1, d_proj, d_att, d_logits, gain_terms, d_scores = run(
        functools.partial(backward_kernel, n_t=n_t),
        [((width + 16, tok), bf16)] * 4
        + [
            ((width, tok), f32),
            ((inner, tok), bf16),
            ((model, tok), bf16),
            ((experts, tok), f32),
            ((model, tok), f32),
            ((n_heads, tok, tok), bf16),
        ],
        *back_packs, *token_packs, routes_t, router, gain2, out_weight, qkv_wt, heads, probs,
        fetch=(8, 9, 11),
        scratch=[pltpu.VMEM((model, tok), f32)] * 4,
    )
    if direct:
        (d_scores,) = after([d_scores], beside2, beside3)
    height = experts + 8
    if direct:
        last_shape = (inner + width + height * (model // tok), tok)
    else:
        last_shape = out_weight.shape
    small, last = run(
        functools.partial(small_grad_kernel, n_t=n_t, n_buckets=n_buckets, direct=direct),
        [((height, model), f32), (last_shape, bf16)],
        *token_packs, d_logits, gain_terms, gain1_row, gain2, saved, d_proj, d_att,
        d_scores, buckets, qkv_w,
        fetch=(6, 12, 13),
        scratch=[pltpu.VMEM((model, tok), f32), padded],
    )
    if direct:
        got = [swap(c, k) for k, c in ((1, c1), (2, c2), (3, c3))]
        (last,) = after([last], *got)
        next_to = swap(last, 1, "expert", n_e)
        last1, last3 = after([step(last, 2), step(last, 6)], next_to)
        lasts = [last, last1, step(last1, 2), last3]
    else:
        got = [swap(c, k) for k, c in ((1, c1), (2, c2), (3, c3))]
    (input_grad,) = run(
        functools.partial(input_grad_kernel, n_t=n_t),
        [((width, tok), f32)],
        c0, *got, dr1, inv1, x, gain1,
        fetch=(6,),
    )
    if direct:
        (att,) = run(
            join_kernel, [((n_e * width, tok), bf16)], *after(saved_all, lasts[1])
        )
        half = n_e // 2
        (part,) = run(
            functools.partial(qkv_grad_kernel, count=half, inner=inner),
            [((inner, model), f32)],
            *lasts, *saved_all[:half],
        )
        lasts += [next_to] + [swap(v, 1, "expert", n_e) for v in lasts[1:]]
        atts = [att, swap(att, 1), swap(att, 2)]
        atts.append(swap(after(atts[2:], lasts[half + 1])[0], 1))
        lasts[half:] = after(lasts[half:], part)
        small, own, q1, q2, q3 = run(
            functools.partial(late_sum_kernel, n_e=n_e, inner=inner),
            [((height, model), f32), ((width, width), f32)]
            + [((width + 16, width), bf16)] * 3,
            *atts, *lasts,
        )
        got = [swap(q, k) for k, q in ((1, q1), (2, q2), (3, q3))]
        (part,) = after([part], own)
        (qkv_grad,) = run(
            functools.partial(qkv_grad_kernel, count=half, inner=inner),
            [((inner, model), f32)],
            *lasts[half:], *saved_all[half:], part,
        )
        out_grad, first, second, router_grad, rel_grad = run(
            functools.partial(out_grad_kernel, n_t=n_t),
            [
                (out_weight.shape, f32),
                ((model,), f32),
                ((model,), f32),
                ((experts, model), f32),
                ((n_heads, n_buckets), f32),
            ],
            own, *got, small,
            scratch=[pltpu.VMEM((n_t, width, width), f32), pltpu.VMEM((1, model), f32)],
        )
    else:
        small, out_grad = lax.psum((small, last.astype(f32)), "expert")
        (qkv_grad,) = run(
            functools.partial(qkv_grad_kernel, count=1, inner=inner),
            [((inner, model), f32)],
            d_proj, saved,
        )
        qkv_grad = lax.psum(qkv_grad, "expert")
        first = lax.psum(small[experts + 1], "tensor")
        second = small[experts]
        router_grad = small[:experts]
        rel_grad = small[experts + 2:experts + 2 + n_heads, :n_buckets]
    return (
        output.T,
        input_grad.T,
        first.reshape(model),
        second.reshape(model),
        qkv_grad.reshape(3, width, model).transpose(0, 2, 1),
        out_grad,
        rel_grad.T,
        router_grad.T,
        up_grad,
        down_grad,
    )


def solution(mesh):
    placed = (
        P("expert", "tensor"),
        P(),
        P(),
        P(None, None, "tensor"),
        P("tensor", None),
        P(None, "tensor"),
        P(),
        P("expert", None, "tensor"),
        P("expert", "tensor", None),
        P("expert", None),
        P("expert", None),
        P(),
        P("expert", "tensor"),
    )
    return jax.shard_map(
        functools.partial(per_device, n_t=mesh.shape["tensor"], n_e=mesh.shape["expert"]),
        mesh=mesh,
        in_specs=placed,
        out_specs=(
            P("expert", "tensor"),
            P("expert", "tensor"),
            P(),
            P(),
            P(None, None, "tensor"),
            P("tensor", None),
            P(None, "tensor"),
            P(),
            P("expert", None, "tensor"),
            P("expert", "tensor", None),
        ),
        check_vma=False,
    )
```

```python
import functools
import math

import jax
import jax.numpy as jnp
from jax import lax
from jax.experimental import pallas as pl
from jax.experimental.pallas import tpu as pltpu
from jax.sharding import PartitionSpec as P

epsilon = 1e-06
highest = lax.Precision.HIGHEST
big_negative = -1e30
bf16 = jnp.bfloat16
f32 = jnp.float32
i32 = jnp.int32


def mm(a, b, contract=(1, 0), precision=None):
    return lax.dot_general(
        a,
        b,
        (((contract[0],), (contract[1],)), ((), ())),
        preferred_element_type=f32,
        precision=precision,
    )


def iota(shape, dim):
    return lax.broadcasted_iota(i32, shape, dim)


def split_hi_lo(v):
    hi = v.astype(bf16).astype(f32)
    return hi, v - hi


def row_block(values, rows=16):
    lanes = values[0].shape[1]
    row = iota((rows, lanes), 0)
    block = jnp.zeros((rows, lanes), f32)
    for i, v in enumerate(values):
        block = jnp.where(row == i, v, block)
    return block


def run(body, outs, *args, fetch=(), scratch=(), limit=32):
    n, m, f = len(args), len(outs), len(fetch)
    moved = sum(a.size * a.dtype.itemsize for a in args)
    moved += sum(math.prod(s) * jnp.dtype(d).itemsize for s, d in outs)
    held = [pltpu.VMEM(args[i].shape, args[i].dtype) for i in fetch]
    sems = [pltpu.SemaphoreType.DMA((f,))] if f else []

    def whole(*refs):
        ins, rest = list(refs[:n]), refs[n + m:]
        copies = [
            pltpu.make_async_copy(ins[i], rest[j], rest[f].at[j]) for j, i in enumerate(fetch)
        ]
        for copy in copies:
            copy.start()
        for copy in copies:
            copy.wait()
        for j, i in enumerate(fetch):
            ins[i] = rest[j]
        body(*ins, *refs[n:n + m], *rest[f + len(sems):])

    return pl.pallas_call(
        whole,
        out_shape=[jax.ShapeDtypeStruct(s, d) for s, d in outs],
        in_specs=[
            pl.BlockSpec(memory_space=pltpu.HBM) if i in fetch else pl.BlockSpec()
            for i in range(n)
        ],
        out_specs=[pl.BlockSpec()] * m,
        scratch_shapes=held + sems + list(scratch),
        compiler_params=pltpu.CompilerParams(vmem_limit_bytes=limit * 2**20),
        cost_estimate=pl.CostEstimate(flops=0, bytes_accessed=moved, transcendentals=0),
    )(*args)


def my_place():
    return lax.axis_index("tensor"), lax.axis_index("expert")


def column_of(row, out):
    for c in range(row.shape[1] // 128):
        part = jnp.broadcast_to(row[:, c * 128:(c + 1) * 128], (128, 128))
        part = jnp.where(iota((128, 128), 0) == iota((128, 128), 1), part, 0.0)
        out[c * 128:(c + 1) * 128, :] = jnp.sum(part, axis=1, keepdims=True)


def skew(values, sign):
    n = values.shape[0]
    row = iota(values.shape, 0)
    bit = 1
    while bit < n:
        moved = pltpu.roll(values, bit if sign > 0 else n - bit, 1)
        values = jnp.where((row & bit) != 0, moved, values)
        bit *= 2
    return values


def bucket_hot(buckets, padded, count):
    padded[...] = jnp.full(padded.shape, -1, i32)
    padded[:, 0:buckets.shape[1]] = buckets[...]
    return (padded[...] == iota((count, padded.shape[1]), 0)).astype(f32)


def prepare_kernel(lengths, gain, out_w, table, buckets, gain_col, out_wt, bias, padded):
    tok = bias.shape[1]
    column_of(gain[...], gain_col)
    out_wt[...] = out_w[...].astype(f32).T.astype(bf16)
    key_pos = iota((tok, tok), 0)
    query_pos = iota((tok, tok), 1)
    end0 = lengths[0:1, 0:1]
    end1 = end0 + lengths[0:1, 1:2]
    seg_k = (key_pos >= end0).astype(i32) + (key_pos >= end1).astype(i32)
    seg_q = (query_pos >= end0).astype(i32) + (query_pos >= end1).astype(i32)
    allowed = (seg_k == seg_q) & (key_pos <= query_pos)
    hot = bucket_hot(buckets, padded, table.shape[1])
    per_head = mm(table[...], hot, precision=highest)
    for h in range(table.shape[0]):
        full = skew(jnp.broadcast_to(per_head[h:h + 1], (tok, tok)), 1)
        bias[h] = jnp.where(allowed, full, big_negative)


def route_kernel(
    routes, router, gain, qkv_w, after, dest, gain_col, rw_own, qkv_wt, chunks,
    *, experts, cap, n_t,
):
    tok = routes.shape[1]
    width = rw_own.shape[1]
    rt = routes[...]
    x_of = iota((experts, tok), 0)
    m0 = (rt[0:1] == x_of).astype(f32)
    m1 = (rt[1:2] == x_of).astype(f32)
    earlier = (iota((tok, tok), 0) < iota((tok, tok), 1)).astype(f32).astype(bf16)
    counts = mm((m0 + m1).astype(bf16), earlier)
    rows = [
        rt[i:i + 1].astype(f32) * cap + jnp.sum(m * counts, axis=0, keepdims=True)
        for i, m in enumerate((m0, m1))
    ]
    dest[...] = row_block(rows, 8)
    column_of(gain[...], gain_col)
    wide = router[...].astype(f32)
    for s in range(n_t):
        chunks[s] = wide[:, s * width:(s + 1) * width]
    rw_own[...] = chunks[my_place()[0]].astype(bf16)
    qkv_wt[...] = qkv_w[...].astype(f32).T.astype(bf16)


def chunk(ref, s, width):
    return ref.at[pl.ds(pl.multiple_of(s * width, 64), width)]


def attention_kernel(
    x0, x1, x2, x3, gain, qkv_w, out_wt, bias,
    own, p1, p2, p3, inv1, heads, probs, saved,
    xs, parts, *, n_t,
):
    width, tok = x0.shape
    n_heads = bias.shape[0]
    size = width // n_heads
    model = n_t * width
    r, _ = my_place()
    for k, x in enumerate((x0, x1, x2, x3)):
        chunk(xs, r ^ k, width)[...] = x[...].astype(f32)
    inverse = lax.rsqrt(jnp.sum(xs[...] * xs[...], axis=0, keepdims=True) / model + epsilon)
    inv1[...] = inverse
    saved[0:model] = (xs[...] * inverse * gain[...]).astype(bf16)
    heads[...] = mm(qkv_w[...], saved[0:model]).astype(bf16)
    for h in range(n_heads):
        q, k, v = (heads[j * width + h * size:j * width + (h + 1) * size] for j in range(3))
        scores = mm(k, q, (0, 0)) * (size ** -0.5) + bias[h]
        weights = jnp.exp(scores - jnp.max(scores, axis=0, keepdims=True))
        prob = weights / jnp.sum(weights, axis=0, keepdims=True)
        probs[h] = prob
        here = model + h * size
        saved[here:here + size] = mm(v, prob.astype(bf16)).astype(bf16)
    parts[...] = mm(out_wt[...], saved[model:])
    own[...] = chunk(parts, r, width)[...]
    for k, p in ((1, p1), (2, p2), (3, p3)):
        p[...] = chunk(parts, r ^ k, width)[...].astype(bf16)


def dispatch_kernel(
    own, p1, p2, p3, x, dy, gain, rw_own, routes, dest, *refs
):
    pieces = refs[:-3]
    token_pack, residual, pack = refs[-3:]
    width, tok = x.shape
    experts = rw_own.shape[0]
    r, _ = my_place()
    res = x[...].astype(f32) + own[...] + (
        p1[...].astype(f32) + p2[...].astype(f32) + p3[...].astype(f32)
    )
    residual[...] = res
    scaled = (res * chunk(gain, r, width)[...]).astype(bf16)
    square = jnp.sum(res * res, axis=0, keepdims=True)
    logits = mm(rw_own[...], scaled)
    x_of = iota((experts, tok), 0)
    c0 = jnp.sum(jnp.where(routes[0:1, :] == x_of, logits, 0.0), axis=0, keepdims=True)
    c1 = jnp.sum(jnp.where(routes[1:2, :] == x_of, logits, 0.0), axis=0, keepdims=True)
    stats = row_block(split_hi_lo(square) + split_hi_lo(c0 - c1)).astype(bf16)
    token_pack[0:width] = res.astype(bf16)
    token_pack[width:width + 16] = stats
    token_pack[width + 16:] = dy[...]
    pack[0:width] = scaled
    pack[width:width + 16] = stats
    pack[width + 16:] = dy[...]
    size = pieces[0].shape[0]
    row = iota((size * len(pieces), tok), 0).astype(f32)
    place0 = (row == dest[0:1, :]).astype(f32)
    place1 = (row == dest[1:2, :]).astype(f32)
    both = mm((place0 + place1).astype(bf16), pack[...], (1, 1))
    signed = mm((place0 - place1).astype(bf16), pack[...], (1, 1))
    lane = iota(both.shape, 1)
    full = jnp.where((lane == width + 2) | (lane == width + 3), signed, both)
    for k, piece in enumerate(pieces):
        piece[...] = full[k * size:(k + 1) * size].astype(bf16)


def gelu_pair(a):
    c = 0.7978845608028654
    t = jnp.tanh(c * (a + 0.044715 * a * a * a))
    value = 0.5 * a * (1.0 + t)
    slope = 0.5 * (1.0 + t) + 0.5 * a * (1.0 - t * t) * c * (1.0 + 3 * 0.044715 * a * a)
    return value, slope


def expert_kernel(
    h0, h1, h2, h3, up, down,
    own, across, mate, u, z, de, da,
    hs, gs, chunks, *, n_t,
):
    width = own.shape[1] // 2
    model = n_t * width
    r, _ = my_place()
    packs = (h0, h1, h2, h3)
    for k, h in enumerate(packs):
        s = r ^ k
        hs[s] = h[:, 0:width].astype(f32)
        gs[s] = h[:, width + 16:].astype(f32)
    stats = h0[:, width:width + 16].astype(f32)
    for h in packs[1:]:
        stats += h[:, width:width + 16].astype(f32)
    inverse = lax.rsqrt((stats[:, 0:1] + stats[:, 1:2]) / model + epsilon)
    gate = 1.0 / (1.0 + jnp.exp(-inverse * (stats[:, 2:3] + stats[:, 3:4])))
    for s in range(n_t):
        cols = slice(s * width, (s + 1) * width)
        u[:, cols] = (hs[s] * inverse).astype(bf16)
        de[:, cols] = (gs[s] * gate).astype(bf16)
    value, slope = gelu_pair(mm(u[...], up[0]))
    z[...] = value.astype(bf16)
    da[...] = (mm(de[...], down[0], (1, 1)) * slope).astype(bf16)
    eo = mm(z[...], down[0]).astype(bf16)
    du = mm(da[...], up[0], (1, 1)).astype(bf16)
    for s in range(n_t):
        cols = slice(s * width, (s + 1) * width)
        chunks[s, :, 0:width] = eo[:, cols]
        chunks[s, :, width:] = du[:, cols]
    rows = own.shape[0]
    own[...] = chunks[r]
    across[...] = chunks[r ^ 2]
    mate[0:rows] = chunks[r ^ 1]
    mate[rows:] = chunks[r ^ 3]


def expert_grad_kernel(u, z, de, da, up_grad, down_grad):
    up_grad[0] = mm(u[...], da[...], (0, 0))
    down_grad[0] = mm(z[...], de[...], (0, 0))


def join_kernel(*refs):
    parts, out = refs[:-1], refs[-1]
    height = out.shape[0] // len(parts)
    for j, part in enumerate(parts):
        out[j * height:(j + 1) * height] = part[part.shape[0] - height:]


def pair_sum_kernel(across, got, out):
    rows = across.shape[0]
    out[...] = (across[...].astype(f32) + got[rows:].astype(f32)).astype(bf16)


def expert_sum_kernel(own, got, far, out):
    rows = own.shape[0]
    total = own[...].astype(f32) + got[0:rows].astype(f32) + far[...].astype(f32)
    out[...] = total.astype(bf16)


def total_stats(packs, width):
    total = packs[0][width:width + 16].astype(f32)
    for p in packs[1:]:
        total += p[width:width + 16].astype(f32)
    return total


def gates_of(stats, model):
    inverse = lax.rsqrt((stats[0:1] + stats[1:2]) / model + epsilon)
    delta = inverse * (stats[2:3] + stats[3:4])
    return inverse, 1.0 / (1.0 + jnp.exp(-delta)), 1.0 / (1.0 + jnp.exp(delta))


def combine_kernel(t0, t1, t2, t3, dest, dy, residual, *refs, n_t):
    pieces, (output, pack) = refs[:-2], refs[-2:]
    width, tok = dy.shape
    _, gate0, gate1 = gates_of(total_stats((t0, t1, t2, t3), width), n_t * width)
    back = pieces[0][...]
    row = iota((back.shape[0], tok), 0).astype(f32)
    pick0 = (row == dest[0:1, :]).astype(f32).astype(bf16)
    pick1 = (row == dest[1:2, :]).astype(f32).astype(bf16)
    got0 = mm(back, pick0, (0, 0))
    got1 = mm(back, pick1, (0, 0))
    e0, e1 = got0[0:width], got1[0:width]
    output[...] = (residual[...] + gate0 * e0 + gate1 * e1).astype(bf16)
    dy_own = dy[...].astype(f32)
    dg0 = jnp.sum(dy_own * e0, axis=0, keepdims=True)
    dg1 = jnp.sum(dy_own * e1, axis=0, keepdims=True)
    pack[0:width] = (got0[width:] + got1[width:]).astype(bf16)
    pack[width:] = row_block(split_hi_lo(dg0) + split_hi_lo(dg1)).astype(bf16)


def backward_kernel(
    b0, b1, b2, b3, t0, t1, t2, t3,
    routes, router, gain, out_w, qkv_wt, heads, probs,
    c0, c1, c2, c3, dr1_own, d_proj, d_att, d_logits, gain_terms, d_scores,
    bs, ts, ys, dr, *, n_t,
):
    width = dr1_own.shape[0]
    tok = b0.shape[1]
    experts = router.shape[0]
    n_heads = probs.shape[0]
    size = width // n_heads
    model = n_t * width
    r, _ = my_place()
    packs, tokens = (b0, b1, b2, b3), (t0, t1, t2, t3)
    for k in range(n_t):
        s = r ^ k
        chunk(bs, s, width)[...] = packs[k][0:width].astype(f32)
        chunk(ts, s, width)[...] = tokens[k][0:width].astype(f32)
        chunk(ys, s, width)[...] = tokens[k][width + 16:].astype(f32)
    inverse, gate0, gate1 = gates_of(total_stats(tokens, width), model)
    back = total_stats(packs, width)
    dg0 = back[0:1] + back[1:2]
    dg1 = back[2:3] + back[3:4]
    mean_gate = gate0 * dg0 + gate1 * dg1
    x_of = iota((experts, tok), 0)
    dlog = jnp.where(routes[0:1, :] == x_of, gate0 * (dg0 - mean_gate), 0.0) + jnp.where(
        routes[1:2, :] == x_of, gate1 * (dg1 - mean_gate), 0.0
    )
    d_logits[...] = dlog
    dh2 = bs[...] + mm(router[...].astype(f32), dlog, (0, 0), precision=highest)
    res = ts[...]
    gain_terms[...] = dh2 * res * inverse
    weighted = dh2 * gain[...]
    dot = jnp.sum(weighted * res, axis=0, keepdims=True) * (inverse**3 / model)
    dr[...] = ys[...] + inverse * weighted - res * dot
    d_att[...] = dr[...].astype(bf16)
    dr1_own[...] = chunk(dr, r, width)[...]
    d_o = mm(out_w[...], d_att[...]).astype(bf16)
    scale = size ** -0.5
    for h in range(n_heads):
        q, k, v = (heads[j * width + h * size:j * width + (h + 1) * size] for j in range(3))
        d_oh = d_o[h * size:(h + 1) * size]
        prob = probs[h]
        d_prob = mm(v, d_oh, (0, 0))
        centre = jnp.sum(prob * d_prob, axis=0, keepdims=True)
        ds = (prob * (d_prob - centre)).astype(bf16)
        d_scores[h] = ds
        here = h * size
        d_proj[here:here + size] = (mm(k, ds) * scale).astype(bf16)
        here += width
        d_proj[here:here + size] = (mm(q, ds, (1, 1)) * scale).astype(bf16)
        here += width
        d_proj[here:here + size] = mm(d_oh, prob.astype(bf16), (1, 1)).astype(bf16)
    row_dot = jnp.sum(
        d_proj[...].astype(f32) * heads[...].astype(f32), axis=0, keepdims=True
    )
    stats = row_block(split_hi_lo(row_dot)).astype(bf16)
    dr[...] = mm(qkv_wt[...], d_proj[...])
    for k, c in enumerate((c0, c1, c2, c3)):
        c[0:width] = chunk(dr, r ^ k, width)[...].astype(bf16)
        c[width:] = stats


def small_grad_kernel(
    t0, t1, t2, t3, d_logits, gain_terms, gain1_row, gain2, saved, d_proj, d_att,
    d_scores, buckets, qkv_w, small, last, ts, padded, *, n_t, n_buckets, direct,
):
    packs = (t0, t1, t2, t3)
    width = d_proj.shape[0] // 3
    model = n_t * width
    inner = d_proj.shape[0]
    experts = d_logits.shape[0]
    tok = t0.shape[1]
    r, _ = my_place()
    for k, t in enumerate(packs):
        chunk(ts, r ^ k, width)[...] = t[0:width].astype(f32)
    inverse, _, _ = gates_of(total_stats(packs, width), model)
    normed = (ts[...] * inverse * gain2[...]).astype(bf16).astype(f32)
    small[0:experts] = mm(d_logits[...], normed, (1, 1), precision=highest)
    ones = jnp.ones((8, tok), f32)
    small[experts:] = jnp.zeros((small.shape[0] - experts, model), f32)
    small[experts:experts + 1] = mm(ones, gain_terms[...], (1, 1), precision=highest)[0:1]
    grad = mm(d_proj[...], saved[0:model], (1, 1))
    first = jnp.sum(grad * qkv_w[...].astype(f32), axis=0, keepdims=True)
    small[experts + 1:experts + 2] = first / gain1_row[...]
    hot = bucket_hot(buckets, padded, n_buckets)
    for h in range(d_scores.shape[0]):
        diagonal = jnp.sum(skew(d_scores[h].astype(f32), -1), axis=0, keepdims=True)
        per_bucket = mm(jnp.broadcast_to(diagonal, (8, tok)), hot, (1, 1), precision=highest)
        here = experts + 2 + h
        small[here:here + 1, 0:n_buckets] = per_bucket[0:1]
    if direct:
        last[0:inner] = d_proj[...]
        last[inner:inner + width] = chunk(d_att, r, width)[...]
        height = small.shape[0]
        for c in range(model // tok):
            here = inner + width + c * height
            last[here:here + height] = small[:, c * tok:(c + 1) * tok].astype(bf16)
    else:
        last[...] = mm(saved[model:], d_att[...], (1, 1)).astype(last.dtype)


def late_sum_kernel(o0, o1, o2, o3, *refs, n_e, inner):
    lasts, (small, own, q1, q2, q3) = refs[:n_e], refs[n_e:]
    width = own.shape[0]
    stride, tok = lasts[0].shape
    height, model = small.shape
    total = lasts[0][inner + width:].astype(f32)
    for last in lasts[1:]:
        total += last[inner + width:].astype(f32)
    for c in range(model // tok):
        small[:, c * tok:(c + 1) * tok] = total[c * height:(c + 1) * height]
    first = small[height - 7:height - 6]
    hi, lo = split_hi_lo(first)
    wide = row_block(
        [v[:, s * width:(s + 1) * width] for v in (hi, lo) for s in range(model // width)]
    )
    for o, q in ((o0, own), (o1, q1), (o2, q2), (o3, q3)):
        grad = 0.0
        for j, last in enumerate(lasts):
            grad += mm(o[j * width:(j + 1) * width], last[inner:inner + width], (1, 1))
        q[0:width] = grad.astype(q.dtype)
        if q is not own:
            q[width:] = wide.astype(bf16)


def out_grad_kernel(
    own, q1, q2, q3, small, out, first, second, router, rel, blocks, line, *, n_t
):
    width = own.shape[0]
    experts, buckets = router.shape[0], rel.shape[1]
    r, _ = my_place()
    blocks[r] = own[...]
    for k, q in ((1, q1), (2, q2), (3, q3)):
        blocks[r ^ k] = q[0:width].astype(f32)
    for s in range(n_t):
        cols = slice(s * width, (s + 1) * width)
        out[:, cols] = blocks[s]
        total = small[experts + 1:experts + 2, cols]
        for q in (q1, q2, q3):
            parts = q[width:].astype(f32)
            total += parts[s:s + 1] + parts[n_t + s:n_t + s + 1]
        line[:, cols] = total
    first[...] = line[0]
    second[...] = small[experts]
    router[...] = small[0:experts]
    rel[...] = small[experts + 2:experts + 2 + rel.shape[0], 0:buckets]


def input_grad_kernel(c0, c1, c2, c3, dr1, inv1, x, gain, out, *, n_t):
    width = x.shape[0]
    total = c0[...].astype(f32) + c1[...].astype(f32) + (c2[...].astype(f32) + c3[...].astype(f32))
    row_dot = (total[width:width + 1] + total[width + 1:width + 2]) / (n_t * width)
    inverse = inv1[...]
    weighted = total[0:width] * chunk(gain, my_place()[0], width)[...]
    out[...] = dr1[...] + inverse * weighted - x[...].astype(f32) * (inverse * inverse * row_dot)


def qkv_grad_kernel(*refs, count, inner):
    lasts, saved, rest = refs[:count], refs[count:2 * count], refs[2 * count:]
    out = rest[-1]
    model = out.shape[1]
    total = 0.0 if len(rest) == 1 else rest[0][...]
    for last, h in zip(lasts, saved):
        total += mm(last[0:inner], h[0:model], (1, 1))
    out[...] = total


def per_device(
    tokens,
    first_gain,
    second_gain,
    qkv_weight,
    out_weight,
    rel_table,
    router_weight,
    up_weight,
    down_weight,
    routes,
    lengths,
    bucket_ids,
    cotangent,
    *,
    n_t,
    n_e,
):
    tok, width = tokens.shape
    model = n_t * width
    inner = 3 * width
    experts = router_weight.shape[1]
    cap = 5 * tok // (2 * experts)
    rows = experts * cap
    n_heads = rel_table.shape[1]
    n_buckets = rel_table.shape[0]
    direct = n_e == 8
    padded = pltpu.VMEM((1, tok), i32)

    def swap(v, k, axis="tensor", n=n_t):
        return lax.ppermute(v, axis, [(i, i ^ k) for i in range(n)])

    def around(v):
        return [v] + [swap(v, k) for k in range(1, n_t)]

    def around_large(v):
        far = swap(v, 2)
        return [v, swap(v, 1), far, swap(far, 1)]

    def exchange(v):
        w = v.shape[-1]
        v = v.reshape(n_e, rows // n_e, w)
        v = lax.all_to_all(v, "expert", split_axis=0, concat_axis=0, tiled=True)
        return v.reshape(rows, w)

    def step(v, k):
        return lax.ppermute(v, "expert", [(i, (i + k) % n_e) for i in range(n_e)])

    def after(values, *others):
        return list(lax.optimization_barrier((tuple(values), others))[0])

    x = tokens.T
    dy = cotangent.T
    qkv_w = qkv_weight.transpose(0, 2, 1).reshape(inner, model)
    router = router_weight.T
    table = rel_table.T
    routes_t = routes.T
    gain1_row = first_gain.reshape(1, model)
    gain2_row = second_gain.reshape(1, model)
    buckets = bucket_ids.reshape(1, -1)

    xs = around(x)
    gain1, out_wt, bias = run(
        prepare_kernel,
        [((model, 1), f32), ((model, width), bf16), ((n_heads, tok, tok), f32)],
        lengths, gain1_row, out_weight, table, buckets,
        fetch=(0, 1, 2, 3, 4),
        scratch=[padded],
    )
    own, p1, p2, p3, inv1, heads, probs, saved = run(
        functools.partial(attention_kernel, n_t=n_t),
        [((width, tok), f32)]
        + [((width, tok), bf16)] * 3
        + [
            ((1, tok), f32),
            ((inner, tok), bf16),
            ((n_heads, tok, tok), f32),
            ((model + width, tok), bf16),
        ],
        *xs, gain1, qkv_w, out_wt, bias,
        fetch=(n_t + 1,),
        scratch=[pltpu.VMEM((model, tok), f32), pltpu.VMEM((model, tok), f32)],
    )
    got = [swap(p, k) for k, p in ((1, p1), (2, p2), (3, p3))]
    dest, gain2, rw_own, qkv_wt = run(
        functools.partial(route_kernel, experts=experts, cap=cap, n_t=n_t),
        [
            ((8, tok), f32),
            ((model, 1), f32),
            ((experts, width), bf16),
            ((model, inner), bf16),
        ],
        routes_t, router, gain2_row, qkv_w, inv1,
        fetch=(0, 1, 2, 3),
        scratch=[pltpu.VMEM((n_t, experts, width), f32)],
    )
    send_rows, token_pack, residual = run(
        dispatch_kernel,
        [
            ((rows, 2 * width + 16), bf16),
            ((2 * width + 16, tok), bf16),
            ((width, tok), f32),
        ],
        own, *got, x, dy, gain2, rw_own, routes_t, dest,
        fetch=(4, 5, 8),
        scratch=[pltpu.VMEM((2 * width + 16, tok), bf16)],
    )
    in_rows = exchange(send_rows)
    if direct:
        (early,) = after([saved], in_rows)
        behind1, beside = step(early, 2), swap(early, 1, "expert", n_e)
        (far,) = after([swap(in_rows, 2)], behind1, beside)
        in_rows = [in_rows, swap(in_rows, 1), far, swap(far, 1)]
    else:
        in_rows = around_large(in_rows)

    own, across, mate, u, z, de, da = run(
        functools.partial(expert_kernel, n_t=n_t),
        [((rows, 2 * width), bf16)] * 2
        + [((2 * rows, 2 * width), bf16)]
        + [((rows, model), bf16)] * 4,
        *in_rows, up_weight, down_weight,
        fetch=(4, 5),
        scratch=[
            pltpu.VMEM((n_t, rows, width), f32),
            pltpu.VMEM((n_t, rows, width), f32),
            pltpu.VMEM((n_t, rows, 2 * width), bf16),
        ],
    )
    got = swap(mate, 1)
    if direct:
        early, behind1 = after([early, behind1], mate)
        behind2, behind3 = step(behind1, 2), step(early, 6)
        beside1 = swap(behind1, 1, "expert", n_e)
    (across,) = run(pair_sum_kernel, [((rows, 2 * width), bf16)], across, got)
    far = swap(across, 2)
    up_grad, down_grad = run(
        expert_grad_kernel,
        [(up_weight.shape, f32), (down_weight.shape, f32)],
        *after([u, z, de, da], across),
    )
    token_packs = around(after([token_pack], up_grad)[0])
    if direct:
        (far,) = after([far], behind2, behind3, beside1)
    (far,) = after([far], up_grad, *token_packs[1:])
    (summed,) = run(expert_sum_kernel, [((rows, 2 * width), bf16)], own, got, far)
    back = exchange(summed)
    output, back_pack = run(
        functools.partial(combine_kernel, n_t=n_t),
        [((width, tok), bf16), ((width + 16, tok), bf16)],
        *token_packs, dest, dy, residual, back,
        fetch=(5,),
    )
    back_packs = around(back_pack)
    if direct:
        beside2, beside3 = (
            swap(v, 1, "expert", n_e) for v in after([behind2, behind3], back_pack)
        )
        saved_all = [saved, behind1, behind2, behind3, beside, beside1, beside2, beside3]

    c0, c1, c2, c3, dr1, d_proj, d_att, d_logits, gain_terms, d_scores = run(
        functools.partial(backward_kernel, n_t=n_t),
        [((width + 16, tok), bf16)] * 4
        + [
            ((width, tok), f32),
            ((inner, tok), bf16),
            ((model, tok), bf16),
            ((experts, tok), f32),
            ((model, tok), f32),
            ((n_heads, tok, tok), bf16),
        ],
        *back_packs, *token_packs, routes_t, router, gain2, out_weight, qkv_wt, heads, probs,
        fetch=(8, 9, 11),
        scratch=[pltpu.VMEM((model, tok), f32)] * 4,
    )
    if direct:
        (d_scores,) = after([d_scores], beside2, beside3)
    height = experts + 8
    if direct:
        last_shape = (inner + width + height * (model // tok), tok)
    else:
        last_shape = out_weight.shape
    small, last = run(
        functools.partial(small_grad_kernel, n_t=n_t, n_buckets=n_buckets, direct=direct),
        [((height, model), f32), (last_shape, bf16)],
        *token_packs, d_logits, gain_terms, gain1_row, gain2, saved, d_proj, d_att,
        d_scores, buckets, qkv_w,
        fetch=(6, 12, 13),
        scratch=[pltpu.VMEM((model, tok), f32), padded],
    )
    if direct:
        got = [swap(c, k) for k, c in ((1, c1), (2, c2), (3, c3))]
        (last,) = after([last], *got)
        next_to = swap(last, 1, "expert", n_e)
        last1, last3 = after([step(last, 2), step(last, 6)], next_to)
        lasts = [last, last1, step(last1, 2), last3]
    else:
        got = [swap(c, k) for k, c in ((1, c1), (2, c2), (3, c3))]
    (input_grad,) = run(
        functools.partial(input_grad_kernel, n_t=n_t),
        [((width, tok), f32)],
        c0, *got, dr1, inv1, x, gain1,
        fetch=(6,),
    )
    if direct:
        (att,) = run(
            join_kernel, [((n_e * width, tok), bf16)], *after(saved_all, lasts[1])
        )
        half = n_e // 2
        (part,) = run(
            functools.partial(qkv_grad_kernel, count=half, inner=inner),
            [((inner, model), f32)],
            *lasts, *saved_all[:half],
        )
        lasts += [next_to] + [swap(v, 1, "expert", n_e) for v in lasts[1:]]
        atts = [att, swap(att, 1), swap(att, 2)]
        atts.append(swap(after(atts[2:], lasts[half + 3])[0], 1))
        lasts[half:] = after(lasts[half:], part)
        small, own, q1, q2, q3 = run(
            functools.partial(late_sum_kernel, n_e=n_e, inner=inner),
            [((height, model), f32), ((width, width), f32)]
            + [((width + 16, width), bf16)] * 3,
            *atts, *lasts,
        )
        got = [swap(q, k) for k, q in ((1, q1), (2, q2), (3, q3))]
        (part,) = after([part], own)
        (qkv_grad,) = run(
            functools.partial(qkv_grad_kernel, count=half, inner=inner),
            [((inner, model), f32)],
            *lasts[half:], *saved_all[half:], part,
        )
        out_grad, first, second, router_grad, rel_grad = run(
            functools.partial(out_grad_kernel, n_t=n_t),
            [
                (out_weight.shape, f32),
                ((model,), f32),
                ((model,), f32),
                ((experts, model), f32),
                ((n_heads, n_buckets), f32),
            ],
            own, *got, small,
            scratch=[pltpu.VMEM((n_t, width, width), f32), pltpu.VMEM((1, model), f32)],
        )
    else:
        small, out_grad = lax.psum((small, last.astype(f32)), "expert")
        (qkv_grad,) = run(
            functools.partial(qkv_grad_kernel, count=1, inner=inner),
            [((inner, model), f32)],
            d_proj, saved,
        )
        qkv_grad = lax.psum(qkv_grad, "expert")
        first = lax.psum(small[experts + 1], "tensor")
        second = small[experts]
        router_grad = small[:experts]
        rel_grad = small[experts + 2:experts + 2 + n_heads, :n_buckets]
    return (
        output.T,
        input_grad.T,
        first.reshape(model),
        second.reshape(model),
        qkv_grad.reshape(3, width, model).transpose(0, 2, 1),
        out_grad,
        rel_grad.T,
        router_grad.T,
        up_grad,
        down_grad,
    )


def solution(mesh):
    placed = (
        P("expert", "tensor"),
        P(),
        P(),
        P(None, None, "tensor"),
        P("tensor", None),
        P(None, "tensor"),
        P(),
        P("expert", None, "tensor"),
        P("expert", "tensor", None),
        P("expert", None),
        P("expert", None),
        P(),
        P("expert", "tensor"),
    )
    return jax.shard_map(
        functools.partial(per_device, n_t=mesh.shape["tensor"], n_e=mesh.shape["expert"]),
        mesh=mesh,
        in_specs=placed,
        out_specs=(
            P("expert", "tensor"),
            P("expert", "tensor"),
            P(),
            P(),
            P(None, None, "tensor"),
            P("tensor", None),
            P(None, "tensor"),
            P(),
            P("expert", None, "tensor"),
            P("expert", "tensor", None),
        ),
        check_vma=False,
    )
```
